32 devices in a mesh: ctx: 8 (over y, x, core), fsdp: 4 (over z).
Axes of the slice: x: 2, y: 2, z: 4, core: 2. Of those that a mesh axis runs over, the one named last changes fastest.
Arguments:
- tokens: bfloat16 [4, 1024, 1024], P('fsdp', 'ctx'), may hold values from -6 to 6
- encoder: bfloat16 [4, 512, 1024], P('fsdp', 'ctx'), may hold values from -6 to 6
- decoder_segments: int32 [4, 1024], P('fsdp', 'ctx'), may hold values from 0 to 3, never falling along the last dimension, each value on 1 to 897 neighbouring positions
- source_segments: int32 [4, 512], P('fsdp', 'ctx'), may hold values from 0 to 3, never falling along the last dimension, each value on 1 to 449 neighbouring positions
- attn_weight: bfloat16 [1024, 8192], P('fsdp'), may hold values from -4 to 4
- up_weight: bfloat16 [1024, 8192], P('fsdp'), may hold values from -0.1875 to 0.1875
- down_weight: bfloat16 [1024, 8192], P('fsdp'), may hold values from -0.0625 to 0.0625
- vector_params: float32 [21, 1024], replicated, may hold values from -1 to 2
- cotangent: bfloat16 [4, 1024, 1024], P('fsdp', 'ctx'), may hold values from -6 to 6
Outputs:
- mixed: bfloat16 [4, 1024, 1024], P('fsdp', 'ctx')
- grad_tokens: float32 [4, 1024, 1024], P('fsdp', 'ctx')
- grad_encoder: float32 [4, 512, 1024], P('fsdp', 'ctx')
- grad_attn: float32 [1024, 8192], P(('ctx', 'fsdp'))
- grad_up: float32 [1024, 8192], P(('ctx', 'fsdp'))
- grad_down: float32 [1024, 8192], P(('ctx', 'fsdp'))
- grad_vectors: float32 [21, 1024], replicated
The draws below stay inside these ranges and needn't reach their ends.
Inputs may be any that keep to these rules, and one draw needn't show every extreme that they name: `decoder_segments`: segment numbers never fall along a sequence; each of the 4 numbers occurs in every sequence; one document of each sequence has exactly 897 tokens. Decoder document k attends to encoder document k. `source_segments`: as for the decoder; one document of each sequence has exactly 449 states.
All inputs are finite; a program needn't handle non-finite values.
Results may differ from the reference program's by a relative error of at most 0.02.
Values may be sent and summed in bfloat16 or wider, within the bound.
A program may use at most 384 MiB of HBM per device.

```python
import math
import jax
import jax.numpy as jnp
import numpy as np
from jax import lax

D = 1024
H = 16
HD = 64
FF = 8192
TOK_DEV = 128
ENC_DEV = 64
DOCS = 4
LEN = 1024
ENC_LEN = 512
SEQS = 4
VROWS = 21


def draw_attn_weight(key, part):
    key = jax.random.fold_in(key, 11)
    base = jnp.clip(jax.random.normal(key, (D, 8 * D), jnp.float32), -4.0, 4.0)
    column_block = jnp.arange(8 * D, dtype=jnp.int32) // D
    output_block = (column_block == 3) | (column_block == 7)
    scale = jnp.where(output_block, (D // 32) ** (-0.5), D ** (-0.5))
    return (base * scale[None, :]).astype(jnp.bfloat16)


def draw_vector_params(key, part):
    key = jax.random.fold_in(key, 23)
    base = jnp.clip(jax.random.normal(key, (VROWS, D), jnp.float32), -4.0, 4.0)
    row_number = jnp.arange(VROWS, dtype=jnp.int32)[:, None]
    gain_row = (row_number < 6) & (row_number % 2 == 0)
    return jnp.where(gain_row, 1.0 + 0.15 * base, 0.2 * base)


def block_scale(rng, shape, split, low, largest):
    def one(position, parts):
        draws = jax.random.uniform(jax.random.fold_in(jax.random.fold_in(rng, 6), position), (parts,), jnp.float32, low / len(split), largest / len(split))
        return jnp.repeat(jnp.exp(draws), shape[position] // parts).reshape((-1,) + (1,) * (len(shape) - position - 1))

    level = one(*split[0])
    for cut in split[1:]:
        level = level * one(*cut)
    return level


def split_up(count, total, most, slope):
    loads = [(1 << 20) // math.isqrt(standing ** slope) + 1 for standing in range(2, count + 1)]
    rest, holding = total - most - (count - 1), [1] * (count - 1)
    while rest > 0:
        movable = [i for i in range(count - 1) if holding[i] < most]
        pool, remaining = sum([loads[i] for i in movable]), rest
        for i in movable:
            extra = min(most - holding[i], max(1, remaining * loads[i] // pool), rest)
            holding[i] = holding[i] + extra
            rest = rest - extra
    return np.array([most] + holding)


def ragged(own_key, count, total, bound, skew):
    if count == 2:
        one = jax.random.randint(own_key, (), max(1, total - bound), min(bound, total - 1) + 1)
        return jnp.stack([one, total - one])
    sizes = jnp.asarray(split_up(count, total, bound, skew), jnp.int32)
    twos = (count - 1) // 2
    giver, receiver = sizes[1:1 + 2 * twos:2], sizes[2:2 + 2 * twos:2]
    margin = jnp.minimum(giver - 1, bound - receiver)
    moved = jax.random.randint(jax.random.fold_in(own_key, 1), (twos,), 0, 1 << 20) % (margin + 1)
    sizes = sizes.at[1:1 + 2 * twos:2].set(giver - moved).at[2:2 + 2 * twos:2].set(receiver + moved)
    return sizes[jax.random.permutation(jax.random.fold_in(own_key, 2), count)]


def bell_draw(key, extent, width, most, shards=(), held_as=jnp.bfloat16):
    values = width * jax.random.normal(key, extent, jnp.float32)
    if shards:
        values = values * block_scale(key, extent, shards, -0.22, 0.18)
    return jnp.clip(values, -most, most).astype(held_as)


def setup_inputs(seed: int = 0) -> dict:
    streams_of = jax.random.split(jax.random.key(seed), 10)
    tokens = bell_draw(streams_of[0], (SEQS, LEN, D), 1.0, 6.0, ((0, 4), (1, 8)))
    encoder = bell_draw(streams_of[1], (SEQS, ENC_LEN, D), 1.0, 6.0, ((0, 4), (1, 8)))
    decoder_segments = jax.vmap(lambda own: jnp.searchsorted(jnp.cumsum(ragged(own, DOCS, LEN, LEN - TOK_DEV + 1, 2)), jnp.arange(LEN), side="right"))(jax.random.split(streams_of[2], SEQS)).reshape((SEQS, LEN)).astype(jnp.int32)
    source_segments = jax.vmap(lambda own: jnp.searchsorted(jnp.cumsum(ragged(own, DOCS, ENC_LEN, ENC_LEN - ENC_DEV + 1, 2)), jnp.arange(ENC_LEN), side="right"))(jax.random.split(streams_of[3], SEQS)).reshape((SEQS, ENC_LEN)).astype(jnp.int32)
    attn_weight = draw_attn_weight(jax.random.fold_in(streams_of[9], 71), 0)
    up_weight = bell_draw(streams_of[5], (D, FF), D ** -0.5, 0.1875, ((0, 4),))
    down_weight = bell_draw(streams_of[6], (D, FF), FF ** -0.5, 0.0625, ((0, 4),))
    vector_params = draw_vector_params(jax.random.fold_in(streams_of[9], 71), 0)
    cotangent = bell_draw(streams_of[8], (SEQS, LEN, D), 1.0, 6.0, ((0, 4), (1, 8)))
    return {"tokens": tokens, "encoder": encoder, "decoder_segments": decoder_segments, "source_segments": source_segments, "attn_weight": attn_weight, "up_weight": up_weight, "down_weight": down_weight, "vector_params": vector_params, "cotangent": cotangent}


EPS = 1e-05
NEG = -1e+30
MATMUL_ACCURACY = lax.Precision.HIGHEST

@jax.custom_vjp
def reduced_float(v):
    return lax.optimization_barrier(v.astype(jnp.bfloat16)).astype(jnp.float32)

@jax.custom_vjp
def low_back(v):
    return v

def low_keep(v):
    return (reduced_float(v), None)

def low_pass(kept, grad):
    return (grad,)

def back_keep(v):
    return (v, None)

def back_low(kept, grad):
    return (reduced_float(grad),)
reduced_float.defvjp(low_keep, low_pass)
low_back.defvjp(back_keep, back_low)

def layer_norm(value, gain, shift):
    mean_row = lax.optimization_barrier(jnp.mean(value, axis=-1, keepdims=True))
    centred = value - mean_row
    spread = lax.optimization_barrier(jnp.mean(centred * centred, axis=-1, keepdims=True))
    return centred * lax.rsqrt(spread + EPS) * gain + shift

def matmul(left, right):
    return jnp.dot(left, right, precision=MATMUL_ACCURACY)

def attend(queries, key_rows, value_rows, query_seg, key_seg, causal):
    length = queries.shape[0]
    kv_len = key_rows.shape[0]
    block_rows = min(512, length)
    count_blocks = length // block_rows
    query_blocks = queries.reshape(count_blocks, block_rows, H, HD)
    seg_blocks = query_seg.reshape(count_blocks, block_rows)
    pos_blocks = jnp.arange(length, dtype=jnp.int32).reshape(count_blocks, block_rows)
    per_head_keys = key_rows.reshape(kv_len, H, HD)
    per_head_values = value_rows.reshape(kv_len, H, HD)
    key_pos = jnp.arange(kv_len, dtype=jnp.int32)

    def one_block(block_item):
        query_tile_rows, seg_block, pos_block = block_item
        unnormalized_logits = jnp.einsum('sft,rft->sfr', query_tile_rows, per_head_keys, precision=MATMUL_ACCURACY)
        scores = low_back(unnormalized_logits) * HD ** (-0.5)
        allowed = seg_block[:, None] == key_seg[None, :]
        if causal:
            allowed = allowed & (pos_block[:, None] >= key_pos[None, :])
        scores = jnp.where(allowed[:, None, :], scores, NEG)
        row_max = lax.optimization_barrier(jnp.max(scores, axis=-1, keepdims=True))
        weights = jnp.exp(scores - row_max)
        softmax_weights = weights / lax.optimization_barrier(jnp.sum(weights, axis=-1, keepdims=True))
        blended_output = jnp.einsum('tna,anu->tnu', reduced_float(softmax_weights), per_head_values, precision=MATMUL_ACCURACY)
        return blended_output.reshape(block_rows, H * HD)
    result_blocks = lax.map(jax.checkpoint(one_block), (query_blocks, seg_blocks, pos_blocks))
    return result_blocks.reshape(length, H * HD)

def forward(stream, source, dec_seg, src_seg, attn_weight, up_weight, down_weight, vector_params):
    gain_self, shift_self, gain_cross, shift_cross, gain_feed, shift_feed, bias_query, bias_value, bias_output, cross_query, cross_value, cross_output, bias_down = [vector_params[row_index] for row_index in range(13)]
    bias_up = vector_params[13:].reshape(-1)
    normed_self = reduced_float(layer_norm(stream, gain_self, shift_self))
    query_self = reduced_float(low_back(matmul(normed_self, attn_weight[:, :D]) + bias_query))
    key_self = reduced_float(low_back(matmul(normed_self, attn_weight[:, D:2 * D])))
    value_self = reduced_float(low_back(matmul(normed_self, attn_weight[:, 2 * D:3 * D]) + bias_value))
    heads_self = reduced_float(low_back(attend(query_self, key_self, value_self, dec_seg, dec_seg, True)))
    after_self = stream + low_back(matmul(heads_self, attn_weight[:, 3 * D:4 * D]) + bias_output)
    normed_cross = reduced_float(layer_norm(after_self, gain_cross, shift_cross))
    query_cross = reduced_float(low_back(matmul(normed_cross, attn_weight[:, 4 * D:5 * D]) + cross_query))
    key_cross = reduced_float(low_back(matmul(source, attn_weight[:, 5 * D:6 * D])))
    value_cross = reduced_float(low_back(matmul(source, attn_weight[:, 6 * D:7 * D]) + cross_value))
    heads_cross = reduced_float(low_back(attend(query_cross, key_cross, value_cross, dec_seg, src_seg, False)))
    after_cross = after_self + low_back(matmul(heads_cross, attn_weight[:, 7 * D:]) + cross_output)
    normed_feed = reduced_float(layer_norm(after_cross, gain_feed, shift_feed))
    inner_act = low_back(matmul(normed_feed, up_weight) + bias_up)
    active = reduced_float(jax.nn.gelu(inner_act, approximate=False))
    branch = low_back(matmul(active, down_weight.T) + bias_down)
    return after_cross + branch

def reference(tokens, encoder, decoder_segments, source_segments, attn_weight, up_weight, down_weight, vector_params, cotangent):
    params = (attn_weight.astype(jnp.float32), up_weight.astype(jnp.float32), down_weight.astype(jnp.float32), vector_params.astype(jnp.float32))

    def one_sequence(totals, item_seq):
        stream, source, dec_seg, src_seg, grad_seq = item_seq

        def run(stream_in, source_in, attn_in, up_in, down_in, vector_in):
            return forward(stream_in, source_in, dec_seg, src_seg, attn_in, up_in, down_in, vector_in)
        result, pull = jax.vjp(run, stream.astype(jnp.float32), source.astype(jnp.float32), params[0], params[1], params[2], params[3])
        grads = pull(grad_seq.astype(jnp.float32))
        totals = tuple((total_now + grad_now for total_now, grad_now in zip(totals, grads[2:])))
        return (totals, (result.astype(jnp.bfloat16), grads[0], grads[1]))
    zeros_start = tuple((jnp.zeros_like(param_now) for param_now in params))
    totals, outputs = lax.scan(one_sequence, zeros_start, (tokens, encoder, decoder_segments, source_segments, cotangent))
    return (outputs[0], outputs[1], outputs[2], totals[0], totals[1], totals[2], totals[3])
```

```python
import jax
import jax.numpy as jnp
from jax import lax
from jax.sharding import PartitionSpec as P

D = 1024
H = 16
HD = 64
EPS = 1e-05
NEG = -1e30
SCALE = HD ** (-0.5)
bf = jnp.bfloat16
f32 = jnp.float32


def layer_norm(value, gain, shift):
    mean_row = jnp.mean(value, axis=-1, keepdims=True)
    centred = value - mean_row
    spread = jnp.mean(centred * centred, axis=-1, keepdims=True)
    return centred * lax.rsqrt(spread + EPS) * gain + shift


def norm_back(value, gain, grad):
    mean_row = jnp.mean(value, axis=-1, keepdims=True)
    centred = value - mean_row
    inv = lax.rsqrt(jnp.mean(centred * centred, axis=-1, keepdims=True) + EPS)
    hat = centred * inv
    gg = grad * gain
    back = inv * (gg - jnp.mean(gg, axis=-1, keepdims=True) - hat * jnp.mean(gg * hat, axis=-1, keepdims=True))
    return back, jnp.sum(grad * hat, axis=0), jnp.sum(grad, axis=0)


def dot(a, b):
    return jnp.dot(a, b, preferred_element_type=f32)


def dot_t(a, b):
    return lax.dot_general(a, b, (((1,), (1,)), ((), ())), preferred_element_type=f32)


def t_dot(a, b):
    return lax.dot_general(a, b, (((0,), (0,)), ((), ())), preferred_element_type=f32)


def gather(a):
    return lax.all_gather(a, "ctx", axis=0, tiled=True)


def scatter(a):
    return lax.psum_scatter(a.astype(bf), "ctx", scatter_dimension=0, tiled=True).astype(f32)


def heads(a):
    return a.reshape(a.shape[0], -1, HD)


def attend(q, k, v, allowed):
    s = jnp.einsum("qhd,khd->hqk", heads(q), heads(k), preferred_element_type=f32) * SCALE
    s = jnp.where(allowed[None], s, NEG)
    m = jnp.max(s, axis=-1, keepdims=True)
    e = jnp.exp(s - m)
    tot = jnp.sum(e, axis=-1, keepdims=True)
    p = (e / tot).astype(bf)
    o = jnp.einsum("hqk,khd->qhd", p, heads(v), preferred_element_type=f32).reshape(q.shape)
    return o, m + jnp.log(tot)


def attend_back(q, k, v, allowed, o, lse, do):
    s = jnp.einsum("qhd,khd->hqk", heads(q), heads(k), preferred_element_type=f32) * SCALE
    p = jnp.where(allowed[None], jnp.exp(s - lse), 0.0)
    delta = jnp.sum(heads(do.astype(f32) * o), axis=-1).T[..., None]
    dv = jnp.einsum("hqk,qhd->khd", p.astype(bf), heads(do), preferred_element_type=f32).reshape(k.shape)
    dp = jnp.einsum("qhd,khd->hqk", heads(do), heads(v), preferred_element_type=f32)
    ds = (p * (dp - delta) * SCALE).astype(bf)
    dq = jnp.einsum("hqk,khd->qhd", ds, heads(k), preferred_element_type=f32).reshape(q.shape)
    dk = jnp.einsum("hqk,qhd->khd", ds, heads(q), preferred_element_type=f32).reshape(k.shape)
    return dq.astype(bf), dk.astype(bf), dv.astype(bf)


def columns(a, width):
    return lax.dynamic_slice_in_dim(a, lax.axis_index("ctx") * width, width, axis=a.ndim - 1)


def body(tokens, encoder, dec_seg, src_seg, attn_w, up_w, down_w, vec, cot):
    n = lax.axis_size("ctx")
    nz = lax.axis_size("fsdp")
    w = D // n
    ff = up_w.shape[1]
    fw = ff // n
    x = tokens[0].astype(f32)
    t = x.shape[0]
    length = n * t
    g = cot[0]
    g1, s1, g2, s2, g3, s3, bq, bv, bo, bqc, bvc, boc, bdown = [vec[i] for i in range(13)]
    bup = columns(vec[13:].reshape(-1), fw)
    rows = attn_w.shape[0]
    mine = columns(attn_w.reshape(rows, 8, D), w).reshape(rows, 8 * w)
    wa = lax.all_gather(mine, "fsdp", axis=0, tiled=True).reshape(D, 8, w)
    up = lax.all_gather(columns(up_w, fw), "fsdp", axis=0, tiled=True)
    down = lax.all_gather(columns(down_w, fw), "fsdp", axis=0, tiled=True)
    wqkv = jnp.concatenate([wa[:, 0], wa[:, 1], wa[:, 2]], axis=1)
    wkvc = jnp.concatenate([wa[:, 5], wa[:, 6]], axis=1)
    outs = jnp.concatenate([wa[:, 3], wa[:, 7]], axis=1)
    outs = lax.all_to_all(outs.reshape(n, w, 2 * w), "ctx", 0, 0, tiled=False)
    outs = jnp.transpose(outs.reshape(n, w, 2, w), (2, 1, 0, 3)).reshape(2, w, D)
    wo, woc = outs[0], outs[1]

    seg = gather(dec_seg[0])
    src = gather(src_seg[0])
    pos = jnp.arange(length)
    causal = (seg[:, None] == seg[None, :]) & (pos[:, None] >= pos[None, :])
    crossed = seg[:, None] == src[None, :]
    gf = gather(g)
    ef = gather(encoder[0])

    n1f = gather(layer_norm(x, g1, s1).astype(bf))
    zero = jnp.zeros((w,), f32)
    qkv = (dot(n1f, wqkv) + jnp.concatenate([columns(bq, w), zero, columns(bv, w)])).astype(bf)
    q1, k1, v1 = qkv[:, :w], qkv[:, w:2 * w], qkv[:, 2 * w:]
    o1, lse1 = attend(q1, k1, v1, causal)
    o1b = o1.astype(bf)
    x1 = x + scatter(dot(o1b, wo)) + bo
    n2f = gather(layer_norm(x1, g2, s2).astype(bf))
    q2 = (dot(n2f, wa[:, 4]) + columns(bqc, w)).astype(bf)
    kv2 = (dot(ef, wkvc) + jnp.concatenate([zero, columns(bvc, w)])).astype(bf)
    k2, v2 = kv2[:, :w], kv2[:, w:]
    o2, lse2 = attend(q2, k2, v2, crossed)
    o2b = o2.astype(bf)
    x2 = x1 + scatter(dot(o2b, woc)) + boc
    n3f = gather(layer_norm(x2, g3, s3).astype(bf))
    u = dot(n3f, up) + bup
    cdf = 0.5 * (1.0 + lax.erf(u * (2.0 ** -0.5)))
    act = (u * cdf).astype(bf)
    mixed = (x2 + scatter(dot_t(act, down)) + bdown).astype(bf)
    da = dot(gf, down)
    slope = cdf + u * jnp.exp(-0.5 * u * u) * ((2.0 * jnp.pi) ** -0.5)
    du = (da * slope).astype(bf)
    back3, gg3, gs3 = norm_back(x2, g3, scatter(dot_t(du, up)))
    dx2 = g.astype(f32) + back3
    dy2 = dx2.astype(bf)
    dy2f = gather(dy2)
    do2 = dot_t(dy2f, woc).astype(bf)
    dq2, dk2, dv2 = attend_back(q2, k2, v2, crossed, o2, lse2, do2)
    dkv2 = jnp.concatenate([dk2, dv2], axis=1)
    grad_encoder = scatter(dot_t(dkv2, wkvc))
    back2, gg2, gs2 = norm_back(x1, g2, scatter(dot_t(dq2, wa[:, 4])))
    dx1 = dx2 + back2
    dy1 = dx1.astype(bf)
    dy1f = gather(dy1)
    do1 = dot_t(dy1f, wo).astype(bf)
    dq1, dk1, dv1 = attend_back(q1, k1, v1, causal, o1, lse1, do1)
    dqkv = jnp.concatenate([dq1, dk1, dv1], axis=1)
    back1, gg1, gs1 = norm_back(x, g1, scatter(dot_t(dqkv, wqkv)))
    grad_tokens = dx1 + back1

    def owned(part):
        m = part.shape[1]
        share = D // (n * nz)
        part = part.astype(bf).reshape(n, nz, share, m)
        part = jnp.transpose(part, (1, 0, 2, 3))
        summed = lax.psum_scatter(part, "fsdp", scatter_dimension=0, tiled=False)
        got = lax.all_to_all(summed, "ctx", 0, 0, tiled=False)
        return got.astype(f32)

    share = D // (n * nz)
    grad_o1 = t_dot(o1b, dy1f)
    grad_o2 = t_dot(o2b, dy2f)
    both = jnp.concatenate([grad_o1, grad_o2], axis=1).astype(bf)
    both = lax.psum_scatter(both, "fsdp", scatter_dimension=0, tiled=True).astype(f32)
    part = jnp.concatenate([t_dot(n1f, dqkv), t_dot(n2f, dq2), t_dot(ef, dkv2)], axis=1)
    part = owned(part).reshape(n, share, 6, w)
    part = jnp.transpose(part, (1, 2, 0, 3)).reshape(share, 6, D)
    grad_attn = jnp.concatenate(
        [part[:, 0], part[:, 1], part[:, 2], both[:, :D], part[:, 3], part[:, 4], part[:, 5], both[:, D:]], axis=1)
    grad_up = jnp.transpose(owned(t_dot(n3f, du)), (1, 0, 2)).reshape(share, ff)
    grad_down = jnp.transpose(owned(t_dot(gf, act)), (1, 0, 2)).reshape(share, ff)

    def csum(a):
        return jnp.sum(a.astype(f32), axis=0)

    def place(vals, total):
        return lax.dynamic_update_slice(jnp.zeros((total,), f32), vals, (lax.axis_index("ctx") * vals.shape[0],))

    terms = jnp.concatenate([
        jnp.stack([gg1, gs1, gg2, gs2, gg3, gs3, place(csum(dq1), D), place(csum(dv1), D), csum(dy1), place(csum(dq2), D),
                   place(csum(dv2), D), csum(dy2), csum(g)]),
        place(csum(du), ff).reshape(-1, D)], axis=0)
    grad_vectors = lax.psum(terms, ("ctx", "fsdp"))
    return (mixed[None], grad_tokens[None], grad_encoder[None], grad_attn, grad_up, grad_down, grad_vectors)


def solution(mesh):
    return jax.shard_map(
        body, mesh=mesh,
        in_specs=(P("fsdp", "ctx", None), P("fsdp", "ctx", None), P("fsdp", "ctx"), P("fsdp", "ctx"), P("fsdp", None),
                  P("fsdp", None), P("fsdp", None), P(), P("fsdp", "ctx", None)),
        out_specs=(P("fsdp", "ctx", None), P("fsdp", "ctx", None), P("fsdp", "ctx", None), P(("ctx", "fsdp"), None),
                   P(("ctx", "fsdp"), None), P(("ctx", "fsdp"), None), P()),
        check_vma=False,
    )
```

```python
import functools

import jax
import jax.numpy as jnp
from jax import lax
from jax.experimental import pallas as pl
from jax.experimental.pallas import tpu as pltpu
from jax.sharding import PartitionSpec as P

D = 1024
HD = 64
LANES = 128
TILE = 256
EPS = 1e-05
NEG = -1e30
SCALE = HD ** (-0.5)
bf = jnp.bfloat16
f32 = jnp.float32
ORDER = (0, 1, 2, 5, 6, 3, 7, 4)


def dot(a, b):
    return jnp.dot(a, b, preferred_element_type=f32)


def dot_t(a, b):
    return lax.dot_general(a, b, (((1,), (1,)), ((), ())), preferred_element_type=f32)


def t_dot(a, b):
    return lax.dot_general(a, b, (((0,), (0,)), ((), ())), preferred_element_type=f32)


def normed(value):
    centred = value - jnp.mean(value, axis=-1, keepdims=True)
    inv = lax.rsqrt(jnp.mean(centred * centred, axis=-1, keepdims=True) + EPS)
    return centred * inv, inv


def norm_back(value, gain, grad):
    hat, inv = normed(value)
    scaled = grad * gain
    back = inv * (
        scaled
        - jnp.mean(scaled, axis=-1, keepdims=True)
        - hat * jnp.mean(scaled * hat, axis=-1, keepdims=True)
    )
    return back, jnp.sum(grad * hat, axis=0, keepdims=True), jnp.sum(grad, axis=0, keepdims=True)


def gelu_parts(u):
    e = jnp.exp(-0.5 * u * u)
    t = 1.0 / (1.0 + (0.3275911 * 2.0**-0.5) * jnp.abs(u))
    poly = 0.5 * 1.061405429
    for term in (-1.453152027, 1.421413741, -0.284496736, 0.254829592):
        poly = poly * t + 0.5 * term
    tail = poly * t * e
    cdf = jnp.where(u >= 0.0, 1.0 - tail, tail)
    return cdf, cdf + u * (e * 0.3989422804014327)


def subsets(items):
    out = [()]
    for item in items:
        out = out + [s + (item,) for s in out]
    return sorted(out, key=len)


class Net:
    def __init__(self, n, nz, send, recv):
        self.n, self.nz = n, nz
        self.c = lax.axis_index("ctx")
        self.z = lax.axis_index("fsdp")
        self.send, self.recv = send, recv
        self.used = 0
        self.named = {}
        self.sent = []
        self.hops = []
        bit = n // 2
        while bit > 1:
            self.hops.append(bit)
            bit //= 2
        self.delta = {b: b - 2 * b * ((self.c // b) % 2) for b in self.hops + [1]}

    def slots(self, count):
        first = self.used
        self.used += count
        return first

    def slot(self, *key):
        if key not in self.named:
            self.named[key] = self.slots(1)
        return self.named[key]

    def at(self, places):
        index = self.c
        for place in places:
            index = index + self.delta[place]
        return index

    def copy(self, src, dst, slot, ctx=None, fsdp=None):
        return pltpu.make_async_remote_copy(
            src_ref=src,
            dst_ref=dst,
            send_sem=self.send.at[slot],
            recv_sem=self.recv.at[slot],
            device_id=(self.c if ctx is None else ctx, self.z if fsdp is None else fsdp),
            device_id_type=pl.DeviceIdType.MESH,
        )

    def go(self, *args, **kw):
        made = self.copy(*args, **kw)
        made.start()
        self.sent.append(made)

    def arrived(self, ref, slot):
        self.copy(ref, ref, slot).wait_recv()

    def drain(self):
        for made in self.sent:
            made.wait_send()
        self.sent = []

    def greet(self):
        barrier = pltpu.get_barrier_semaphore()
        for d in range(1, self.n):
            pl.semaphore_signal(
                barrier, inc=1, device_id=(lax.rem(self.c + d, self.n), self.z), device_id_type=pl.DeviceIdType.MESH
            )
        for d in range(1, self.nz):
            pl.semaphore_signal(
                barrier, inc=1, device_id=(self.c, lax.rem(self.z + d, self.nz)), device_id_type=pl.DeviceIdType.MESH
            )
        pl.semaphore_wait(barrier, self.n + self.nz - 2)

    def cuts(self, columns):
        count = max(1, len(self.hops))
        units = columns // LANES
        out, first = [], 0
        for k in range(count):
            size = (units * (k + 1) // count - units * k // count) * LANES
            out.append(pl.ds(first, size))
            first += size
        return out

    def turned(self, k):
        return self.hops[k:] + self.hops[:k]


class Gather:
    def __init__(self, net, buf, pool):
        self.net, self.buf = net, buf
        self.parts = net.cuts(buf.shape[2])
        self.sent = []
        self.slot = {}
        self.slot["own"] = net.slot(pool, "own")
        for k in range(len(self.parts)):
            for s in subsets(net.turned(k)):
                if s:
                    self.slot[k, s, "hop"] = net.slot(pool, k, s, "hop")
                    self.slot[k, s, "core"] = net.slot(pool, k, s, "core")

    def go(self, *args, **kw):
        made = self.net.copy(*args, **kw)
        made.start()
        self.sent.append(made)

    def drain(self):
        for made in self.sent:
            made.wait_send()
        self.sent = []

    def ref(self, k, s):
        return self.buf.at[self.net.at(s), :, self.parts[k]]

    def forward(self, k, s, core):
        net = self.net
        order = net.turned(k)
        later = order[order.index(s[-1]) + 1:] if s else order
        for hop in later:
            ref = self.ref(k, s)
            self.go(ref, ref, self.slot[k, s + (hop,), "hop"], ctx=net.at((hop,)))
        if core:
            ref = self.ref(k, s)
            self.go(ref, ref, self.slot[k, s, "core"], ctx=net.at((1,)))

    def start(self):
        net = self.net
        for k in range(len(self.parts)):
            if net.hops:
                self.forward(k, (), False)
        own = self.buf.at[net.c]
        self.go(own, own, self.slot["own"], ctx=net.at((1,)))

    def level(self, m):
        net = self.net
        for k in range(len(self.parts)):
            for s in subsets(net.turned(k)):
                if len(s) == m:
                    net.arrived(self.ref(k, s), self.slot[k, s, "hop"])
                    self.forward(k, s, True)

    def levels(self):
        for m in range(1, len(self.net.hops) + 1):
            self.level(m)

    def done(self):
        net = self.net
        net.arrived(self.buf.at[net.at((1,))], self.slot["own"])
        for k in range(len(self.parts)):
            for s in subsets(net.turned(k)):
                if s:
                    net.arrived(self.ref(k, s + (1,)), self.slot[k, s, "core"])

    def finish(self):
        self.levels()
        self.done()


class Scatter:
    def __init__(self, net, part, came, pool):
        self.net, self.part, self.came = net, part, came
        self.parts = net.cuts(part.shape[2])
        self.sets = subsets(net.hops)[::-1]
        if (pool, "base") not in net.named:
            net.named[pool, "base"] = net.slots(len(self.sets))
        self.base = net.named[pool, "base"]
        self.slot = {}
        for k in range(len(self.parts)):
            for step in range(len(net.hops)):
                for s in subsets(net.turned(k)[step:]):
                    if net.turned(k)[step] in s:
                        self.slot[k, s] = net.slot(pool, k, s)
        self.sent = []

    def go(self, *args, **kw):
        made = self.net.copy(*args, **kw)
        made.start()
        self.sent.append(made)

    def chip(self, k):
        net = self.net
        count = len(net.hops)
        index = 0
        turn = len(self.sets) - 1 - k
        for j, hop in enumerate(net.hops):
            far = (turn // (2 ** (count - 1 - j))) % 2
            index = index + hop * (((net.c // hop) + far) % 2)
        return index

    def sets_of(self, k):
        net = self.net
        count = len(net.hops)
        turn = len(self.sets) - 1 - k
        return tuple(hop for j, hop in enumerate(net.hops) if (turn // (2 ** (count - 1 - j))) % 2)

    def core_copy(self, k):
        net = self.net
        first = self.chip(k)
        mine = lax.rem(net.c, 2)
        return net.copy(
            self.part.at[first + 1 - mine], self.came.at[first + mine], self.base + k, ctx=net.at((1,))
        )

    def push(self, k):
        self.core_copy(k).start()

    def fold(self):
        net = self.net
        part, came = self.part, self.came
        for k in range(len(self.sets)):
            s = self.sets_of(k)
            mine = net.at(s)
            other = net.at(s + (1,))
            net.arrived(came.at[other], self.base + k)
            part[mine] = (part[mine].astype(f32) + came[other].astype(f32)).astype(bf)
            for p in range(len(self.parts)):
                self.onward(p, 0, s)

    def onward(self, p, step, s):
        net = self.net
        order = net.turned(p)
        if step < len(order) and order[step] in s:
            key = tuple(h for h in order if h in s)
            rest = tuple(h for h in s if h != order[step])
            cut = self.parts[p]
            self.go(
                self.part.at[net.at(s), :, cut],
                self.came.at[net.at(rest), :, cut],
                self.slot[p, key],
                ctx=net.at((order[step],)),
            )

    def reduce(self, result):
        net = self.net
        part, came = self.part, self.came
        count = len(net.hops)
        for step in range(count):
            for p in range(len(self.parts)):
                order = net.turned(p)
                cut = self.parts[p]
                for s in subsets(order[step + 1:])[::-1]:
                    far = s + (order[step],)
                    key = tuple(h for h in order if h in far)
                    net.arrived(came.at[net.at(far), :, cut], self.slot[p, key])
                    total = part[net.at(s), :, cut].astype(f32) + came[net.at(far), :, cut].astype(f32)
                    if step == count - 1:
                        result(cut, total)
                    else:
                        part[net.at(s), :, cut] = total.astype(bf)
                        self.onward(p, step + 1, s)
        if not count:
            result(slice(None), part[net.c].astype(f32))

    def drain(self):
        for k in range(len(self.sets)):
            self.core_copy(k).wait_send()
        for made in self.sent:
            made.wait_send()
        self.sent = []


def count_slots(n, nz):
    hops = n.bit_length() - 2
    trees = 1 + max(1, hops) * 2 * (2**hops - 1)
    sums = 2**hops + max(1, hops) * (2**hops - 1)
    return 2 * trees + 2 * sums + 12 * (nz - 1) + 6 * (n - 1) + n.bit_length() + nz.bit_length() - 2


def layer(dims, *refs):
    (n, nz, t, te, w, fw, hpd) = dims
    (x_ref, e_ref, g_ref, segd_ref, segs_ref, wsl_ref, up_ref, down_ref, vec_ref,
     mixed_ref, gtok_ref, genc_ref, fu, fd, fas, fac, fos, foc, vt, hold1, hold2,
     n1x, ex, n2f, wbuf, wo, wup, wdown,
     qa1, ka1, v1, vt1, ot1, ob1, lse1, qa2, ka2, v2, vt2, ot2, ob2, lse2,
     x1, x2, pa, ra, pm, rm, dy2f,
     act, du, gu, gd, gas, gac, gos, goc, ru, rd, ras, rac, ros, roc,
     vcame, dlt, dqacc, bias_ref, bup_ref,
     send, recv, local) = refs
    length, lenc = n * t, n * te
    share = D // (n * nz)
    dz = D // nz
    nq, nk2 = length // TILE, lenc // TILE
    nbt, nbe = TILE // t, TILE // te
    net = Net(n, nz, send, recv)
    c, z = net.c, net.z
    lane = lax.broadcasted_iota(jnp.int32, (1, LANES), 1)

    dqkv, dq2, dkv2 = act.at[:, pl.ds(0, 384)], act.at[:, pl.ds(0, LANES)], act.at[pl.ds(0, lenc), pl.ds(LANES, 256)]
    dom = [du.at[:, pl.ds(h * LANES, LANES)] for h in range(hpd)]
    dx = gtok_ref

    def wor_of(j, cc):
        return pm.at[cc, pl.ds(0, w), pl.ds(j * LANES, LANES)]

    wide = -(-n * LANES // D)

    def row(k):
        return vec_ref[k:k + 1, :]

    def into(ref):
        def store(cut, total):
            ref[:, cut] = total
        return store

    zrows = pl.ds(pl.multiple_of(z * dz, dz), dz)
    fcols = pl.ds(pl.multiple_of(c * fw, LANES), fw)

    def local_copy(src, dst, k):
        made = pltpu.make_async_copy(src, dst, local.at[k])
        made.start()
        return made

    if w == LANES:
        own_cols = [
            local_copy(
                wsl_ref.at[:, pl.ds(pl.multiple_of(block * D + c * LANES, LANES), LANES)],
                wbuf.at[zrows, pl.ds(k * LANES, LANES)], k)
            for k, block in enumerate(ORDER)
        ]
    else:
        own_cols = [local_copy(wsl_ref, wbuf.at[zrows, :], 0)]
    own_feed = [
        local_copy(up_ref.at[:, fcols], wup.at[zrows, :], 8),
        local_copy(down_ref.at[:, fcols], wdown.at[zrows, :], 9),
    ]
    net.greet()

    groups = ((0, 384), (384, 256), (640, 256), (896, 128))
    wslots = [net.slots(nz - 1) - 1 for _ in groups]
    upslot, downslot = net.slots(nz - 1) - 1, net.slots(nz - 1) - 1
    def push_z(src, dst, slot):
        for d in range(1, nz):
            net.go(src, dst, slot + d, fsdp=lax.rem(z + d, nz))

    def await_z(dst_of, slot):
        for d in range(1, nz):
            net.arrived(dst_of(lax.rem(z + nz - d, nz)), slot + d)

    def weight_rows(zz, k):
        first, size = groups[k]
        return wbuf.at[pl.ds(pl.multiple_of(zz * dz, dz), dz), pl.ds(first, size)]

    def push_weights(k):
        first, size = groups[k]
        push_z(weight_rows(z, k), weight_rows(z, k), wslots[k])

    for made in own_cols:
        made.wait()
    push_weights(0)

    hat, _ = normed(x_ref[...].astype(f32))
    n1x[c, :, pl.ds(0, D)] = (hat * row(0) + row(1)).astype(bf)

    def hot(seg, rows):
        place = lax.broadcasted_iota(jnp.int32, (LANES, rows), 0) % HD
        return jnp.where(place == seg[...], 1.0, 0.0).T.astype(bf)

    n1x[c, :, pl.ds(D, LANES)] = hot(segd_ref, t)
    gat1 = Gather(net, n1x, "main")
    gat1.start()
    ex[c, :, pl.ds(0, D)] = e_ref[...]
    ex[c, :, pl.ds(D, LANES)] = hot(segs_ref, te)
    for k in range(1, len(groups)):
        push_weights(k)
    vt[...] = jnp.zeros_like(vt)
    bias_ref[...] = jnp.zeros_like(bias_ref)
    for k, line in enumerate((6, 7, 9, 10)):
        own = vec_ref[line:line + 1, 0:w]
        for cc in range(1, n):
            own = jnp.where(c == cc, vec_ref[line:line + 1, cc * w:(cc + 1) * w], own)
        bias_ref[k:k + 1, 0:w] = own
    own = vec_ref[13:14, 0:fw]
    for cc in range(1, n):
        line, first = 13 + cc * fw // D, cc * fw % D
        own = jnp.where(c == cc, vec_ref[line:line + 1, first:first + fw], own)
    bup_ref[0:1, :] = own
    vt[8:9, :] = jnp.sum(g_ref[...].astype(f32), axis=0, keepdims=True)
    gat1.levels()
    gate = Gather(net, ex, "side")
    gate.start()
    gat1.done()
    await_z(lambda zz: weight_rows(zz, 0), wslots[0])

    def tile_of(buf, i, per, columns):
        return buf[pl.ds(i * per, per), :, columns].reshape(TILE, columns.size)

    head_of = lane // HD

    def put_q(qa, q, oh, rows):
        q = (q.astype(bf).astype(f32) * SCALE).astype(bf)
        for h in range(hpd):
            qa[h, rows, :] = jnp.where(head_of == h, q, oh)

    def put_k(ka, k, oh, rows):
        k = k.astype(bf)
        pen = ((oh.astype(f32) - 1.0) * -NEG).astype(bf)
        for h in range(hpd):
            ka[h, rows, :] = jnp.where(head_of == h, k, pen)

    def put_v(v, vt_ref, value, rows, i):
        value = value.astype(bf)
        v[rows, :] = value
        vt_ref[i] = value.astype(f32).T.astype(bf)

    def tile_rows(i):
        return pl.ds(pl.multiple_of(i * TILE, TILE), TILE)

    def qkv_tile(i, _):
        rows = tile_rows(i)
        got = dot(tile_of(n1x, i, nbt, pl.ds(0, D)), wbuf[:, 0:384])
        oh = tile_of(n1x, i, nbt, pl.ds(D, LANES))
        put_q(qa1, got[:, 0:128] + bias_ref[0:1, :], oh, rows)
        put_k(ka1, got[:, 128:256], oh, rows)
        put_v(v1, vt1, got[:, 256:384] + bias_ref[1:2, :], rows, i)
        return _

    lax.fori_loop(0, nq, qkv_tile, 0)

    gf, n3f, dy1f = n1x.at[:, :, pl.ds(0, D)], n2f, n2f

    away1 = local_copy(gf, hold1, 10)

    push_z(up_ref.at[:, fcols], wup.at[zrows, :], upslot)
    push_z(down_ref.at[:, fcols], wdown.at[zrows, :], downslot)

    def attend(qa, ka, vt_ref, ot, ob, lse, keys, causal):
        def one(j, _):
            qrows = tile_rows(j)

            def step(i, state, diagonal):
                out = []
                for h in range(hpd):
                    top, total, acc = state[h]
                    s = dot_t(ka[h, tile_rows(i), :], qa[h, qrows, :])
                    if diagonal:
                        kp = lax.broadcasted_iota(jnp.int32, (TILE, TILE), 0)
                        qp = lax.broadcasted_iota(jnp.int32, (TILE, TILE), 1)
                        s = jnp.where(kp <= qp, s, NEG)
                    new = jnp.maximum(top, jnp.max(s, axis=0, keepdims=True))
                    p = jnp.exp(s - new)
                    fix = jnp.exp(top - new)
                    total = total * fix + jnp.sum(p, axis=0, keepdims=True)
                    acc = acc * fix + dot(vt_ref[i, pl.ds(h * HD, HD), :], p.astype(bf))
                    out.append((new, total, acc))
                return tuple(out)

            state = tuple(
                (jnp.full((1, TILE), -3e38, f32), jnp.zeros((1, TILE), f32), jnp.zeros((HD, TILE), f32))
                for _ in range(hpd)
            )
            if causal:
                state = step(j, state, True)
                state = lax.fori_loop(0, j, lambda i, st: step(i, st, False), state)
            else:
                state = lax.fori_loop(0, keys, lambda i, st: step(i, st, False), state)
            for h in range(hpd):
                top, total, acc = state[h]
                ot[j, pl.ds(h * HD, HD), :] = acc * (1.0 / total)
                lse[j, h:h + 1, :] = top + jnp.log(total)
            ob[qrows, :] = ot[j].T.astype(bf)
            return _

        if hpd * HD < LANES:
            ot[...] = jnp.zeros_like(ot)
        lax.fori_loop(0, nq, one, 0)

    attend(qa1, ka1, vt1, ot1, ob1, lse1, nq, True)

    await_z(lambda zz: weight_rows(zz, 1), wslots[1])
    await_z(lambda zz: weight_rows(zz, 2), wslots[2])
    oslots = [net.slots(n - 1) - 1, net.slots(n - 1) - 1]

    def out_rows(j, cc):
        return wbuf.at[pl.ds(pl.multiple_of(cc * w, w), w), pl.ds(640 + j * LANES, LANES)]

    for j in range(2):
        for d in range(1, n):
            peer = lax.rem(c + d, n)
            net.go(out_rows(j, peer), wor_of(j, c), oslots[j] + d, ctx=peer)
        wor_of(j, c)[...] = wbuf[pl.ds(pl.multiple_of(c * w, w), w), pl.ds(640 + j * LANES, LANES)]

    def await_out(j):
        for d in range(1, n):
            net.arrived(wor_of(j, lax.rem(c + n - d, n)), oslots[j] + d)
        if w < LANES:
            wo[j] = jnp.zeros((LANES, D), bf)
        wo[j, pl.ds(0, w), :] = jnp.concatenate(
            [pm[cc, pl.ds(0, w), pl.ds(j * LANES, LANES)][:, :w] for cc in range(n)], axis=-1)

    gate.finish()
    await_out(0)

    def partial(scat, rows_of, weight_of, per):
        def one(k, _):
            first = scat.chip(k)
            scat.part[pl.ds(first, 2)] = weight_of(rows_of(first)).astype(bf).reshape(2, per, D)
            scat.push(k)
            return _

        lax.fori_loop(0, n // 2, one, 0)

    def flat(buf, per):
        return lambda first: buf[pl.ds(pl.multiple_of(first * per, 2 * per), 2 * per), :]

    rs1 = Scatter(net, pa, ra, "sum")
    partial(rs1, flat(ob1, t), lambda rows: dot(rows, wo[0]), t)

    def kv2_tile(i, _):
        rows = tile_rows(i)
        got = dot(tile_of(ex, i, nbe, pl.ds(0, D)), wbuf[:, 384:640])
        oh = tile_of(ex, i, nbe, pl.ds(D, LANES))
        put_k(ka2, got[:, 0:128], oh, rows)
        put_v(v2, vt2, got[:, 128:256] + bias_ref[3:4, :], rows, i)
        return _

    rs1.fold()
    lax.fori_loop(0, nk2, kv2_tile, 0)
    rs1.reduce(into(x1))
    x1[...] = x_ref[...].astype(f32) + (x1[...] + row(8))
    hat, _ = normed(x1[...])
    n2f[c] = (hat * row(2) + row(3)).astype(bf)
    gat1.drain()
    away1.wait()
    gat2 = Gather(net, n2f, "main")
    gat2.start()
    rs1.drain()
    gate.drain()
    await_out(1)
    await_z(lambda zz: weight_rows(zz, 3), wslots[3])
    gat2.finish()
    gf[c] = g_ref[...]
    gatg = Gather(net, gf, "side")
    gatg.start()

    def q2_tile(i, _):
        got = dot(tile_of(n2f, i, nbt, pl.ds(0, D)), wbuf[:, 896:1024])
        put_q(qa2, got + bias_ref[2:3, :], tile_of(n1x, i, nbt, pl.ds(D, LANES)), tile_rows(i))
        return _

    lax.fori_loop(0, nq, q2_tile, 0)
    away2 = local_copy(n2f, hold2, 11)
    gatg.level(1)
    attend(qa2, ka2, vt2, ot2, ob2, lse2, nk2, False)
    away2.wait()
    gat2.drain()
    rs2 = Scatter(net, pa, ra, "sum")
    partial(rs2, flat(ob2, t), lambda rows: dot(rows, wo[1]), t)
    for m in range(2, len(net.hops) + 1):
        gatg.level(m)
    rs2.fold()
    rs2.reduce(into(x2))
    x2[...] = x1[...] + (x2[...] + row(11))
    hat, _ = normed(x2[...])
    n3f[c] = (hat * row(4) + row(5)).astype(bf)
    gat3 = Gather(net, n3f, "main")
    gat3.start()
    rs2.drain()
    gatg.done()
    for made in own_feed:
        made.wait()
    gat3.finish()
    await_z(lambda zz: wup.at[pl.ds(pl.multiple_of(zz * dz, dz), dz), :], upslot)
    await_z(lambda zz: wdown.at[pl.ds(pl.multiple_of(zz * dz, dz), dz), :], downslot)

    rs3 = Scatter(net, pa, ra, "sum")
    rsm = Scatter(net, pm, rm, "sum2")
    fc = min(fw, 512)

    def feed_tile(k, sums):
        first = rs3.chip(k)
        rows = pl.ds(pl.multiple_of(first * t, 2 * t), 2 * t)
        left = n3f[pl.ds(first, 2)].reshape(2 * t, D)
        grad = gf[pl.ds(first, 2)].reshape(2 * t, D)
        out = []
        for f in range(fw // fc):
            cols = pl.ds(f * fc, fc)
            u = dot(left, wup[:, cols]) + bup_ref[0:1, cols]
            cdf, slope = gelu_parts(u)
            act[rows, cols] = (u * cdf).astype(bf)
            low = (dot(grad, wdown[:, cols]) * slope).astype(bf)
            du[rows, cols] = low
            out.append(sums[f] + jnp.sum(low.astype(f32), axis=0, keepdims=True))
        pa[pl.ds(first, 2)] = dot_t(du[rows, :], wup[...]).astype(bf).reshape(2, t, D)
        rs3.push(k)
        return tuple(out)

    sums = lax.fori_loop(0, n // 2, feed_tile, tuple(jnp.zeros((1, fc), f32) for _ in range(fw // fc)))
    for f in range(fw // fc):
        for cc in range(n):
            place = cc * fw + f * fc
            line = 9 + 4 * wide + place // D
            vt[line:line + 1, pl.ds(place % D, fc)] = jnp.where(c == cc, sums[f], 0.0)
    rs3.fold()
    partial(rsm, flat(act, t), lambda rows: dot_t(rows, wdown[...]), t)
    rsm.fold()

    per = TILE // (share * nz)

    def weight_grad(left_of, right, out, columns):
        def one(r, _):
            got = t_dot(left_of(tile_rows(r)), right())
            for k in range(TILE // share):
                out[k % nz, r * per + k // nz, :, columns] = got[k * share:(k + 1) * share].astype(bf)
            return _

        lax.fori_loop(0, D // TILE, one, 0)

    def whole(buf, rows):
        return lambda cols: buf[:, :, cols].reshape(rows, TILE)

    zslots = [net.slots(nz - 1) - 1 for _ in range(6)]

    def push_grad(mine, came, k):
        for d in range(1, nz):
            peer = lax.rem(z + d, nz)
            net.go(mine.at[peer], came.at[z], zslots[k] + d, fsdp=peer)

    def sum_grad(mine, came, k):
        total = mine[z].astype(f32)
        for d in range(1, nz):
            peer = lax.rem(z + nz - d, nz)
            net.arrived(came.at[peer], zslots[k] + d)
            total = total + came[peer].astype(f32)
        return total.astype(bf)

    weight_grad(whole(n3f, length), lambda: du[...], gu, pl.ds(0, fw))
    push_grad(gu, ru, 0)
    gat3.drain()
    gatg.drain()
    rs3.reduce(into(dx))
    back, gain_g, shift_g = norm_back(x2[...], row(4), dx[...])
    vt[4:5, :] = gain_g
    vt[5:6, :] = shift_g
    dx[...] = g_ref[...].astype(f32) + back
    dy = dx[...].astype(bf)
    dy2f[c] = dy
    gat4 = Gather(net, dy2f, "main")
    gat4.start()
    vt[7:8, :] = jnp.sum(dy.astype(f32), axis=0, keepdims=True)
    rs3.drain()
    gat4.levels()
    weight_grad(whole(gf, length), lambda: act[...], gd, pl.ds(0, fw))
    push_grad(gd, rd, 1)
    back2 = local_copy(hold2, gf, 12)

    def store_mixed(cut, total):
        mixed_ref[:, cut] = (x2[:, cut] + (total + vec_ref[12:13, cut])).astype(bf)

    rsm.reduce(store_mixed)
    gat4.done()

    def attend_back(qa, ka, v, ot, lse, dyf, out_w, keys, causal, dq_ref, dq_cols, dkv_ref, dk_cols, dv_cols):
        def grads(i, _):
            rows = tile_rows(i)
            low = dot_t(tile_of(dyf, i, nbt, pl.ds(0, D)), out_w[...]).astype(bf)
            for h in range(hpd):
                dom[h][rows, :] = jnp.where(head_of == h, low, jnp.zeros_like(low))
            prod = low.astype(f32).T * ot[i]
            for h in range(hpd):
                dlt[i, h:h + 1, :] = jnp.sum(prod[h * HD:(h + 1) * HD], axis=0, keepdims=True)
            dqacc[rows, :] = jnp.zeros((TILE, LANES), f32)
            return _

        lax.fori_loop(0, nq, grads, 0)

        def one(i, _):
            krows = tile_rows(i)

            def step(j, state, diagonal):
                qrows = tile_rows(j)
                dv, dks = state
                new_dks, dqs = [], []
                for h in range(hpd):
                    s = dot_t(ka[h, krows, :], qa[h, qrows, :])
                    p = jnp.exp(s - lse[j, h:h + 1, :])
                    if diagonal:
                        kp = lax.broadcasted_iota(jnp.int32, (TILE, TILE), 0)
                        qp = lax.broadcasted_iota(jnp.int32, (TILE, TILE), 1)
                        p = jnp.where(kp <= qp, p, 0.0)
                    dp = dot_t(v[krows, :], dom[h][qrows, :])
                    ds = (p * (dp - dlt[j, h:h + 1, :])).astype(bf)
                    dv = dv + dot(p.astype(bf), dom[h][qrows, :])
                    new_dks.append(dks[h] + dot(ds, qa[h, qrows, :]))
                    dqs.append(t_dot(ds, ka[h, krows, :]))
                dq = jnp.where(head_of == 0, dqs[0], dqs[-1] if hpd > 1 else 0.0)
                dqacc[qrows, :] = dqacc[qrows, :] + dq
                return dv, tuple(new_dks)

            zero = jnp.zeros((TILE, LANES), f32)
            state = (zero, tuple(zero for _ in range(hpd)))
            if causal:
                state = step(i, state, True)
                state = lax.fori_loop(i + 1, nq, lambda j, st: step(j, st, False), state)
            else:
                state = lax.fori_loop(0, nq, lambda j, st: step(j, st, False), state)
            dv, dks = state
            dk = jnp.where(head_of == 0, dks[0], dks[-1] if hpd > 1 else 0.0)
            dkv_ref[krows, dk_cols] = dk.astype(bf)
            dkv_ref[krows, dv_cols] = dv.astype(bf)
            return _

        lax.fori_loop(0, keys, one, 0)

        def close(i, _):
            rows = tile_rows(i)
            dq_ref[rows, dq_cols] = (dqacc[rows, :] * SCALE).astype(bf)
            return _

        lax.fori_loop(0, nq, close, 0)

    def head_sum(k, ref, cols):
        own = jnp.sum(ref[:, cols].astype(f32), axis=0, keepdims=True)
        for cc in range(n):
            line = 9 + k * wide + cc * LANES // D
            vt[line:line + 1, pl.ds(cc * LANES % D, LANES)] = jnp.where(c == cc, own, 0.0)

    first3 = [pl.ds(k * LANES, LANES) for k in range(3)]
    attend_back(qa2, ka2, v2, ot2, lse2, dy2f, wo.at[1], nk2, False, dq2, first3[0], dkv2, first3[0], first3[1])
    rs4 = Scatter(net, pa, ra, "sum")
    partial(rs4, flat(dq2, t), lambda rows: dot_t(rows, wbuf[:, 896:1024]), t)
    rs4.fold()

    weight_grad(whole(ex, lenc), lambda: dkv2[...], gac, pl.ds(0, 256))
    back2.wait()
    weight_grad(whole(gf, length), lambda: dq2[...], gac, pl.ds(256, 128))
    back1 = local_copy(hold1, gf, 13)
    push_grad(gac, rac, 2)

    def out_grad(ob, dyf, out):
        for cut in (0, 1):
            cols = pl.ds(cut * (D // 2), D // 2)
            got = t_dot(ob[...], dyf[:, :, cols].reshape(length, D // 2))
            for k in range(nz):
                out[k, :, cols] = got[k * share:(k + 1) * share].astype(bf)

    rs4.reduce(into(x2))
    back, gain_g, shift_g = norm_back(x1[...], row(2), x2[...])
    vt[2:3, :] = gain_g
    vt[3:4, :] = shift_g
    dx[...] = dx[...] + back
    dy = dx[...].astype(bf)
    dy1f[c] = dy
    gat4.drain()
    gat5 = Gather(net, dy1f, "main")
    gat5.start()
    vt[6:7, :] = jnp.sum(dy.astype(f32), axis=0, keepdims=True)
    head_sum(2, dq2, first3[0])
    head_sum(3, dkv2, first3[1])
    rs4.drain()
    rsm.drain()
    rse = Scatter(net, pm.at[:, pl.ds(0, te), :], rm.at[:, pl.ds(0, te), :], "sum2")
    partial(rse, flat(dkv2, te), lambda rows: dot_t(rows, wbuf[:, 384:640]), te)
    gat5.levels()
    rse.fold()
    out_grad(ob2, dy2f, goc)
    push_grad(goc, roc, 3)
    rse.reduce(into(genc_ref))
    gat5.done()
    attend_back(qa1, ka1, v1, ot1, lse1, dy1f, wo.at[0], nq, True, dqkv, first3[0], dqkv, first3[1], first3[2])
    rs5 = Scatter(net, pa, ra, "sum")
    partial(rs5, flat(dqkv, t), lambda rows: dot_t(rows, wbuf[:, 0:384]), t)
    rs5.fold()
    back1.wait()
    weight_grad(whole(gf, length), lambda: dqkv[...], gas, pl.ds(0, 384))
    push_grad(gas, ras, 4)
    out_grad(ob1, dy1f, gos)
    push_grad(gos, ros, 5)
    rs5.reduce(into(x2))
    back, gain_g, shift_g = norm_back(x_ref[...].astype(f32), row(0), x2[...])
    vt[0:1, :] = gain_g
    vt[1:2, :] = shift_g
    gtok_ref[...] = dx[...] + back
    head_sum(0, dqkv, first3[0])
    head_sum(1, dqkv, first3[2])

    vslots = net.slots(vcame.shape[0])
    pairs = [("ctx", b) for b in net.hops + [1]] + [("fsdp", 1 << k) for k in range(nz.bit_length() - 1)]

    def swap(k):
        axis, b = pairs[k]
        own = c if axis == "ctx" else z
        peer = own + b - 2 * b * ((own // b) % 2)
        made = net.copy(vt, vcame.at[k], vslots + k, **{axis: peer})
        made.start()
        return made

    def merge(k, made):
        made.wait_send()
        net.arrived(vcame.at[k], vslots + k)
        vt[...] = vt[...] + vcame[k]

    def exchange(mine, came, k, out):
        slot = net.slots(n - 1) - 1
        mine[z] = sum_grad(mine, came, k)
        out[c] = mine[z, c]
        for d in range(1, n):
            peer = lax.rem(c + d, n)
            net.go(mine.at[z, peer], out.at[c], slot + d, ctx=peer)

        def done():
            for d in range(1, n):
                net.arrived(out.at[lax.rem(c + n - d, n)], slot + d)
        return done

    waits = []
    todo = [
        lambda: waits.append(exchange(gu, ru, 0, fu)),
        lambda: waits.append(exchange(gd, rd, 1, fd)),
        lambda: waits.append(exchange(gac, rac, 2, fac)),
    ]
    for k in range(len(pairs)):
        made = swap(k)
        if todo:
            todo.pop(0)()
        merge(k, made)
    for step in todo:
        step()
    foc[...] = sum_grad(goc, roc, 3)
    waits.append(exchange(gas, ras, 4, fas))
    fos[...] = sum_grad(gos, ros, 5)
    for wait in waits:
        wait()
    rs5.drain()
    rse.drain()
    gat5.drain()
    net.drain()
    assert net.used == count_slots(n, nz)


def body(tokens, encoder, dec_seg, src_seg, attn_w, up_w, down_w, vec, cot):
    n, nz = lax.axis_size("ctx"), lax.axis_size("fsdp")
    c = lax.axis_index("ctx")
    t, te = tokens.shape[1], encoder.shape[1]
    ff = up_w.shape[1]
    w, fw = D // n, ff // n
    hpd = w // HD
    dz = D // nz
    share = D // (n * nz)
    length, lenc = n * t, n * te

    if w < LANES:
        wsl = lax.dynamic_slice_in_dim(attn_w.reshape(dz, 8, D), c * w, w, axis=2)
        wsl = jnp.stack([wsl[:, k] for k in ORDER], axis=1)
        attn_w = jnp.pad(wsl, ((0, 0), (0, 0), (0, LANES - w))).reshape(dz, 8 * LANES)

    nq, nk2 = length // TILE, lenc // TILE
    slots = count_slots(n, nz)
    dims = (n, nz, t, te, w, fw, hpd)
    wide = -(-n * LANES // D)
    vrows = -(-(9 + 4 * wide + ff // D) // 8) * 8
    steps = n.bit_length() + nz.bit_length() - 2
    out_shape = (
        jax.ShapeDtypeStruct((t, D), bf),
        jax.ShapeDtypeStruct((t, D), f32),
        jax.ShapeDtypeStruct((te, D), f32),
        jax.ShapeDtypeStruct((n, share, fw), bf),
        jax.ShapeDtypeStruct((n, share, fw), bf),
        jax.ShapeDtypeStruct((n, share, 384), bf),
        jax.ShapeDtypeStruct((n, share, 384), bf),
        jax.ShapeDtypeStruct((share, D), bf),
        jax.ShapeDtypeStruct((share, D), bf),
        jax.ShapeDtypeStruct((vrows, D), f32),
        jax.ShapeDtypeStruct((n, t, D), bf),
        jax.ShapeDtypeStruct((n, t, D), bf),
    )

    def attn_scratch(keys):
        return [
            pltpu.VMEM((hpd, length, LANES), bf), pltpu.VMEM((hpd, keys, LANES), bf), pltpu.VMEM((keys, LANES), bf),
            pltpu.VMEM((keys // TILE, LANES, TILE), bf), pltpu.VMEM((nq, LANES, TILE), f32),
            pltpu.VMEM((length, LANES), bf), pltpu.VMEM((nq, 8, TILE), f32),
        ]

    scratch = [
        pltpu.VMEM((n, t, D + LANES), bf), pltpu.VMEM((n, te, D + LANES), bf), pltpu.VMEM((n, t, D), bf),
        pltpu.VMEM((D, 8 * LANES), bf), pltpu.VMEM((2, LANES, D), bf),
        pltpu.VMEM((D, fw), bf), pltpu.VMEM((D, fw), bf),
        *attn_scratch(length), *attn_scratch(lenc),
        pltpu.VMEM((t, D), f32), pltpu.VMEM((t, D), f32),
        pltpu.VMEM((n, t, D), bf), pltpu.VMEM((n, t, D), bf), pltpu.VMEM((n, t, D), bf), pltpu.VMEM((n, t, D), bf),
        pltpu.VMEM((n, t, D), bf),
        pltpu.VMEM((length, fw), bf), pltpu.VMEM((length, fw), bf),
    ]
    for _ in range(2):
        scratch += [
            pltpu.VMEM((nz, n, share, fw), bf), pltpu.VMEM((nz, n, share, fw), bf),
            pltpu.VMEM((nz, n, share, 384), bf), pltpu.VMEM((nz, n, share, 384), bf),
            pltpu.VMEM((nz, share, D), bf), pltpu.VMEM((nz, share, D), bf),
        ]
    scratch += [
        pltpu.VMEM((steps, vrows, D), f32),
        pltpu.VMEM((nq, 8, TILE), f32), pltpu.VMEM((length, LANES), f32),
        pltpu.VMEM((8, LANES), f32), pltpu.VMEM((8, fw), f32),
        pltpu.SemaphoreType.DMA((slots,)), pltpu.SemaphoreType.DMA((slots,)), pltpu.SemaphoreType.DMA((16,)),
    ]
    vmem = pl.BlockSpec(memory_space=pltpu.VMEM)
    hbm = pl.BlockSpec(memory_space=pl.ANY)
    mixed, gtok, genc, fu, fd, fas, fac, fos, foc, vsum, _, _ = pl.pallas_call(
        functools.partial(layer, dims),
        out_shape=out_shape,
        in_specs=[vmem] * 5 + [hbm] * 3 + [vmem],
        out_specs=[vmem] * (len(out_shape) - 2) + [hbm] * 2,
        scratch_shapes=scratch,
        compiler_params=pltpu.CompilerParams(
            collective_id=0, has_side_effects=True, vmem_limit_bytes=63 * 1024 * 1024
        ),
        cost_estimate=pl.CostEstimate(flops=21_000_000_000, bytes_accessed=30_000_000, transcendentals=8_000_000),
        name="layer",
    )(tokens[0], encoder[0], cot[0], dec_seg, src_seg, attn_w, up_w, down_w, vec)

    return pl.pallas_call(
        functools.partial(closing, (n, w, fw, wide)),
        out_shape=(
            jax.ShapeDtypeStruct((1, t, D), bf), jax.ShapeDtypeStruct((1, t, D), f32),
            jax.ShapeDtypeStruct((1, te, D), f32), jax.ShapeDtypeStruct((share, 8 * D), f32),
            jax.ShapeDtypeStruct((share, ff), f32), jax.ShapeDtypeStruct((share, ff), f32),
            jax.ShapeDtypeStruct(vec.shape, f32),
        ),
        in_specs=[hbm] * 10,
        out_specs=[hbm] * 7,
        scratch_shapes=[pltpu.VMEM(a.shape, a.dtype) for a in (mixed, gtok, genc, fu, fd, fas, fac, fos, foc, vsum)] + [
            pltpu.VMEM((share, 8 * D), f32), pltpu.VMEM((share, ff), f32), pltpu.VMEM((share, ff), f32),
            pltpu.VMEM(vec.shape, f32), pltpu.SemaphoreType.DMA((17,)),
        ],
        compiler_params=pltpu.CompilerParams(vmem_limit_bytes=62 * 1024 * 1024),
        name="closing",
    )(mixed, gtok, genc, fu, fd, fas, fac, fos, foc, vsum)


def closing(dims, *refs):
    n, w, fw, wide = dims
    given, outs, kept, made, sems = refs[:10], refs[10:17], refs[17:27], refs[27:31], refs[31]
    coming = [pltpu.make_async_copy(given[k], kept[k], sems.at[k]) for k in range(10)]
    straight = [pltpu.make_async_copy(kept[k], outs[k].at[0], sems.at[10 + k]) for k in range(3)]
    going = [pltpu.make_async_copy(made[k], outs[3 + k], sems.at[13 + k]) for k in range(4)]
    for copy in coming:
        copy.start()
    for k in range(3):
        coming[k].wait()
        straight[k].start()
    kept, coming = kept[3:], coming[3:]
    fu, fd, fas, fac, fos, foc, vsum = kept
    o_attn, o_up, o_down, o_vec = made
    coming[0].wait()
    for cc in range(n):
        o_up[:, pl.ds(cc * fw, fw)] = fu[cc].astype(f32)
    going[1].start()
    coming[1].wait()
    for cc in range(n):
        o_down[:, pl.ds(cc * fw, fw)] = fd[cc].astype(f32)
    going[2].start()
    for k in range(2, 7):
        coming[k].wait()
    for block, (ref, k) in enumerate(
        ((fas, 0), (fas, 1), (fas, 2), (fos, None), (fac, 2), (fac, 0), (fac, 1), (foc, None))
    ):
        if k is None:
            got = ref[...]
        else:
            got = jnp.concatenate([ref[cc, :, pl.ds(k * LANES, LANES)][:, :w] for cc in range(n)], axis=-1)
        o_attn[:, pl.ds(block * D, D)] = got.astype(f32)
    going[0].start()

    def heads(k):
        parts = []
        for cc in range(n):
            line, first = 9 + k * wide + cc * LANES // D, cc * LANES % D
            parts.append(vsum[line:line + 1, first:first + LANES][:, :w])
        return jnp.concatenate(parts, axis=-1)

    o_vec[0:6] = vsum[0:6]
    o_vec[6:7] = heads(0)
    o_vec[7:8] = heads(1)
    o_vec[8:9] = vsum[6:7]
    o_vec[9:10] = heads(2)
    o_vec[10:11] = heads(3)
    o_vec[11:13] = vsum[7:9]
    up = 9 + 4 * wide
    o_vec[13:] = vsum[up:up + o_vec.shape[0] - 13]
    going[3].start()
    for copy in straight + going:
        copy.wait()


def solution(mesh):
    return jax.shard_map(
        body, mesh=mesh,
        in_specs=(P("fsdp", "ctx", None), P("fsdp", "ctx", None), P("fsdp", "ctx"), P("fsdp", "ctx"), P("fsdp", None),
                  P("fsdp", None), P("fsdp", None), P(), P("fsdp", "ctx", None)),
        out_specs=(P("fsdp", "ctx", None), P("fsdp", "ctx", None), P("fsdp", "ctx", None), P(("ctx", "fsdp"), None),
                   P(("ctx", "fsdp"), None), P(("ctx", "fsdp"), None), P()),
        check_vma=False,
    )
```

```python
import functools

import jax
import jax.numpy as jnp
from jax import lax
from jax.experimental import pallas as pl
from jax.experimental.pallas import tpu as pltpu
from jax.sharding import PartitionSpec as P

D = 1024
HD = 64
LANES = 128
TILE = 256
EXTRAS = 16
EPS = 1e-05
NEG = -1e30
SCALE = HD ** (-0.5)
bf = jnp.bfloat16
f32 = jnp.float32
ORDER = (0, 1, 2, 3, 5, 6, 7, 4)
OUT_AT = (384, 768)


def dot(a, b):
    return jnp.dot(a, b, preferred_element_type=f32)


def dot_t(a, b):
    return lax.dot_general(a, b, (((1,), (1,)), ((), ())), preferred_element_type=f32)


def t_dot(a, b):
    return lax.dot_general(a, b, (((0,), (0,)), ((), ())), preferred_element_type=f32)


def normed(value):
    centred = value - jnp.mean(value, axis=-1, keepdims=True)
    inv = lax.rsqrt(jnp.mean(centred * centred, axis=-1, keepdims=True) + EPS)
    return centred * inv, inv


def norm_back(value, gain, grad):
    hat, inv = normed(value)
    scaled = grad * gain
    back = inv * (
        scaled
        - jnp.mean(scaled, axis=-1, keepdims=True)
        - hat * jnp.mean(scaled * hat, axis=-1, keepdims=True)
    )
    return back, jnp.sum(grad * hat, axis=0, keepdims=True), jnp.sum(grad, axis=0, keepdims=True)


def gelu_parts(u):
    e = jnp.exp(-0.5 * u * u)
    t = 1.0 / (1.0 + (0.3275911 * 2.0**-0.5) * jnp.abs(u))
    poly = 0.5 * 1.061405429
    for term in (-1.453152027, 1.421413741, -0.284496736, 0.254829592):
        poly = poly * t + 0.5 * term
    tail = poly * t * e
    cdf = jnp.where(u >= 0.0, 1.0 - tail, tail)
    return cdf, cdf + u * (e * 0.3989422804014327)


def subsets(items):
    out = [()]
    for item in items:
        out = out + [s + (item,) for s in out]
    return sorted(out, key=len)


class Net:
    def __init__(self, n, nz, q, send, recv):
        self.n, self.nz = n, nz
        self.c = lax.axis_index("ctx")
        self.z = lax.axis_index("fsdp")
        self.send, self.recv = send, recv
        self.used = self.extras = 0
        self.named = {}
        self.sent = []
        hops = [n >> k for k in range(1, n.bit_length() - 1)]
        self.parity = lax.rem(self.z, q)
        self.delta = {b: b - 2 * b * ((self.c // b) % 2) for b in hops + [1]}
        self.delta["z"] = n * (1 - 2 * self.parity)
        self.plane = Group(self, hops, self.c)
        self.wide = Group(self, ["z"] + hops, self.parity * n + self.c) if q == 2 else self.plane

    def slots(self, count):
        first = self.used
        self.used += count
        return first

    def extra(self):
        self.extras += 1
        return self.send.shape[0] - self.extras

    def slot(self, *key):
        if key not in self.named:
            self.named[key] = self.slots(1)
        return self.named[key]

    def copy(self, src, dst, slot, ctx=None, fsdp=None, out=None):
        return pltpu.make_async_remote_copy(
            src_ref=src,
            dst_ref=dst,
            send_sem=self.send.at[slot if out is None else out],
            recv_sem=self.recv.at[slot],
            device_id=(self.c if ctx is None else ctx, self.z if fsdp is None else fsdp),
            device_id_type=pl.DeviceIdType.MESH,
        )

    def go(self, *args, when=None, **kw):
        made = self.copy(*args, **kw)
        if when is None:
            made.start()
        else:
            pl.when(when)(made.start)
        self.sent.append((made, when))

    def arrived(self, ref, slot):
        self.copy(ref, ref, slot).wait_recv()

    def drain(self):
        for made, when in self.sent:
            if when is None:
                made.wait_send()
            else:
                pl.when(when)(made.wait_send)
        self.sent = []

    def greet(self):
        barrier = pltpu.get_barrier_semaphore()
        for d in range(1, self.n):
            pl.semaphore_signal(
                barrier, inc=1, device_id=(lax.rem(self.c + d, self.n), self.z), device_id_type=pl.DeviceIdType.MESH
            )
        for d in range(1, self.nz):
            pl.semaphore_signal(
                barrier, inc=1, device_id=(self.c, lax.rem(self.z + d, self.nz)), device_id_type=pl.DeviceIdType.MESH
            )
        pl.semaphore_wait(barrier, self.n + self.nz - 2)


class Group:
    def __init__(self, net, hops, own):
        self.net, self.hops, self.own = net, hops, own
        self.blocks = 2 ** (len(hops) + 1)

    def at(self, places):
        index = self.own
        for place in places:
            index = index + self.net.delta[place]
        return index

    def peer(self, hop):
        if hop == "z":
            return {"fsdp": self.net.z + 1 - 2 * self.net.parity}
        return {"ctx": self.net.c + self.net.delta[hop]}

    def chip(self, turn):
        net, count = self.net, len(self.hops)
        index = 0
        for j, hop in enumerate(self.hops):
            far = (turn // (2 ** (count - 1 - j))) % 2
            if hop == "z":
                index = index + net.n * ((net.parity + far) % 2)
            else:
                index = index + hop * (((net.c // hop) + far) % 2)
        return index

    def cuts(self, columns):
        count = max(1, len(self.hops))
        units = columns // LANES
        out, first = [], 0
        for k in range(count):
            size = (units * (k + 1) // count - units * k // count) * LANES
            out.append(pl.ds(first, size))
            first += size
        return out

    def turned(self, k):
        return self.hops[k:] + self.hops[:k]


class Gather:
    def __init__(self, net, group, buf, pool):
        self.net, self.group, self.buf = net, group, buf
        self.parts = group.cuts(buf.shape[2])
        self.out = net.slot(pool, "own")
        self.slot = {}
        for k in range(len(self.parts)):
            for s in subsets(group.turned(k)):
                if s:
                    self.slot[k, s, "hop"] = net.slot(pool, k, s, "hop")
                    self.slot[k, s, "core"] = net.slot(pool, k, s, "core")

    def go(self, ref, slot, hop):
        self.net.copy(ref, ref, slot, out=self.out, **self.group.peer(hop)).start()

    def drain(self):
        ref = self.buf.at[pl.ds(0, self.group.blocks - 1)]
        self.net.copy(ref, ref, self.out, out=self.out).wait_send()

    def ref(self, k, s):
        return self.buf.at[self.group.at(s), :, self.parts[k]]

    def forward(self, k, s, core):
        order = self.group.turned(k)
        later = order[order.index(s[-1]) + 1:] if s else order
        for hop in later:
            self.go(self.ref(k, s), self.slot[k, s + (hop,), "hop"], hop)
        if core:
            self.go(self.ref(k, s), self.slot[k, s, "core"], 1)

    def start(self):
        for k in range(len(self.parts)):
            if self.group.hops:
                self.forward(k, (), False)
        self.go(self.buf.at[self.group.own], self.out, 1)

    def level(self, m):
        for k in range(len(self.parts)):
            for s in subsets(self.group.turned(k)):
                if len(s) == m:
                    self.net.arrived(self.ref(k, s), self.slot[k, s, "hop"])
                    self.forward(k, s, True)

    def levels(self, first=1):
        for m in range(first, len(self.group.hops) + 1):
            self.level(m)

    def done(self):
        self.net.arrived(self.buf.at[self.group.at((1,))], self.out)
        for k in range(len(self.parts)):
            for s in subsets(self.group.turned(k)):
                if s:
                    self.net.arrived(self.ref(k, s + (1,)), self.slot[k, s, "core"])

    def finish(self):
        self.levels()
        self.done()


class Scatter:
    def __init__(self, net, group, part, came, pool):
        self.net, self.group, self.part, self.came = net, group, part, came
        self.parts = group.cuts(part.shape[2])
        self.sets = subsets(group.hops)[::-1]
        self.count = len(self.sets)
        if (pool, "base") not in net.named:
            net.named[pool, "base"] = net.slots(self.count)
        self.base = net.named[pool, "base"]
        self.slot = {}
        for k in range(len(self.parts)):
            for step in range(len(group.hops)):
                for s in subsets(group.turned(k)[step:]):
                    if group.turned(k)[step] in s:
                        self.slot[k, s] = net.slot(pool, k, s)

    def chip(self, k):
        return self.group.chip(self.count - 1 - k)

    def sets_of(self, k):
        hops = self.group.hops
        turn = self.count - 1 - k
        return tuple(hop for j, hop in enumerate(hops) if (turn // (2 ** (len(hops) - 1 - j))) % 2)

    def push(self, k):
        first = self.chip(k)
        mine = lax.rem(self.net.c, 2)
        self.net.copy(
            self.part.at[first + 1 - mine], self.came.at[first + mine], self.base + k, out=self.base, **self.group.peer(1)
        ).start()

    def fold(self):
        part, came, at = self.part, self.came, self.group.at
        for k in range(self.count):
            s = self.sets_of(k)
            self.net.arrived(came.at[at(s + (1,))], self.base + k)
            part[at(s)] = (part[at(s)].astype(f32) + came[at(s + (1,))].astype(f32)).astype(bf)
            for p in range(len(self.parts)):
                self.onward(p, 0, s)

    def onward(self, p, step, s):
        order = self.group.turned(p)
        if step < len(order) and order[step] in s:
            key = tuple(h for h in order if h in s)
            rest = tuple(h for h in s if h != order[step])
            cut = self.parts[p]
            self.net.copy(
                self.part.at[self.group.at(s), :, cut],
                self.came.at[self.group.at(rest), :, cut],
                self.slot[p, key], out=self.base, **self.group.peer(order[step]),
            ).start()

    def reduce(self, result):
        part, came, at = self.part, self.came, self.group.at
        count = len(self.group.hops)
        for step in range(count):
            for p in range(len(self.parts)):
                order = self.group.turned(p)
                cut = self.parts[p]
                for s in subsets(order[step + 1:])[::-1]:
                    far = s + (order[step],)
                    key = tuple(h for h in order if h in far)
                    self.net.arrived(came.at[at(far), :, cut], self.slot[p, key])
                    total = part[at(s), :, cut].astype(f32) + came[at(far), :, cut].astype(f32)
                    if step == count - 1:
                        result(cut, total)
                    else:
                        part[at(s), :, cut] = total.astype(bf)
                        self.onward(p, step + 1, s)
        if not count:
            result(slice(None), part[self.group.own].astype(f32))

    def drain(self):
        ref = self.part.at[pl.ds(0, self.group.blocks - 1)]
        self.net.copy(ref, ref, self.base, out=self.base).wait_send()


def count_slots(n, nz, q):
    hops = n.bit_length() - 2
    total = 13 * (nz - 1) + 6 + 6 * (n - 1) + n.bit_length() + nz.bit_length() - 2
    for h in (hops, hops + 1)[:q]:
        total += 2 * (1 + max(1, h) * 2 * (2**h - 1)) + 2 * (2**h + max(1, h) * (2**h - 1))
    return total


def layer(dims, *refs):
    (n, nz, q, t, te, w, fw, hpd) = dims
    (x_ref, e_ref, g_ref, segd_ref, segs_ref, wsl_ref, up_ref, down_ref, vec_ref,
     mixed_ref, gtok_ref, genc_ref, fu, fd, fas, fac, fos, foc, vt, hold1, hold2,
     n1x, ex, gbuf, nbuf, wbuf, wo, wup, wdown,
     qa1, ka1, v1, vt1, ot1, ob1, lse1, qa2, ka2, v2, vt2, ot2, ob2, lse2,
     x1, x2, pa, ra, pm, rm, dy2f,
     act, du, gu, gd, gas, gac, gos, goc, ru, rd, ras, rac, ros, roc,
     su, sd, vcame, dlt, dqacc, bias_ref, bup_ref,
     send, recv, local) = refs
    length, lenc = n * t, n * te
    rows_wide = q * length
    share = D // (n * nz)
    dz = D // nz
    nq, nk2 = length // TILE, lenc // TILE
    nbt, nbe = TILE // t, TILE // te
    net = Net(n, nz, q, send, recv)
    plane, wide_group = net.plane, net.wide
    c, z, parity = net.c, net.z, net.parity
    lane = lax.broadcasted_iota(jnp.int32, (1, LANES), 1)

    rows1 = pl.ds(0, length)
    dqkv, dq2, dkv2 = act.at[rows1, pl.ds(0, 384)], act.at[rows1, pl.ds(0, LANES)], act.at[pl.ds(0, lenc), pl.ds(LANES, 256)]
    dom = [du.at[:, pl.ds(h * LANES, LANES)] for h in range(hpd)]
    dx = gtok_ref

    def wor_of(j, cc):
        return pm.at[cc, pl.ds(0, w), pl.ds(j * LANES, LANES)]

    wide = -(-n * LANES // D)

    def row(k):
        return vec_ref[k:k + 1, :]

    def into(ref):
        def store(cut, total):
            ref[:, cut] = total
        return store

    zrows = pl.ds(pl.multiple_of(z * dz, dz), dz)

    def feed_cols(zz):
        return pl.ds(pl.multiple_of((lax.rem(zz, q) * n + c) * fw, LANES), fw)

    def local_copy(src, dst, k):
        made = pltpu.make_async_copy(src, dst, local.at[k])
        made.start()
        return made

    if w == LANES:
        own_cols = [
            local_copy(
                wsl_ref.at[:, pl.ds(pl.multiple_of(block * D + c * LANES, LANES), LANES)],
                wbuf.at[zrows, pl.ds(k * LANES, LANES)], k)
            for k, block in enumerate(ORDER)
        ]
    else:
        own_cols = [local_copy(wsl_ref, wbuf.at[zrows, :], 0)]
    own_feed = [
        local_copy(up_ref.at[:, feed_cols(z)], wup.at[zrows, :], 8),
        local_copy(down_ref.at[:, feed_cols(z)], wdown.at[zrows, :], 9),
    ]
    hat, _ = normed(x_ref[...].astype(f32))
    n1x[c, :, pl.ds(0, D)] = (hat * row(0) + row(1)).astype(bf)

    def hot(seg, rows):
        place = lax.broadcasted_iota(jnp.int32, (LANES, rows), 0) % HD
        return jnp.where(place == seg[...], 1.0, 0.0).T.astype(bf)

    n1x[c, :, pl.ds(D, LANES)] = hot(segd_ref, t)
    net.greet()

    groups = ((0, 384), (384, 128), (512, 512))
    wslots = [net.slots(nz - 1) - 1 for _ in groups]
    fslots = [net.slots(nz - 1) - 1 for _ in range(4)]

    ends = jnp.logical_or(z == 0, z == nz - 1)
    inner = jnp.logical_or(z == 1, z == nz - 2)
    far_end = jnp.where(z <= 1, nz - 1, 0)
    near_end = jnp.where(z <= 1, 0, nz - 1)
    relayed = nz >= 4

    def push_z(src_of, dst, slot, relay):
        for d in range(1, nz):
            peer = lax.rem(z + d, nz)
            straight = None
            if relay and d in (1, nz - 1):
                straight = z != (nz - 1 if d == 1 else 0)
            net.go(src_of(peer), dst, slot + d, fsdp=peer, when=straight)

    def relay_z(rows_of, slot):
        rows = rows_of(far_end)
        came = slot + lax.rem(z + nz - far_end, nz)

        @pl.when(inner)
        def _():
            net.arrived(rows, came)

        net.go(rows, rows, slot + jnp.where(z <= 1, 1, nz - 1), out=net.extra(), fsdp=near_end, when=inner)

    def await_z(rows_of, slot, relay):
        for d in range(1, nz):
            source = lax.rem(z + nz - d, nz)
            if not relay:
                net.arrived(rows_of(source), slot + d)
                continue

            @pl.when(jnp.logical_not(jnp.logical_and(inner, source == far_end)))
            def _():
                net.arrived(rows_of(source), slot + d)

    def weight_rows(zz, k):
        first, size = groups[k]
        return wbuf.at[pl.ds(pl.multiple_of(zz * dz, dz), dz), pl.ds(first, size)]

    def push_weights(k):
        push_z(lambda peer: weight_rows(z, k), weight_rows(z, k), wslots[k], relayed and k == 2)

    half = dz // 2

    def feed_rows(k):
        buf = (wup, wdown)[k // 2]
        return lambda zz: buf.at[pl.ds(pl.multiple_of(zz * dz + (k % 2) * half, half), half), :]

    def push_feed(k):
        ref = (up_ref, down_ref)[k // 2]
        push_z(lambda peer: ref.at[pl.ds((k % 2) * half, half), feed_cols(peer)], feed_rows(k)(z), fslots[k], relayed and k < 3)

    gat1 = Gather(net, plane, n1x, "main")
    gat1.start()
    for made in own_cols:
        made.wait()
    push_weights(0)
    ex[c, :, pl.ds(0, D)] = e_ref[...]
    ex[c, :, pl.ds(D, LANES)] = hot(segs_ref, te)
    for k in range(1, len(groups)):
        push_weights(k)
    vt[...] = jnp.zeros_like(vt)
    bias_ref[...] = jnp.zeros_like(bias_ref)
    for k, line in enumerate((6, 7, 9, 10)):
        own = vec_ref[line:line + 1, 0:w]
        for cc in range(1, n):
            own = jnp.where(c == cc, vec_ref[line:line + 1, cc * w:(cc + 1) * w], own)
        bias_ref[k:k + 1, 0:w] = own
    own = vec_ref[13:14, 0:fw]
    for cc in range(1, n * q):
        line, first = 13 + cc * fw // D, cc * fw % D
        own = jnp.where(wide_group.own == cc, vec_ref[line:line + 1, first:first + fw], own)
    bup_ref[0:1, :] = own
    vt[8:9, :] = jnp.sum(g_ref[...].astype(f32), axis=0, keepdims=True)
    if relayed:
        @pl.when(ends)
        def _():
            for came in (ru, rd, rac, roc):
                came[far_end] = jnp.zeros(came.shape[1:], bf)

    gat1.levels()
    gate = Gather(net, plane, ex, "side")
    gate.start()
    gat1.done()
    await_z(lambda zz: weight_rows(zz, 0), wslots[0], False)

    def tile_of(buf, i, per, columns):
        return buf[pl.ds(i * per, per), :, columns].reshape(TILE, columns.size)

    head_of = lane // HD

    def put_q(qa, q, oh, rows):
        q = (q.astype(bf).astype(f32) * SCALE).astype(bf)
        for h in range(hpd):
            qa[h, rows, :] = jnp.where(head_of == h, q, oh)

    def put_k(ka, k, oh, rows):
        k = k.astype(bf)
        pen = ((oh.astype(f32) - 1.0) * -NEG).astype(bf)
        for h in range(hpd):
            ka[h, rows, :] = jnp.where(head_of == h, k, pen)

    def put_v(v, vt_ref, value, rows, i):
        value = value.astype(bf)
        v[rows, :] = value
        vt_ref[i] = value.astype(f32).T.astype(bf)

    def tile_rows(i):
        return pl.ds(pl.multiple_of(i * TILE, TILE), TILE)

    def qkv_tile(i, _):
        rows = tile_rows(i)
        got = dot(tile_of(n1x, i, nbt, pl.ds(0, D)), wbuf[:, 0:384])
        oh = tile_of(n1x, i, nbt, pl.ds(D, LANES))
        put_q(qa1, got[:, 0:128] + bias_ref[0:1, :], oh, rows)
        put_k(ka1, got[:, 128:256], oh, rows)
        put_v(v1, vt1, got[:, 256:384] + bias_ref[1:2, :], rows, i)
        return _

    lax.fori_loop(0, nq, qkv_tile, 0)

    n1f, n3f = n1x.at[:, :, pl.ds(0, D)], nbuf
    n2f = dy1f = nbuf.at[pl.ds(parity * n, n)] if q == 2 else nbuf
    gf = gbuf if q == 2 else n1f
    n2back = gf.at[pl.ds(0, n)]

    if q == 1:
        away1 = local_copy(n1f, hold1, 10)

    push_feed(0)
    push_feed(1)

    def attend(qa, ka, vt_ref, ot, ob, lse, keys, causal):
        def one(j, _):
            qrows = tile_rows(j)

            def step(i, state, diagonal):
                out = []
                for h in range(hpd):
                    top, total, acc = state[h]
                    s = dot_t(ka[h, tile_rows(i), :], qa[h, qrows, :])
                    if diagonal:
                        kp = lax.broadcasted_iota(jnp.int32, (TILE, TILE), 0)
                        qp = lax.broadcasted_iota(jnp.int32, (TILE, TILE), 1)
                        s = jnp.where(kp <= qp, s, NEG)
                    new = jnp.maximum(top, jnp.max(s, axis=0, keepdims=True))
                    p = jnp.exp(s - new)
                    fix = jnp.exp(top - new)
                    total = total * fix + jnp.sum(p, axis=0, keepdims=True)
                    acc = acc * fix + dot(vt_ref[i, pl.ds(h * HD, HD), :], p.astype(bf))
                    out.append((new, total, acc))
                return tuple(out)

            state = tuple(
                (jnp.full((1, TILE), -3e38, f32), jnp.zeros((1, TILE), f32), jnp.zeros((HD, TILE), f32))
                for _ in range(hpd)
            )
            if causal:
                state = step(j, state, True)
                state = lax.fori_loop(0, j, lambda i, st: step(i, st, False), state)
            else:
                state = lax.fori_loop(0, keys, lambda i, st: step(i, st, False), state)
            for h in range(hpd):
                top, total, acc = state[h]
                ot[j, pl.ds(h * HD, HD), :] = acc * (1.0 / total)
                lse[j, h:h + 1, :] = top + jnp.log(total)
            ob[qrows, :] = ot[j].T.astype(bf)
            return _

        if hpd * HD < LANES:
            ot[...] = jnp.zeros_like(ot)
        lax.fori_loop(0, nq, one, 0)

    await_z(lambda zz: weight_rows(zz, 1), wslots[1], False)
    oslots = [net.slots(n - 1) - 1, net.slots(n - 1) - 1]

    def out_rows(j, cc):
        return wbuf.at[pl.ds(pl.multiple_of(cc * w, w), w), pl.ds(OUT_AT[j], LANES)]

    def push_out(j):
        for d in range(1, n):
            peer = lax.rem(c + d, n)
            net.go(out_rows(j, peer), wor_of(j, c), oslots[j] + d, ctx=peer)
        wor_of(j, c)[...] = wbuf[pl.ds(pl.multiple_of(c * w, w), w), pl.ds(OUT_AT[j], LANES)]

    push_out(0)

    def await_out(j):
        for d in range(1, n):
            net.arrived(wor_of(j, lax.rem(c + n - d, n)), oslots[j] + d)
        if w < LANES:
            wo[j] = jnp.zeros((LANES, D), bf)
        wo[j, pl.ds(0, w), :] = jnp.concatenate(
            [pm[cc, pl.ds(0, w), pl.ds(j * LANES, LANES)][:, :w] for cc in range(n)], axis=-1)

    gate.levels()
    attend(qa1, ka1, vt1, ot1, ob1, lse1, nq, True)

    gate.done()
    await_out(0)

    def partial(scat, rows_of, weight_of, per):
        def one(k, _):
            first = scat.chip(k)
            scat.part[pl.ds(first, 2)] = weight_of(rows_of(first)).astype(bf).reshape(2, per, D)
            scat.push(k)
            return _

        lax.fori_loop(0, scat.count, one, 0)

    def flat(buf, per):
        return lambda first: buf[pl.ds(pl.multiple_of(first * per, 2 * per), 2 * per), :]

    rs1 = Scatter(net, plane, pa.at[pl.ds(0, n)], ra.at[pl.ds(0, n)], "sum")
    partial(rs1, flat(ob1, t), lambda rows: dot(rows, wo[0]), t)

    def kv2_tile(i, _):
        rows = tile_rows(i)
        got = dot(tile_of(ex, i, nbe, pl.ds(0, D)), wbuf[:, 512:768])
        oh = tile_of(ex, i, nbe, pl.ds(D, LANES))
        put_k(ka2, got[:, 0:128], oh, rows)
        put_v(v2, vt2, got[:, 128:256] + bias_ref[3:4, :], rows, i)
        return _

    rs1.fold()
    if relayed:
        relay_z(lambda zz: weight_rows(zz, 2), wslots[2])
    rs1.reduce(into(x1))
    x1[...] = x_ref[...].astype(f32) + (x1[...] + row(8))
    hat, _ = normed(x1[...])
    n2f[c] = (hat * row(2) + row(3)).astype(bf)
    gat1.drain()
    if q == 1:
        away1.wait()
    gat2 = Gather(net, plane, n2f, "main")
    gat2.start()
    rs1.drain()
    gate.drain()
    push_feed(2)
    push_feed(3)
    gat2.levels()
    await_z(lambda zz: weight_rows(zz, 2), wslots[2], relayed)
    push_out(1)
    gat2.done()
    gf[wide_group.own] = g_ref[...]
    gatg = Gather(net, wide_group, gf, "side" if q == 1 else "wideside")
    gatg.start()

    def q2_tile(i, _):
        got = dot(tile_of(n2f, i, nbt, pl.ds(0, D)), wbuf[:, 896:1024])
        put_q(qa2, got + bias_ref[2:3, :], tile_of(n1x, i, nbt, pl.ds(D, LANES)), tile_rows(i))
        return _

    lax.fori_loop(0, nq, q2_tile, 0)
    lax.fori_loop(0, nk2, kv2_tile, 0)
    if relayed:
        relay_z(feed_rows(0), fslots[0])
    away2 = local_copy(n2f, hold2, 11)
    gatg.level(1)
    attend(qa2, ka2, vt2, ot2, ob2, lse2, nk2, False)
    away2.wait()
    gat2.drain()
    await_out(1)
    rs2 = Scatter(net, plane, pa.at[pl.ds(0, n)], ra.at[pl.ds(0, n)], "sum")
    partial(rs2, flat(ob2, t), lambda rows: dot(rows, wo[1]), t)
    gatg.levels(2)
    rs2.fold()
    if relayed:
        relay_z(feed_rows(1), fslots[1])
    rs2.reduce(into(x2))
    x2[...] = x1[...] + (x2[...] + row(11))
    hat, _ = normed(x2[...])
    n3f[wide_group.own] = (hat * row(4) + row(5)).astype(bf)
    gat3 = Gather(net, wide_group, n3f, "main" if q == 1 else "wide")
    gat3.start()
    rs2.drain()
    gatg.done()
    for made in own_feed:
        made.wait()
    gat3.finish()
    if relayed:
        relay_z(feed_rows(2), fslots[2])
    for k in range(4):
        await_z(feed_rows(k), fslots[k], relayed and k < 3)

    rs3 = Scatter(net, wide_group, pa, ra, "sum" if q == 1 else "widesum")
    rsm = Scatter(net, wide_group, pm, rm, "sum2" if q == 1 else "widesum2")
    fc = min(fw, 512)

    def feed_tile(k, sums):
        first = rs3.chip(k)
        rows = pl.ds(pl.multiple_of(first * t, 2 * t), 2 * t)
        left = n3f[pl.ds(first, 2)].reshape(2 * t, D)
        grad = gf[pl.ds(first, 2)].reshape(2 * t, D)
        out = []
        for f in range(fw // fc):
            cols = pl.ds(f * fc, fc)
            u = dot(left, wup[:, cols]) + bup_ref[0:1, cols]
            cdf, slope = gelu_parts(u)
            act[rows, cols] = (u * cdf).astype(bf)
            low = (dot(grad, wdown[:, cols]) * slope).astype(bf)
            du[rows, cols] = low
            out.append(sums[f] + jnp.sum(low.astype(f32), axis=0, keepdims=True))
        pa[pl.ds(first, 2)] = dot_t(du[rows, :], wup[...]).astype(bf).reshape(2, t, D)
        rs3.push(k)
        return tuple(out)

    sums = lax.fori_loop(0, rs3.count, feed_tile, tuple(jnp.zeros((1, fc), f32) for _ in range(fw // fc)))
    for f in range(fw // fc):
        for cc in range(n * q):
            place = cc * fw + f * fc
            line = 9 + 4 * wide + place // D
            vt[line:line + 1, pl.ds(place % D, fc)] = jnp.where(wide_group.own == cc, sums[f], 0.0)
    rs3.fold()
    partial(rsm, flat(act, t), lambda rows: dot_t(rows, wdown[...]), t)
    rsm.fold()

    per = TILE // (share * nz)

    def weight_grad(left_of, right, out, columns):
        def one(r, _):
            got = t_dot(left_of(tile_rows(r)), right())
            for k in range(TILE // share):
                out[k % nz, r * per + k // nz, :, columns] = got[k * share:(k + 1) * share].astype(bf)
            return _

        lax.fori_loop(0, D // TILE, one, 0)

    def whole(buf, rows):
        return lambda cols: buf[:, :, cols].reshape(rows, TILE)

    zslots = [net.slots(nz) - 1 for _ in range(6)]
    last = (4, 5)

    def push_grad(mine, came, k):
        for d in range(1, nz):
            peer = lax.rem(z + d, nz)
            when = None
            if relayed and k not in last:
                when = jnp.logical_not(jnp.logical_and(
                    jnp.logical_or(ends, inner), peer == far_end))
            net.go(mine.at[peer], came.at[z], zslots[k] + d, fsdp=peer, when=when)
        if relayed and k not in last:
            step = jnp.where(z == 0, 1, nz - 2)
            net.go(mine.at[far_end], came.at[step], zslots[k] + nz, out=net.extra(), fsdp=step, when=ends)

    def relay_grad(mine, came, k):
        if not relayed:
            return

        @pl.when(inner)
        def _():
            net.arrived(came.at[z], zslots[k] + nz)
            mine[far_end] = (mine[far_end].astype(f32) + came[z].astype(f32)).astype(bf)

        net.go(mine.at[far_end], came.at[z], zslots[k] + lax.rem(far_end - z + nz, nz), out=net.extra(), fsdp=far_end,
               when=inner)

    def grad_arrived(came, k, d):
        peer = lax.rem(z + nz - d, nz)
        if relayed and k not in last and d in (1, nz - 1):
            @pl.when(z != (0 if d == 1 else nz - 1))
            def _():
                net.arrived(came.at[peer], zslots[k] + d)
        else:
            net.arrived(came.at[peer], zslots[k] + d)
        return came[peer].astype(f32)

    def sum_grad(mine, came, k):
        total = mine[z].astype(f32)
        for d in range(1, nz):
            total = total + grad_arrived(came, k, d)
        return total.astype(bf)

    weight_grad(whole(n3f, rows_wide), lambda: du[...], gu, pl.ds(0, fw))
    push_grad(gu, ru, 0)
    gat3.drain()
    gatg.drain()
    rs3.reduce(into(dx))
    back, gain_g, shift_g = norm_back(x2[...], row(4), dx[...])
    vt[4:5, :] = gain_g
    vt[5:6, :] = shift_g
    dx[...] = g_ref[...].astype(f32) + back
    dy = dx[...].astype(bf)
    dy2f[c] = dy
    gat4 = Gather(net, plane, dy2f, "main")
    gat4.start()
    vt[7:8, :] = jnp.sum(dy.astype(f32), axis=0, keepdims=True)
    rs3.drain()
    gat4.levels()
    weight_grad(whole(gf, rows_wide), lambda: act[...], gd, pl.ds(0, fw))
    push_grad(gd, rd, 1)
    back2 = local_copy(hold2, n2back, 12)
    gat4.done()
    relay_grad(gu, ru, 0)

    def attend_back(qa, ka, v, ot, lse, dyf, out_w, keys, causal, dq_ref, dq_cols, dkv_ref, dk_cols, dv_cols):
        def grads(i, _):
            rows = tile_rows(i)
            low = dot_t(tile_of(dyf, i, nbt, pl.ds(0, D)), out_w[...]).astype(bf)
            for h in range(hpd):
                dom[h][rows, :] = jnp.where(head_of == h, low, jnp.zeros_like(low))
            prod = low.astype(f32).T * ot[i]
            for h in range(hpd):
                dlt[i, h:h + 1, :] = jnp.sum(prod[h * HD:(h + 1) * HD], axis=0, keepdims=True)
            dqacc[rows, :] = jnp.zeros((TILE, LANES), f32)
            return _

        lax.fori_loop(0, nq, grads, 0)

        def one(i, _):
            krows = tile_rows(i)

            def step(j, state, diagonal):
                qrows = tile_rows(j)
                dv, dks = state
                new_dks, dqs = [], []
                for h in range(hpd):
                    s = dot_t(ka[h, krows, :], qa[h, qrows, :])
                    p = jnp.exp(s - lse[j, h:h + 1, :])
                    if diagonal:
                        kp = lax.broadcasted_iota(jnp.int32, (TILE, TILE), 0)
                        qp = lax.broadcasted_iota(jnp.int32, (TILE, TILE), 1)
                        p = jnp.where(kp <= qp, p, 0.0)
                    dp = dot_t(v[krows, :], dom[h][qrows, :])
                    ds = (p * (dp - dlt[j, h:h + 1, :])).astype(bf)
                    dv = dv + dot(p.astype(bf), dom[h][qrows, :])
                    new_dks.append(dks[h] + dot(ds, qa[h, qrows, :]))
                    dqs.append(t_dot(ds, ka[h, krows, :]))
                dq = jnp.where(head_of == 0, dqs[0], dqs[-1] if hpd > 1 else 0.0)
                dqacc[qrows, :] = dqacc[qrows, :] + dq
                return dv, tuple(new_dks)

            zero = jnp.zeros((TILE, LANES), f32)
            state = (zero, tuple(zero for _ in range(hpd)))
            if causal:
                state = step(i, state, True)
                state = lax.fori_loop(i + 1, nq, lambda j, st: step(j, st, False), state)
            else:
                state = lax.fori_loop(0, nq, lambda j, st: step(j, st, False), state)
            dv, dks = state
            dk = jnp.where(head_of == 0, dks[0], dks[-1] if hpd > 1 else 0.0)
            dkv_ref[krows, dk_cols] = dk.astype(bf)
            dkv_ref[krows, dv_cols] = dv.astype(bf)
            return _

        lax.fori_loop(0, keys, one, 0)

        def close(i, _):
            rows = tile_rows(i)
            dq_ref[rows, dq_cols] = (dqacc[rows, :] * SCALE).astype(bf)
            return _

        lax.fori_loop(0, nq, close, 0)

    def head_sum(k, ref, cols):
        own = jnp.sum(ref[:, cols].astype(f32), axis=0, keepdims=True)
        for cc in range(n):
            line = 9 + k * wide + cc * LANES // D
            vt[line:line + 1, pl.ds(cc * LANES % D, LANES)] = jnp.where(c == cc, own, 0.0)

    first3 = [pl.ds(k * LANES, LANES) for k in range(3)]
    attend_back(qa2, ka2, v2, ot2, lse2, dy2f, wo.at[1], nk2, False, dq2, first3[0], dkv2, first3[0], first3[1])
    rs4 = Scatter(net, plane, pa.at[pl.ds(0, n)], ra.at[pl.ds(0, n)], "sum")
    partial(rs4, flat(dq2, t), lambda rows: dot_t(rows, wbuf[:, 896:1024]), t)
    def store_mixed(cut, total):
        mixed_ref[:, cut] = (x2[:, cut] + (total + vec_ref[12:13, cut])).astype(bf)

    rsm.reduce(store_mixed)
    rs4.fold()

    weight_grad(whole(ex, lenc), lambda: dkv2[...], gac, pl.ds(0, 256))
    back2.wait()
    weight_grad(whole(n2back, length), lambda: dq2[...], gac, pl.ds(256, 128))
    if q == 1:
        back1 = local_copy(hold1, n1f, 13)
    push_grad(gac, rac, 2)
    relay_grad(gd, rd, 1)

    def out_grad(ob, dyf, out):
        for cut in (0, 1):
            cols = pl.ds(cut * (D // 2), D // 2)
            got = t_dot(ob[...], dyf[:, :, cols].reshape(length, D // 2))
            for k in range(nz):
                out[k, :, cols] = got[k * share:(k + 1) * share].astype(bf)

    rs4.reduce(into(x2))
    back, gain_g, shift_g = norm_back(x1[...], row(2), x2[...])
    vt[2:3, :] = gain_g
    vt[3:4, :] = shift_g
    dx[...] = dx[...] + back
    dy = dx[...].astype(bf)
    dy1f[c] = dy
    gat4.drain()
    gat5 = Gather(net, plane, dy1f, "main")
    gat5.start()
    vt[6:7, :] = jnp.sum(dy.astype(f32), axis=0, keepdims=True)
    head_sum(2, dq2, first3[0])
    head_sum(3, dkv2, first3[1])
    rs4.drain()
    rsm.drain()
    rse = Scatter(net, plane, pm.at[pl.ds(0, n), pl.ds(0, te), :], rm.at[pl.ds(0, n), pl.ds(0, te), :], "sum2")
    partial(rse, flat(dkv2, te), lambda rows: dot_t(rows, wbuf[:, 512:768]), te)
    gat5.levels()
    rse.fold()
    out_grad(ob2, dy2f, goc)
    push_grad(goc, roc, 3)
    gat5.done()
    relay_grad(gac, rac, 2)
    out_grad(ob1, dy1f, gos)
    push_grad(gos, ros, 5)
    attend_back(qa1, ka1, v1, ot1, lse1, dy1f, wo.at[0], nq, True, dqkv, first3[0], dqkv, first3[1], first3[2])
    rs5 = Scatter(net, plane, pa.at[pl.ds(0, n)], ra.at[pl.ds(0, n)], "sum")
    partial(rs5, flat(dqkv, t), lambda rows: dot_t(rows, wbuf[:, 0:384]), t)
    rs5.fold()
    rse.reduce(into(genc_ref))
    if q == 1:
        back1.wait()
    weight_grad(whole(n1f, length), lambda: dqkv[...], gas, pl.ds(0, 384))
    push_grad(gas, ras, 4)
    relay_grad(goc, roc, 3)
    rs5.reduce(into(x2))
    back, gain_g, shift_g = norm_back(x_ref[...].astype(f32), row(0), x2[...])
    vt[0:1, :] = gain_g
    vt[1:2, :] = shift_g
    gtok_ref[...] = dx[...] + back
    head_sum(0, dqkv, first3[0])
    head_sum(1, dqkv, first3[2])

    vslots = net.slots(vcame.shape[0])
    pairs = [("ctx", b) for b in plane.hops + [1]] + [("fsdp", 1 << k) for k in range(nz.bit_length() - 1)]

    def swap(k):
        axis, b = pairs[k]
        own = c if axis == "ctx" else z
        peer = own + b - 2 * b * ((own // b) % 2)
        made = net.copy(vt, vcame.at[k], vslots + k, **{axis: peer})
        made.start()
        return made

    def merge(k, made):
        made.wait_send()
        net.arrived(vcame.at[k], vslots + k)
        vt[...] = vt[...] + vcame[k]

    def sum_feed(mine, came, k, total):
        for r in range(q):
            got = 0.0
            for d in range(r, nz, q):
                if d == 0:
                    got = got + mine[z].astype(f32)
                else:
                    got = got + grad_arrived(came, k, d)
            total[:, lax.rem(parity + q - r, q)] = got.astype(bf)

    def sum_heads(mine, came, k):
        mine[z] = sum_grad(mine, came, k)
        return mine.at[z]

    def exchange(total, out):
        slot = net.slots(n - 1) - 1
        out[c] = total[c]
        for d in range(1, n):
            peer = lax.rem(c + d, n)
            net.go(total.at[peer], out.at[c], slot + d, ctx=peer)

        def done():
            for d in range(1, n):
                net.arrived(out.at[lax.rem(c + n - d, n)], slot + d)
        return done

    waits = []
    todo = [
        lambda: (sum_feed(gu, ru, 0, su), waits.append(exchange(su, fu))),
        lambda: (sum_feed(gd, rd, 1, sd), waits.append(exchange(sd, fd))),
        lambda: waits.append(exchange(sum_heads(gac, rac, 2), fac)),
    ]
    for k in range(len(pairs)):
        made = swap(k)
        if todo:
            todo.pop(0)()
        merge(k, made)
    for step in todo:
        step()
    foc[...] = sum_grad(goc, roc, 3)
    waits.append(exchange(sum_heads(gas, ras, 4), fas))
    fos[...] = sum_grad(gos, ros, 5)
    for wait in waits:
        wait()
    rs5.drain()
    rse.drain()
    gat5.drain()
    net.drain()
    assert net.used == count_slots(n, nz, q) and net.extras <= EXTRAS


def body(tokens, encoder, dec_seg, src_seg, attn_w, up_w, down_w, vec, cot):
    n, nz = lax.axis_size("ctx"), lax.axis_size("fsdp")
    c = lax.axis_index("ctx")
    t, te = tokens.shape[1], encoder.shape[1]
    ff = up_w.shape[1]
    q = 1
    w, fw = D // n, ff // (n * q)
    hpd = w // HD
    dz = D // nz
    share = D // (n * nz)
    length, lenc = n * t, n * te

    if w < LANES:
        wsl = lax.dynamic_slice_in_dim(attn_w.reshape(dz, 8, D), c * w, w, axis=2)
        wsl = jnp.stack([wsl[:, k] for k in ORDER], axis=1)
        attn_w = jnp.pad(wsl, ((0, 0), (0, 0), (0, LANES - w))).reshape(dz, 8 * LANES)

    nq, nk2 = length // TILE, lenc // TILE
    slots = count_slots(n, nz, q)
    dims = (n, nz, q, t, te, w, fw, hpd)
    wide = -(-n * LANES // D)
    vrows = -(-(9 + 4 * wide + ff // D) // 8) * 8
    steps = n.bit_length() + nz.bit_length() - 2
    out_shape = (
        jax.ShapeDtypeStruct((t, D), bf),
        jax.ShapeDtypeStruct((t, D), f32),
        jax.ShapeDtypeStruct((te, D), f32),
        jax.ShapeDtypeStruct((n, q, share, fw), bf),
        jax.ShapeDtypeStruct((n, q, share, fw), bf),
        jax.ShapeDtypeStruct((n, share, 384), bf),
        jax.ShapeDtypeStruct((n, share, 384), bf),
        jax.ShapeDtypeStruct((share, D), bf),
        jax.ShapeDtypeStruct((share, D), bf),
        jax.ShapeDtypeStruct((vrows, D), f32),
        jax.ShapeDtypeStruct((n, t, D), bf),
        jax.ShapeDtypeStruct((n, t, D), bf),
    )

    def attn_scratch(keys):
        return [
            pltpu.VMEM((hpd, length, LANES), bf), pltpu.VMEM((hpd, keys, LANES), bf), pltpu.VMEM((keys, LANES), bf),
            pltpu.VMEM((keys // TILE, LANES, TILE), bf), pltpu.VMEM((nq, LANES, TILE), f32),
            pltpu.VMEM((length, LANES), bf), pltpu.VMEM((nq, 8, TILE), f32),
        ]

    scratch = [
        pltpu.VMEM((n, t, D + LANES), bf), pltpu.VMEM((n, te, D + LANES), bf),
        pltpu.VMEM((q * n, t, D) if q == 2 else (1, 16, LANES), bf), pltpu.VMEM((q * n, t, D), bf),
        pltpu.VMEM((D, 8 * LANES), bf), pltpu.VMEM((2, LANES, D), bf),
        pltpu.VMEM((D, fw), bf), pltpu.VMEM((D, fw), bf),
        *attn_scratch(length), *attn_scratch(lenc),
        pltpu.VMEM((t, D), f32), pltpu.VMEM((t, D), f32),
        *[pltpu.VMEM((q * n, t, D), bf) for _ in range(4)], pltpu.VMEM((n, t, D), bf),
        pltpu.VMEM((q * length, fw), bf), pltpu.VMEM((q * length, fw), bf),
    ]
    for _ in range(2):
        scratch += [
            pltpu.VMEM((nz, n, share, fw), bf), pltpu.VMEM((nz, n, share, fw), bf),
            pltpu.VMEM((nz, n, share, 384), bf), pltpu.VMEM((nz, n, share, 384), bf),
            pltpu.VMEM((nz, share, D), bf), pltpu.VMEM((nz, share, D), bf),
        ]
    scratch += [
        pltpu.VMEM((n, q, share, fw), bf), pltpu.VMEM((n, q, share, fw), bf), pltpu.VMEM((steps, vrows, D), f32),
        pltpu.VMEM((nq, 8, TILE), f32), pltpu.VMEM((length, LANES), f32),
        pltpu.VMEM((8, LANES), f32), pltpu.VMEM((8, fw), f32),
        pltpu.SemaphoreType.DMA((slots + EXTRAS,)), pltpu.SemaphoreType.DMA((slots,)), pltpu.SemaphoreType.DMA((16,)),
    ]
    vmem = pl.BlockSpec(memory_space=pltpu.VMEM)
    hbm = pl.BlockSpec(memory_space=pl.ANY)
    mixed, gtok, genc, fu, fd, fas, fac, fos, foc, vsum, _, _ = pl.pallas_call(
        functools.partial(layer, dims),
        out_shape=out_shape,
        in_specs=[vmem] * 5 + [hbm] * 3 + [vmem],
        out_specs=[vmem] * (len(out_shape) - 2) + [hbm] * 2,
        scratch_shapes=scratch,
        compiler_params=pltpu.CompilerParams(
            collective_id=0, has_side_effects=True, vmem_limit_bytes=63 * 1024 * 1024
        ),
        cost_estimate=pl.CostEstimate(flops=21_000_000_000, bytes_accessed=30_000_000, transcendentals=8_000_000),
        name="layer",
    )(tokens[0], encoder[0], cot[0], dec_seg, src_seg, attn_w, up_w, down_w, vec)

    return pl.pallas_call(
        functools.partial(closing, (n, q, w, fw, wide)),
        out_shape=(
            jax.ShapeDtypeStruct((1, t, D), bf), jax.ShapeDtypeStruct((1, t, D), f32),
            jax.ShapeDtypeStruct((1, te, D), f32), jax.ShapeDtypeStruct((share, 8 * D), f32),
            jax.ShapeDtypeStruct((share, ff), f32), jax.ShapeDtypeStruct((share, ff), f32),
            jax.ShapeDtypeStruct(vec.shape, f32),
        ),
        in_specs=[hbm] * 10,
        out_specs=[hbm] * 7,
        scratch_shapes=[pltpu.VMEM(a.shape, a.dtype) for a in (mixed, gtok, genc, fu, fd, fas, fac, fos, foc, vsum)] + [
            pltpu.VMEM((share, 8 * D), f32), pltpu.VMEM((share, ff), f32), pltpu.VMEM((share, ff), f32),
            pltpu.VMEM(vec.shape, f32), pltpu.SemaphoreType.DMA((17,)),
        ],
        compiler_params=pltpu.CompilerParams(vmem_limit_bytes=62 * 1024 * 1024),
        name="closing",
    )(mixed, gtok, genc, fu, fd, fas, fac, fos, foc, vsum)


def closing(dims, *refs):
    n, q, w, fw, wide = dims
    given, outs, kept, made, sems = refs[:10], refs[10:17], refs[17:27], refs[27:31], refs[31]
    coming = [pltpu.make_async_copy(given[k], kept[k], sems.at[k]) for k in range(10)]
    straight = [pltpu.make_async_copy(kept[k], outs[k].at[0], sems.at[10 + k]) for k in range(3)]
    going = [pltpu.make_async_copy(made[k], outs[3 + k], sems.at[13 + k]) for k in range(4)]
    for copy in coming:
        copy.start()
    for k in range(3):
        coming[k].wait()
        straight[k].start()
    kept, coming = kept[3:], coming[3:]
    fu, fd, fas, fac, fos, foc, vsum = kept
    o_attn, o_up, o_down, o_vec = made
    coming[0].wait()
    for cc in range(n * q):
        o_up[:, pl.ds(cc * fw, fw)] = fu[cc % n, cc // n].astype(f32)
    going[1].start()
    coming[1].wait()
    for cc in range(n * q):
        o_down[:, pl.ds(cc * fw, fw)] = fd[cc % n, cc // n].astype(f32)
    going[2].start()
    for k in range(2, 7):
        coming[k].wait()
    for block, (ref, k) in enumerate(
        ((fas, 0), (fas, 1), (fas, 2), (fos, None), (fac, 2), (fac, 0), (fac, 1), (foc, None))
    ):
        if k is None:
            got = ref[...]
        else:
            got = jnp.concatenate([ref[cc, :, pl.ds(k * LANES, LANES)][:, :w] for cc in range(n)], axis=-1)
        o_attn[:, pl.ds(block * D, D)] = got.astype(f32)
    going[0].start()

    def heads(k):
        parts = []
        for cc in range(n):
            line, first = 9 + k * wide + cc * LANES // D, cc * LANES % D
            parts.append(vsum[line:line + 1, first:first + LANES][:, :w])
        return jnp.concatenate(parts, axis=-1)

    o_vec[0:6] = vsum[0:6]
    o_vec[6:7] = heads(0)
    o_vec[7:8] = heads(1)
    o_vec[8:9] = vsum[6:7]
    o_vec[9:10] = heads(2)
    o_vec[10:11] = heads(3)
    o_vec[11:13] = vsum[7:9]
    up = 9 + 4 * wide
    o_vec[13:] = vsum[up:up + o_vec.shape[0] - 13]
    going[3].start()
    for copy in straight + going:
        copy.wait()


def solution(mesh):
    return jax.shard_map(
        body, mesh=mesh,
        in_specs=(P("fsdp", "ctx", None), P("fsdp", "ctx", None), P("fsdp", "ctx"), P("fsdp", "ctx"), P("fsdp", None),
                  P("fsdp", None), P("fsdp", None), P(), P("fsdp", "ctx", None)),
        out_specs=(P("fsdp", "ctx", None), P("fsdp", "ctx", None), P("fsdp", "ctx", None), P(("ctx", "fsdp"), None),
                   P(("ctx", "fsdp"), None), P(("ctx", "fsdp"), None), P()),
        check_vma=False,
    )
```

```python
import functools

import jax
import jax.numpy as jnp
from jax import lax
from jax.experimental import pallas as pl
from jax.experimental.pallas import tpu as pltpu
from jax.sharding import PartitionSpec as P

D = 1024
HD = 64
LANES = 128
TILE = 256
EXTRAS = 16
EPS = 1e-05
NEG = -1e30
SCALE = HD ** (-0.5)
bf = jnp.bfloat16
f32 = jnp.float32
ORDER = (0, 1, 2, 3, 5, 6, 7, 4)
OUT_AT = (384, 768)


def dot(a, b):
    return jnp.dot(a, b, preferred_element_type=f32)


def dot_t(a, b):
    return lax.dot_general(a, b, (((1,), (1,)), ((), ())), preferred_element_type=f32)


def t_dot(a, b):
    return lax.dot_general(a, b, (((0,), (0,)), ((), ())), preferred_element_type=f32)


def normed(value):
    centred = value - jnp.mean(value, axis=-1, keepdims=True)
    inv = lax.rsqrt(jnp.mean(centred * centred, axis=-1, keepdims=True) + EPS)
    return centred * inv, inv


def norm_back(value, gain, grad):
    hat, inv = normed(value)
    scaled = grad * gain
    back = inv * (
        scaled
        - jnp.mean(scaled, axis=-1, keepdims=True)
        - hat * jnp.mean(scaled * hat, axis=-1, keepdims=True)
    )
    return back, jnp.sum(grad * hat, axis=0, keepdims=True), jnp.sum(grad, axis=0, keepdims=True)


def gelu_parts(u):
    e = jnp.exp(-0.5 * u * u)
    t = 1.0 / (1.0 + (0.3275911 * 2.0**-0.5) * jnp.abs(u))
    poly = 0.5 * 1.061405429
    for term in (-1.453152027, 1.421413741, -0.284496736, 0.254829592):
        poly = poly * t + 0.5 * term
    tail = poly * t * e
    cdf = jnp.where(u >= 0.0, 1.0 - tail, tail)
    return cdf, cdf + u * (e * 0.3989422804014327)


def subsets(items):
    out = [()]
    for item in items:
        out = out + [s + (item,) for s in out]
    return sorted(out, key=len)


class Net:
    def __init__(self, n, nz, q, send, recv):
        self.n, self.nz = n, nz
        self.c = lax.axis_index("ctx")
        self.z = lax.axis_index("fsdp")
        self.send, self.recv = send, recv
        self.used = self.extras = 0
        self.named = {}
        self.sent = []
        hops = [n >> k for k in range(1, n.bit_length() - 1)]
        self.parity = lax.rem(self.z, q)
        self.delta = {b: b - 2 * b * ((self.c // b) % 2) for b in hops + [1]}
        self.delta["z"] = n * (1 - 2 * self.parity)
        self.plane = Group(self, hops, self.c)
        self.wide = Group(self, ["z"] + hops, self.parity * n + self.c) if q == 2 else self.plane

    def slots(self, count):
        first = self.used
        self.used += count
        return first

    def extra(self):
        self.extras += 1
        return self.send.shape[0] - self.extras

    def slot(self, *key):
        if key not in self.named:
            self.named[key] = self.slots(1)
        return self.named[key]

    def copy(self, src, dst, slot, ctx=None, fsdp=None, out=None):
        return pltpu.make_async_remote_copy(
            src_ref=src,
            dst_ref=dst,
            send_sem=self.send.at[slot if out is None else out],
            recv_sem=self.recv.at[slot],
            device_id=(self.c if ctx is None else ctx, self.z if fsdp is None else fsdp),
            device_id_type=pl.DeviceIdType.MESH,
        )

    def go(self, *args, when=None, **kw):
        made = self.copy(*args, **kw)
        if when is None:
            made.start()
        else:
            pl.when(when)(made.start)
        self.sent.append((made, when))

    def arrived(self, ref, slot):
        self.copy(ref, ref, slot).wait_recv()

    def drain(self):
        for made, when in self.sent:
            if when is None:
                made.wait_send()
            else:
                pl.when(when)(made.wait_send)
        self.sent = []

    def greet(self):
        barrier = pltpu.get_barrier_semaphore()
        for d in range(1, self.n):
            pl.semaphore_signal(
                barrier, inc=1, device_id=(lax.rem(self.c + d, self.n), self.z), device_id_type=pl.DeviceIdType.MESH
            )
        for d in range(1, self.nz):
            pl.semaphore_signal(
                barrier, inc=1, device_id=(self.c, lax.rem(self.z + d, self.nz)), device_id_type=pl.DeviceIdType.MESH
            )
        pl.semaphore_wait(barrier, self.n + self.nz - 2)


class Group:
    def __init__(self, net, hops, own):
        self.net, self.hops, self.own = net, hops, own
        self.blocks = 2 ** (len(hops) + 1)

    def at(self, places):
        index = self.own
        for place in places:
            index = index + self.net.delta[place]
        return index

    def peer(self, hop):
        if hop == "z":
            return {"fsdp": self.net.z + 1 - 2 * self.net.parity}
        return {"ctx": self.net.c + self.net.delta[hop]}

    def chip(self, turn):
        net, count = self.net, len(self.hops)
        index = 0
        for j, hop in enumerate(self.hops):
            far = (turn // (2 ** (count - 1 - j))) % 2
            if hop == "z":
                index = index + net.n * ((net.parity + far) % 2)
            else:
                index = index + hop * (((net.c // hop) + far) % 2)
        return index

    def cuts(self, columns):
        count = max(1, len(self.hops))
        units = columns // LANES
        out, first = [], 0
        for k in range(count):
            size = (units * (k + 1) // count - units * k // count) * LANES
            out.append(pl.ds(first, size))
            first += size
        return out

    def turned(self, k):
        return self.hops[k:] + self.hops[:k]


class Gather:
    def __init__(self, net, group, buf, pool):
        self.net, self.group, self.buf = net, group, buf
        self.parts = group.cuts(buf.shape[2])
        self.out = net.slot(pool, "own")
        self.slot = {}
        for k in range(len(self.parts)):
            for s in subsets(group.turned(k)):
                if s:
                    self.slot[k, s, "hop"] = net.slot(pool, k, s, "hop")
                    self.slot[k, s, "core"] = net.slot(pool, k, s, "core")

    def go(self, ref, slot, hop):
        self.net.copy(ref, ref, slot, out=self.out, **self.group.peer(hop)).start()

    def drain(self):
        ref = self.buf.at[pl.ds(0, self.group.blocks - 1)]
        self.net.copy(ref, ref, self.out, out=self.out).wait_send()

    def ref(self, k, s):
        return self.buf.at[self.group.at(s), :, self.parts[k]]

    def forward(self, k, s, core):
        order = self.group.turned(k)
        later = order[order.index(s[-1]) + 1:] if s else order
        for hop in later:
            self.go(self.ref(k, s), self.slot[k, s + (hop,), "hop"], hop)
        if core:
            self.go(self.ref(k, s), self.slot[k, s, "core"], 1)

    def start(self):
        for k in range(len(self.parts)):
            if self.group.hops:
                self.forward(k, (), False)
        self.go(self.buf.at[self.group.own], self.out, 1)

    def level(self, m):
        for k in range(len(self.parts)):
            for s in subsets(self.group.turned(k)):
                if len(s) == m:
                    self.net.arrived(self.ref(k, s), self.slot[k, s, "hop"])
                    self.forward(k, s, True)

    def levels(self, first=1):
        for m in range(first, len(self.group.hops) + 1):
            self.level(m)

    def done(self):
        self.net.arrived(self.buf.at[self.group.at((1,))], self.out)
        for k in range(len(self.parts)):
            for s in subsets(self.group.turned(k)):
                if s:
                    self.net.arrived(self.ref(k, s + (1,)), self.slot[k, s, "core"])

    def finish(self):
        self.levels()
        self.done()


class Scatter:
    def __init__(self, net, group, part, came, pool):
        self.net, self.group, self.part, self.came = net, group, part, came
        self.parts = group.cuts(part.shape[2])
        self.sets = subsets(group.hops)[::-1]
        self.count = len(self.sets)
        if (pool, "base") not in net.named:
            net.named[pool, "base"] = net.slots(self.count)
        self.base = net.named[pool, "base"]
        self.slot = {}
        for k in range(len(self.parts)):
            for step in range(len(group.hops)):
                for s in subsets(group.turned(k)[step:]):
                    if group.turned(k)[step] in s:
                        self.slot[k, s] = net.slot(pool, k, s)

    def chip(self, k):
        return self.group.chip(self.count - 1 - k)

    def sets_of(self, k):
        hops = self.group.hops
        turn = self.count - 1 - k
        return tuple(hop for j, hop in enumerate(hops) if (turn // (2 ** (len(hops) - 1 - j))) % 2)

    def push(self, k):
        first = self.chip(k)
        mine = lax.rem(self.net.c, 2)
        self.net.copy(
            self.part.at[first + 1 - mine], self.came.at[first + mine], self.base + k, out=self.base, **self.group.peer(1)
        ).start()

    def fold(self):
        part, came, at = self.part, self.came, self.group.at
        for k in range(self.count):
            s = self.sets_of(k)
            self.net.arrived(came.at[at(s + (1,))], self.base + k)
            part[at(s)] = (part[at(s)].astype(f32) + came[at(s + (1,))].astype(f32)).astype(bf)
            for p in range(len(self.parts)):
                self.onward(p, 0, s)

    def onward(self, p, step, s):
        order = self.group.turned(p)
        if step < len(order) and order[step] in s:
            key = tuple(h for h in order if h in s)
            rest = tuple(h for h in s if h != order[step])
            cut = self.parts[p]
            self.net.copy(
                self.part.at[self.group.at(s), :, cut],
                self.came.at[self.group.at(rest), :, cut],
                self.slot[p, key], out=self.base, **self.group.peer(order[step]),
            ).start()

    def reduce(self, result):
        part, came, at = self.part, self.came, self.group.at
        count = len(self.group.hops)
        for step in range(count):
            for p in range(len(self.parts)):
                order = self.group.turned(p)
                cut = self.parts[p]
                for s in subsets(order[step + 1:])[::-1]:
                    far = s + (order[step],)
                    key = tuple(h for h in order if h in far)
                    self.net.arrived(came.at[at(far), :, cut], self.slot[p, key])
                    total = part[at(s), :, cut].astype(f32) + came[at(far), :, cut].astype(f32)
                    if step == count - 1:
                        result(cut, total)
                    else:
                        part[at(s), :, cut] = total.astype(bf)
                        self.onward(p, step + 1, s)
        if not count:
            result(slice(None), part[self.group.own].astype(f32))

    def drain(self):
        ref = self.part.at[pl.ds(0, self.group.blocks - 1)]
        self.net.copy(ref, ref, self.base, out=self.base).wait_send()


def count_slots(n, nz, q):
    hops = n.bit_length() - 2
    total = 13 * (nz - 1) + 6 + 6 * (n - 1) + n.bit_length() + nz.bit_length() - 2
    for h in (hops, hops + 1)[:q]:
        total += 2 * (1 + max(1, h) * 2 * (2**h - 1)) + 2 * (2**h + max(1, h) * (2**h - 1))
    return total


def layer(dims, *refs):
    (n, nz, q, t, te, w, fw, hpd) = dims
    (x_ref, e_ref, g_ref, segd_ref, segs_ref, wsl_ref, up_ref, down_ref, vec_ref,
     mixed_ref, gtok_ref, genc_ref, fu, fd, fas, fac, fos, foc, vt, hold1, hold2,
     n1x, ex, gbuf, nbuf, wbuf, wo, wup, wdown,
     qa1, ka1, v1, vt1, ot1, ob1, lse1, qa2, ka2, v2, vt2, ot2, ob2, lse2,
     x1, x2, pa, ra, pm, rm, dy2f,
     act, du, gu, gd, gas, gac, gos, goc, ru, rd, ras, rac, ros, roc,
     su, sd, vcame, dlt, dqacc, bias_ref, bup_ref,
     send, recv, local) = refs
    length, lenc = n * t, n * te
    rows_wide = q * length
    share = D // (n * nz)
    dz = D // nz
    nq, nk2 = length // TILE, lenc // TILE
    nbt, nbe = TILE // t, TILE // te
    net = Net(n, nz, q, send, recv)
    plane, wide_group = net.plane, net.wide
    c, z, parity = net.c, net.z, net.parity
    lane = lax.broadcasted_iota(jnp.int32, (1, LANES), 1)

    rows1 = pl.ds(0, length)
    dqkv, dq2, dkv2 = act.at[rows1, pl.ds(0, 384)], act.at[rows1, pl.ds(0, LANES)], act.at[pl.ds(0, lenc), pl.ds(LANES, 256)]
    dom = [du.at[:, pl.ds(h * LANES, LANES)] for h in range(hpd)]
    dx = gtok_ref

    def wor_of(j, cc):
        return pm.at[cc, pl.ds(0, w), pl.ds(j * LANES, LANES)]

    wide = -(-n * LANES // D)

    def row(k):
        return vec_ref[k:k + 1, :]

    def into(ref):
        def store(cut, total):
            ref[:, cut] = total
        return store

    zrows = pl.ds(pl.multiple_of(z * dz, dz), dz)

    def feed_cols(zz):
        return pl.ds(pl.multiple_of((lax.rem(zz, q) * n + c) * fw, LANES), fw)

    def local_copy(src, dst, k):
        made = pltpu.make_async_copy(src, dst, local.at[k])
        made.start()
        return made

    if w == LANES:
        own_cols = [
            local_copy(
                wsl_ref.at[:, pl.ds(pl.multiple_of(block * D + c * LANES, LANES), LANES)],
                wbuf.at[zrows, pl.ds(k * LANES, LANES)], k)
            for k, block in enumerate(ORDER)
        ]
    else:
        own_cols = [local_copy(wsl_ref, wbuf.at[zrows, :], 0)]
    own_feed = [
        local_copy(up_ref.at[:, feed_cols(z)], wup.at[zrows, :], 8),
        local_copy(down_ref.at[:, feed_cols(z)], wdown.at[zrows, :], 9),
    ]
    hat, _ = normed(x_ref[...].astype(f32))
    n1x[c, :, pl.ds(0, D)] = (hat * row(0) + row(1)).astype(bf)

    def hot(seg, rows):
        place = lax.broadcasted_iota(jnp.int32, (LANES, rows), 0) % HD
        return jnp.where(place == seg[...], 1.0, 0.0).T.astype(bf)

    n1x[c, :, pl.ds(D, LANES)] = hot(segd_ref, t)
    net.greet()

    groups = ((0, 384), (384, 128), (512, 512))
    wslots = [net.slots(nz - 1) - 1 for _ in groups]
    fslots = [net.slots(nz - 1) - 1 for _ in range(4)]

    ends = jnp.logical_or(z == 0, z == nz - 1)
    inner = jnp.logical_or(z == 1, z == nz - 2)
    far_end = jnp.where(z <= 1, nz - 1, 0)
    near_end = jnp.where(z <= 1, 0, nz - 1)
    relayed = nz >= 4

    def push_z(src_of, dst, slot, relay):
        for d in range(1, nz):
            peer = lax.rem(z + d, nz)
            straight = None
            if relay and d in (1, nz - 1):
                straight = z != (nz - 1 if d == 1 else 0)
            net.go(src_of(peer), dst, slot + d, fsdp=peer, when=straight)

    def relay_z(rows_of, slot):
        rows = rows_of(far_end)
        came = slot + lax.rem(z + nz - far_end, nz)

        @pl.when(inner)
        def _():
            net.arrived(rows, came)

        net.go(rows, rows, slot + jnp.where(z <= 1, 1, nz - 1), out=net.extra(), fsdp=near_end, when=inner)

    def await_z(rows_of, slot, relay):
        for d in range(1, nz):
            source = lax.rem(z + nz - d, nz)
            if not relay:
                net.arrived(rows_of(source), slot + d)
                continue

            @pl.when(jnp.logical_not(jnp.logical_and(inner, source == far_end)))
            def _():
                net.arrived(rows_of(source), slot + d)

    def weight_rows(zz, k):
        first, size = groups[k]
        return wbuf.at[pl.ds(pl.multiple_of(zz * dz, dz), dz), pl.ds(first, size)]

    def push_weights(k):
        push_z(lambda peer: weight_rows(z, k), weight_rows(z, k), wslots[k], relayed and k != 1)

    half = dz // 2

    def feed_rows(k):
        buf = (wup, wdown)[k // 2]
        return lambda zz: buf.at[pl.ds(pl.multiple_of(zz * dz + (k % 2) * half, half), half), :]

    def push_feed(k):
        ref = (up_ref, down_ref)[k // 2]
        push_z(lambda peer: ref.at[pl.ds((k % 2) * half, half), feed_cols(peer)], feed_rows(k)(z), fslots[k], relayed and k < 3)

    gat1 = Gather(net, plane, n1x, "main")
    gat1.start()
    for made in own_cols:
        made.wait()
    push_weights(0)
    ex[c, :, pl.ds(0, D)] = e_ref[...]
    ex[c, :, pl.ds(D, LANES)] = hot(segs_ref, te)
    for k in range(1, len(groups)):
        push_weights(k)
    vt[...] = jnp.zeros_like(vt)
    bias_ref[...] = jnp.zeros_like(bias_ref)
    for k, line in enumerate((6, 7, 9, 10)):
        own = vec_ref[line:line + 1, 0:w]
        for cc in range(1, n):
            own = jnp.where(c == cc, vec_ref[line:line + 1, cc * w:(cc + 1) * w], own)
        bias_ref[k:k + 1, 0:w] = own
    own = vec_ref[13:14, 0:fw]
    for cc in range(1, n * q):
        line, first = 13 + cc * fw // D, cc * fw % D
        own = jnp.where(wide_group.own == cc, vec_ref[line:line + 1, first:first + fw], own)
    bup_ref[0:1, :] = own
    vt[8:9, :] = jnp.sum(g_ref[...].astype(f32), axis=0, keepdims=True)
    if relayed:
        @pl.when(ends)
        def _():
            for came in (ru, rd, rac, roc):
                came[far_end] = jnp.zeros(came.shape[1:], bf)

    gat1.levels()
    gate = Gather(net, plane, ex, "side")
    gate.start()
    gat1.done()
    if relayed:
        relay_z(lambda zz: weight_rows(zz, 0), wslots[0])
    await_z(lambda zz: weight_rows(zz, 0), wslots[0], relayed)

    def tile_of(buf, i, per, columns):
        return buf[pl.ds(i * per, per), :, columns].reshape(TILE, columns.size)

    head_of = lane // HD

    def put_q(qa, q, oh, rows):
        q = (q.astype(bf).astype(f32) * SCALE).astype(bf)
        for h in range(hpd):
            qa[h, rows, :] = jnp.where(head_of == h, q, oh)

    def put_k(ka, k, oh, rows):
        k = k.astype(bf)
        pen = ((oh.astype(f32) - 1.0) * -NEG).astype(bf)
        for h in range(hpd):
            ka[h, rows, :] = jnp.where(head_of == h, k, pen)

    def put_v(v, vt_ref, value, rows, i):
        value = value.astype(bf)
        v[rows, :] = value
        vt_ref[i] = value.astype(f32).T.astype(bf)

    def tile_rows(i):
        return pl.ds(pl.multiple_of(i * TILE, TILE), TILE)

    def qkv_tile(i, _):
        rows = tile_rows(i)
        got = dot(tile_of(n1x, i, nbt, pl.ds(0, D)), wbuf[:, 0:384])
        oh = tile_of(n1x, i, nbt, pl.ds(D, LANES))
        put_q(qa1, got[:, 0:128] + bias_ref[0:1, :], oh, rows)
        put_k(ka1, got[:, 128:256], oh, rows)
        put_v(v1, vt1, got[:, 256:384] + bias_ref[1:2, :], rows, i)
        return _

    lax.fori_loop(0, nq, qkv_tile, 0)

    n1f, n3f = n1x.at[:, :, pl.ds(0, D)], nbuf
    n2f = dy1f = nbuf.at[pl.ds(parity * n, n)] if q == 2 else nbuf
    gf = gbuf if q == 2 else n1f
    n2back = gf.at[pl.ds(0, n)]

    if q == 1:
        away1 = local_copy(n1f, hold1, 10)

    for k in range(4):
        push_feed(k)

    def attend(qa, ka, vt_ref, ot, ob, lse, keys, causal):
        def one(j, _):
            qrows = tile_rows(j)

            def step(i, state, diagonal):
                out = []
                for h in range(hpd):
                    top, total, acc = state[h]
                    s = dot_t(ka[h, tile_rows(i), :], qa[h, qrows, :])
                    if diagonal:
                        kp = lax.broadcasted_iota(jnp.int32, (TILE, TILE), 0)
                        qp = lax.broadcasted_iota(jnp.int32, (TILE, TILE), 1)
                        s = jnp.where(kp <= qp, s, NEG)
                    new = jnp.maximum(top, jnp.max(s, axis=0, keepdims=True))
                    p = jnp.exp(s - new)
                    fix = jnp.exp(top - new)
                    total = total * fix + jnp.sum(p, axis=0, keepdims=True)
                    acc = acc * fix + dot(vt_ref[i, pl.ds(h * HD, HD), :], p.astype(bf))
                    out.append((new, total, acc))
                return tuple(out)

            state = tuple(
                (jnp.full((1, TILE), -3e38, f32), jnp.zeros((1, TILE), f32), jnp.zeros((HD, TILE), f32))
                for _ in range(hpd)
            )
            if causal:
                state = step(j, state, True)
                state = lax.fori_loop(0, j, lambda i, st: step(i, st, False), state)
            else:
                state = lax.fori_loop(0, keys, lambda i, st: step(i, st, False), state)
            for h in range(hpd):
                top, total, acc = state[h]
                ot[j, pl.ds(h * HD, HD), :] = acc * (1.0 / total)
                lse[j, h:h + 1, :] = top + jnp.log(total)
            ob[qrows, :] = ot[j].T.astype(bf)
            return _

        if hpd * HD < LANES:
            ot[...] = jnp.zeros_like(ot)
        lax.fori_loop(0, nq, one, 0)

    await_z(lambda zz: weight_rows(zz, 1), wslots[1], False)
    oslots = [net.slots(n - 1) - 1, net.slots(n - 1) - 1]

    def out_rows(j, cc):
        return wbuf.at[pl.ds(pl.multiple_of(cc * w, w), w), pl.ds(OUT_AT[j], LANES)]

    def push_out(j):
        for d in range(1, n):
            peer = lax.rem(c + d, n)
            net.go(out_rows(j, peer), wor_of(j, c), oslots[j] + d, ctx=peer)
        wor_of(j, c)[...] = wbuf[pl.ds(pl.multiple_of(c * w, w), w), pl.ds(OUT_AT[j], LANES)]

    push_out(0)

    def await_out(j):
        for d in range(1, n):
            net.arrived(wor_of(j, lax.rem(c + n - d, n)), oslots[j] + d)
        if w < LANES:
            wo[j] = jnp.zeros((LANES, D), bf)
        wo[j, pl.ds(0, w), :] = jnp.concatenate(
            [pm[cc, pl.ds(0, w), pl.ds(j * LANES, LANES)][:, :w] for cc in range(n)], axis=-1)

    gate.levels()
    attend(qa1, ka1, vt1, ot1, ob1, lse1, nq, True)

    gate.done()
    await_out(0)

    def partial(scat, rows_of, weight_of, per):
        def one(k, _):
            first = scat.chip(k)
            scat.part[pl.ds(first, 2)] = weight_of(rows_of(first)).astype(bf).reshape(2, per, D)
            scat.push(k)
            return _

        lax.fori_loop(0, scat.count, one, 0)

    def flat(buf, per):
        return lambda first: buf[pl.ds(pl.multiple_of(first * per, 2 * per), 2 * per), :]

    rs1 = Scatter(net, plane, pa.at[pl.ds(0, n)], ra.at[pl.ds(0, n)], "sum")
    partial(rs1, flat(ob1, t), lambda rows: dot(rows, wo[0]), t)

    def kv2_tile(i, _):
        rows = tile_rows(i)
        got = dot(tile_of(ex, i, nbe, pl.ds(0, D)), wbuf[:, 512:768])
        oh = tile_of(ex, i, nbe, pl.ds(D, LANES))
        put_k(ka2, got[:, 0:128], oh, rows)
        put_v(v2, vt2, got[:, 128:256] + bias_ref[3:4, :], rows, i)
        return _

    rs1.fold()
    if relayed:
        relay_z(lambda zz: weight_rows(zz, 2), wslots[2])
    rs1.reduce(into(x1))
    x1[...] = x_ref[...].astype(f32) + (x1[...] + row(8))
    hat, _ = normed(x1[...])
    n2f[c] = (hat * row(2) + row(3)).astype(bf)
    gat1.drain()
    if q == 1:
        away1.wait()
    gat2 = Gather(net, plane, n2f, "main")
    gat2.start()
    rs1.drain()
    gate.drain()
    gat2.levels()
    await_z(lambda zz: weight_rows(zz, 2), wslots[2], relayed)
    push_out(1)
    gat2.done()
    gf[wide_group.own] = g_ref[...]
    gatg = Gather(net, wide_group, gf, "side" if q == 1 else "wideside")
    gatg.start()

    def q2_tile(i, _):
        got = dot(tile_of(n2f, i, nbt, pl.ds(0, D)), wbuf[:, 896:1024])
        put_q(qa2, got + bias_ref[2:3, :], tile_of(n1x, i, nbt, pl.ds(D, LANES)), tile_rows(i))
        return _

    lax.fori_loop(0, nq, q2_tile, 0)
    lax.fori_loop(0, nk2, kv2_tile, 0)
    if relayed:
        relay_z(feed_rows(0), fslots[0])
    away2 = local_copy(n2f, hold2, 11)
    gatg.level(1)
    attend(qa2, ka2, vt2, ot2, ob2, lse2, nk2, False)
    away2.wait()
    gat2.drain()
    await_out(1)
    rs2 = Scatter(net, plane, pa.at[pl.ds(0, n)], ra.at[pl.ds(0, n)], "sum")
    partial(rs2, flat(ob2, t), lambda rows: dot(rows, wo[1]), t)
    gatg.levels(2)
    rs2.fold()
    if relayed:
        relay_z(feed_rows(1), fslots[1])
    rs2.reduce(into(x2))
    x2[...] = x1[...] + (x2[...] + row(11))
    hat, _ = normed(x2[...])
    n3f[wide_group.own] = (hat * row(4) + row(5)).astype(bf)
    gat3 = Gather(net, wide_group, n3f, "main" if q == 1 else "wide")
    gat3.start()
    rs2.drain()
    gatg.done()
    for made in own_feed:
        made.wait()
    gat3.finish()
    for k in range(2):
        await_z(feed_rows(k), fslots[k], relayed)
    if relayed:
        relay_z(feed_rows(2), fslots[2])

    rs3 = Scatter(net, wide_group, pa, ra, "sum" if q == 1 else "widesum")
    rsm = Scatter(net, wide_group, pm, rm, "sum2" if q == 1 else "widesum2")
    fc = min(fw, 512)

    def up_tile(k, _):
        first = rs3.chip(k)
        rows = pl.ds(pl.multiple_of(first * t, 2 * t), 2 * t)
        left = n3f[pl.ds(first, 2)].reshape(2 * t, D)
        for f in range(fw // fc):
            cols = pl.ds(f * fc, fc)
            u = dot(left, wup[:, cols]) + bup_ref[0:1, cols]
            cdf, slope = gelu_parts(u)
            act[rows, cols] = (u * cdf).astype(bf)
            du[rows, cols] = slope.astype(bf)
        return _

    lax.fori_loop(0, rs3.count, up_tile, 0)
    per = TILE // (share * nz)

    def weight_grad(left_of, right, out, columns):
        def one(r, _):
            got = t_dot(left_of(tile_rows(r)), right())
            for k in range(TILE // share):
                out[k % nz, r * per + k // nz, :, columns] = got[k * share:(k + 1) * share].astype(bf)
            return _

        lax.fori_loop(0, D // TILE, one, 0)

    def whole(buf, rows):
        return lambda cols: buf[:, :, cols].reshape(rows, TILE)

    zslots = [net.slots(nz) - 1 for _ in range(6)]
    last = (4, 5)

    def push_grad(mine, came, k):
        if relayed and k not in last:
            step = jnp.where(z == 0, 1, nz - 2)
            net.go(mine.at[far_end], came.at[step], zslots[k] + nz, out=net.extra(), fsdp=step, when=ends)
        for d in range(1, nz):
            peer = lax.rem(z + d, nz)
            when = None
            if relayed and k not in last:
                when = jnp.logical_not(jnp.logical_and(
                    jnp.logical_or(ends, inner), peer == far_end))
            net.go(mine.at[peer], came.at[z], zslots[k] + d, fsdp=peer, when=when)

    def relay_grad(mine, came, k):
        if not relayed:
            return

        @pl.when(inner)
        def _():
            net.arrived(came.at[z], zslots[k] + nz)
            mine[far_end] = (mine[far_end].astype(f32) + came[z].astype(f32)).astype(bf)

        net.go(mine.at[far_end], came.at[z], zslots[k] + lax.rem(far_end - z + nz, nz), out=net.extra(), fsdp=far_end,
               when=inner)

    def grad_arrived(came, k, d):
        peer = lax.rem(z + nz - d, nz)
        if relayed and k not in last and d in (1, nz - 1):
            @pl.when(z != (0 if d == 1 else nz - 1))
            def _():
                net.arrived(came.at[peer], zslots[k] + d)
        else:
            net.arrived(came.at[peer], zslots[k] + d)
        return came[peer].astype(f32)

    def sum_grad(mine, came, k):
        total = mine[z].astype(f32)
        for d in range(1, nz):
            total = total + grad_arrived(came, k, d)
        return total.astype(bf)

    weight_grad(whole(gf, rows_wide), lambda: act[...], gd, pl.ds(0, fw))
    for k in range(2, 4):
        await_z(feed_rows(k), fslots[k], relayed and k < 3)

    push_grad(gd, rd, 1)

    def down_tile(k, sums):
        first = rs3.chip(k)
        rows = pl.ds(pl.multiple_of(first * t, 2 * t), 2 * t)
        grad = gf[pl.ds(first, 2)].reshape(2 * t, D)
        out = []
        for f in range(fw // fc):
            cols = pl.ds(f * fc, fc)
            low = (dot(grad, wdown[:, cols]) * du[rows, cols].astype(f32)).astype(bf)
            du[rows, cols] = low
            out.append(sums[f] + jnp.sum(low.astype(f32), axis=0, keepdims=True))
        pa[pl.ds(first, 2)] = dot_t(du[rows, :], wup[...]).astype(bf).reshape(2, t, D)
        rs3.push(k)
        return tuple(out)

    sums = lax.fori_loop(0, rs3.count, down_tile, tuple(jnp.zeros((1, fc), f32) for _ in range(fw // fc)))
    for f in range(fw // fc):
        for cc in range(n * q):
            place = cc * fw + f * fc
            line = 9 + 4 * wide + place // D
            vt[line:line + 1, pl.ds(place % D, fc)] = jnp.where(wide_group.own == cc, sums[f], 0.0)
    rs3.fold()
    weight_grad(whole(n3f, rows_wide), lambda: du[...], gu, pl.ds(0, fw))
    push_grad(gu, ru, 0)
    partial(rsm, flat(act, t), lambda rows: dot_t(rows, wdown[...]), t)
    rsm.fold()

    gat3.drain()
    gatg.drain()
    rs3.reduce(into(dx))
    back, gain_g, shift_g = norm_back(x2[...], row(4), dx[...])
    vt[4:5, :] = gain_g
    vt[5:6, :] = shift_g
    dx[...] = g_ref[...].astype(f32) + back
    dy = dx[...].astype(bf)
    dy2f[c] = dy
    gat4 = Gather(net, plane, dy2f, "main")
    gat4.start()
    vt[7:8, :] = jnp.sum(dy.astype(f32), axis=0, keepdims=True)
    rs3.drain()
    gat4.levels()
    back2 = local_copy(hold2, n2back, 12)
    gat4.done()

    def attend_back(qa, ka, v, ot, lse, dyf, out_w, keys, causal, dq_ref, dq_cols, dkv_ref, dk_cols, dv_cols):
        def grads(i, _):
            rows = tile_rows(i)
            low = dot_t(tile_of(dyf, i, nbt, pl.ds(0, D)), out_w[...]).astype(bf)
            for h in range(hpd):
                dom[h][rows, :] = jnp.where(head_of == h, low, jnp.zeros_like(low))
            prod = low.astype(f32).T * ot[i]
            for h in range(hpd):
                dlt[i, h:h + 1, :] = jnp.sum(prod[h * HD:(h + 1) * HD], axis=0, keepdims=True)
            dqacc[rows, :] = jnp.zeros((TILE, LANES), f32)
            return _

        lax.fori_loop(0, nq, grads, 0)

        def one(i, _):
            krows = tile_rows(i)

            def step(j, state, diagonal):
                qrows = tile_rows(j)
                dv, dks = state
                new_dks, dqs = [], []
                for h in range(hpd):
                    s = dot_t(ka[h, krows, :], qa[h, qrows, :])
                    p = jnp.exp(s - lse[j, h:h + 1, :])
                    if diagonal:
                        kp = lax.broadcasted_iota(jnp.int32, (TILE, TILE), 0)
                        qp = lax.broadcasted_iota(jnp.int32, (TILE, TILE), 1)
                        p = jnp.where(kp <= qp, p, 0.0)
                    dp = dot_t(v[krows, :], dom[h][qrows, :])
                    ds = (p * (dp - dlt[j, h:h + 1, :])).astype(bf)
                    dv = dv + dot(p.astype(bf), dom[h][qrows, :])
                    new_dks.append(dks[h] + dot(ds, qa[h, qrows, :]))
                    dqs.append(t_dot(ds, ka[h, krows, :]))
                dq = jnp.where(head_of == 0, dqs[0], dqs[-1] if hpd > 1 else 0.0)
                dqacc[qrows, :] = dqacc[qrows, :] + dq
                return dv, tuple(new_dks)

            zero = jnp.zeros((TILE, LANES), f32)
            state = (zero, tuple(zero for _ in range(hpd)))
            if causal:
                state = step(i, state, True)
                state = lax.fori_loop(i + 1, nq, lambda j, st: step(j, st, False), state)
            else:
                state = lax.fori_loop(0, nq, lambda j, st: step(j, st, False), state)
            dv, dks = state
            dk = jnp.where(head_of == 0, dks[0], dks[-1] if hpd > 1 else 0.0)
            dkv_ref[krows, dk_cols] = dk.astype(bf)
            dkv_ref[krows, dv_cols] = dv.astype(bf)
            return _

        lax.fori_loop(0, keys, one, 0)

        def close(i, _):
            rows = tile_rows(i)
            dq_ref[rows, dq_cols] = (dqacc[rows, :] * SCALE).astype(bf)
            return _

        lax.fori_loop(0, nq, close, 0)

    def head_sum(k, ref, cols):
        own = jnp.sum(ref[:, cols].astype(f32), axis=0, keepdims=True)
        for cc in range(n):
            line = 9 + k * wide + cc * LANES // D
            vt[line:line + 1, pl.ds(cc * LANES % D, LANES)] = jnp.where(c == cc, own, 0.0)

    first3 = [pl.ds(k * LANES, LANES) for k in range(3)]
    attend_back(qa2, ka2, v2, ot2, lse2, dy2f, wo.at[1], nk2, False, dq2, first3[0], dkv2, first3[0], first3[1])
    rs4 = Scatter(net, plane, pa.at[pl.ds(0, n)], ra.at[pl.ds(0, n)], "sum")
    partial(rs4, flat(dq2, t), lambda rows: dot_t(rows, wbuf[:, 896:1024]), t)
    def store_mixed(cut, total):
        mixed_ref[:, cut] = (x2[:, cut] + (total + vec_ref[12:13, cut])).astype(bf)

    rsm.reduce(store_mixed)
    rs4.fold()
    relay_grad(gd, rd, 1)

    weight_grad(whole(ex, lenc), lambda: dkv2[...], gac, pl.ds(0, 256))
    back2.wait()
    weight_grad(whole(n2back, length), lambda: dq2[...], gac, pl.ds(256, 128))
    if q == 1:
        back1 = local_copy(hold1, n1f, 13)
    push_grad(gac, rac, 2)

    def out_grad(ob, dyf, out):
        for cut in (0, 1):
            cols = pl.ds(cut * (D // 2), D // 2)
            got = t_dot(ob[...], dyf[:, :, cols].reshape(length, D // 2))
            for k in range(nz):
                out[k, :, cols] = got[k * share:(k + 1) * share].astype(bf)

    rs4.reduce(into(x2))
    back, gain_g, shift_g = norm_back(x1[...], row(2), x2[...])
    vt[2:3, :] = gain_g
    vt[3:4, :] = shift_g
    dx[...] = dx[...] + back
    dy = dx[...].astype(bf)
    dy1f[c] = dy
    gat4.drain()
    gat5 = Gather(net, plane, dy1f, "main")
    gat5.start()
    vt[6:7, :] = jnp.sum(dy.astype(f32), axis=0, keepdims=True)
    head_sum(2, dq2, first3[0])
    head_sum(3, dkv2, first3[1])
    rs4.drain()
    rsm.drain()
    rse = Scatter(net, plane, pm.at[pl.ds(0, n), pl.ds(0, te), :], rm.at[pl.ds(0, n), pl.ds(0, te), :], "sum2")
    partial(rse, flat(dkv2, te), lambda rows: dot_t(rows, wbuf[:, 512:768]), te)
    gat5.levels()
    rse.fold()
    out_grad(ob2, dy2f, goc)
    push_grad(goc, roc, 3)
    gat5.done()
    out_grad(ob1, dy1f, gos)
    push_grad(gos, ros, 5)
    attend_back(qa1, ka1, v1, ot1, lse1, dy1f, wo.at[0], nq, True, dqkv, first3[0], dqkv, first3[1], first3[2])
    relay_grad(gu, ru, 0)
    rs5 = Scatter(net, plane, pa.at[pl.ds(0, n)], ra.at[pl.ds(0, n)], "sum")
    partial(rs5, flat(dqkv, t), lambda rows: dot_t(rows, wbuf[:, 0:384]), t)
    rs5.fold()
    relay_grad(gac, rac, 2)
    rse.reduce(into(genc_ref))
    if q == 1:
        back1.wait()
    weight_grad(whole(n1f, length), lambda: dqkv[...], gas, pl.ds(0, 384))
    push_grad(gas, ras, 4)
    relay_grad(goc, roc, 3)
    rs5.reduce(into(x2))
    back, gain_g, shift_g = norm_back(x_ref[...].astype(f32), row(0), x2[...])
    vt[0:1, :] = gain_g
    vt[1:2, :] = shift_g
    gtok_ref[...] = dx[...] + back
    head_sum(0, dqkv, first3[0])
    head_sum(1, dqkv, first3[2])

    vslots = net.slots(vcame.shape[0])
    pairs = [("ctx", b) for b in plane.hops + [1]] + [("fsdp", 1 << k) for k in range(nz.bit_length() - 1)]

    def swap(k):
        axis, b = pairs[k]
        own = c if axis == "ctx" else z
        peer = own + b - 2 * b * ((own // b) % 2)
        made = net.copy(vt, vcame.at[k], vslots + k, **{axis: peer})
        made.start()
        return made

    def merge(k, made):
        made.wait_send()
        net.arrived(vcame.at[k], vslots + k)
        vt[...] = vt[...] + vcame[k]

    def sum_feed(mine, came, k, total):
        for r in range(q):
            got = 0.0
            for d in range(r, nz, q):
                if d == 0:
                    got = got + mine[z].astype(f32)
                else:
                    got = got + grad_arrived(came, k, d)
            total[:, lax.rem(parity + q - r, q)] = got.astype(bf)

    def sum_heads(mine, came, k):
        mine[z] = sum_grad(mine, came, k)
        return mine.at[z]

    def exchange(total, out):
        slot = net.slots(n - 1) - 1
        out[c] = total[c]
        for d in range(1, n):
            peer = lax.rem(c + d, n)
            net.go(total.at[peer], out.at[c], slot + d, ctx=peer)

        def done():
            for d in range(1, n):
                net.arrived(out.at[lax.rem(c + n - d, n)], slot + d)
        return done

    waits = []
    todo = [
        lambda: (sum_feed(gu, ru, 0, su), waits.append(exchange(su, fu))),
        lambda: (sum_feed(gd, rd, 1, sd), waits.append(exchange(sd, fd))),
        lambda: waits.append(exchange(sum_heads(gac, rac, 2), fac)),
    ]
    for k in range(len(pairs)):
        made = swap(k)
        if todo:
            todo.pop(0)()
        merge(k, made)
    for step in todo:
        step()
    foc[...] = sum_grad(goc, roc, 3)
    waits.append(exchange(sum_heads(gas, ras, 4), fas))
    fos[...] = sum_grad(gos, ros, 5)
    for wait in waits:
        wait()
    rs5.drain()
    rse.drain()
    gat5.drain()
    net.drain()
    assert net.used == count_slots(n, nz, q) and net.extras <= EXTRAS


def body(tokens, encoder, dec_seg, src_seg, attn_w, up_w, down_w, vec, cot):
    n, nz = lax.axis_size("ctx"), lax.axis_size("fsdp")
    c = lax.axis_index("ctx")
    t, te = tokens.shape[1], encoder.shape[1]
    ff = up_w.shape[1]
    q = 1
    w, fw = D // n, ff // (n * q)
    hpd = w // HD
    dz = D // nz
    share = D // (n * nz)
    length, lenc = n * t, n * te

    if w < LANES:
        wsl = lax.dynamic_slice_in_dim(attn_w.reshape(dz, 8, D), c * w, w, axis=2)
        wsl = jnp.stack([wsl[:, k] for k in ORDER], axis=1)
        attn_w = jnp.pad(wsl, ((0, 0), (0, 0), (0, LANES - w))).reshape(dz, 8 * LANES)

    nq, nk2 = length // TILE, lenc // TILE
    slots = count_slots(n, nz, q)
    dims = (n, nz, q, t, te, w, fw, hpd)
    wide = -(-n * LANES // D)
    vrows = -(-(9 + 4 * wide + ff // D) // 8) * 8
    steps = n.bit_length() + nz.bit_length() - 2
    out_shape = (
        jax.ShapeDtypeStruct((t, D), bf),
        jax.ShapeDtypeStruct((t, D), f32),
        jax.ShapeDtypeStruct((te, D), f32),
        jax.ShapeDtypeStruct((n, q, share, fw), bf),
        jax.ShapeDtypeStruct((n, q, share, fw), bf),
        jax.ShapeDtypeStruct((n, share, 384), bf),
        jax.ShapeDtypeStruct((n, share, 384), bf),
        jax.ShapeDtypeStruct((share, D), bf),
        jax.ShapeDtypeStruct((share, D), bf),
        jax.ShapeDtypeStruct((vrows, D), f32),
        jax.ShapeDtypeStruct((n, t, D), bf),
        jax.ShapeDtypeStruct((n, t, D), bf),
    )

    def attn_scratch(keys):
        return [
            pltpu.VMEM((hpd, length, LANES), bf), pltpu.VMEM((hpd, keys, LANES), bf), pltpu.VMEM((keys, LANES), bf),
            pltpu.VMEM((keys // TILE, LANES, TILE), bf), pltpu.VMEM((nq, LANES, TILE), f32),
            pltpu.VMEM((length, LANES), bf), pltpu.VMEM((nq, 8, TILE), f32),
        ]

    scratch = [
        pltpu.VMEM((n, t, D + LANES), bf), pltpu.VMEM((n, te, D + LANES), bf),
        pltpu.VMEM((q * n, t, D) if q == 2 else (1, 16, LANES), bf), pltpu.VMEM((q * n, t, D), bf),
        pltpu.VMEM((D, 8 * LANES), bf), pltpu.VMEM((2, LANES, D), bf),
        pltpu.VMEM((D, fw), bf), pltpu.VMEM((D, fw), bf),
        *attn_scratch(length), *attn_scratch(lenc),
        pltpu.VMEM((t, D), f32), pltpu.VMEM((t, D), f32),
        *[pltpu.VMEM((q * n, t, D), bf) for _ in range(4)], pltpu.VMEM((n, t, D), bf),
        pltpu.VMEM((q * length, fw), bf), pltpu.VMEM((q * length, fw), bf),
    ]
    for _ in range(2):
        scratch += [
            pltpu.VMEM((nz, n, share, fw), bf), pltpu.VMEM((nz, n, share, fw), bf),
            pltpu.VMEM((nz, n, share, 384), bf), pltpu.VMEM((nz, n, share, 384), bf),
            pltpu.VMEM((nz, share, D), bf), pltpu.VMEM((nz, share, D), bf),
        ]
    scratch += [
        pltpu.VMEM((n, q, share, fw), bf), pltpu.VMEM((n, q, share, fw), bf), pltpu.VMEM((steps, vrows, D), f32),
        pltpu.VMEM((nq, 8, TILE), f32), pltpu.VMEM((length, LANES), f32),
        pltpu.VMEM((8, LANES), f32), pltpu.VMEM((8, fw), f32),
        pltpu.SemaphoreType.DMA((slots + EXTRAS,)), pltpu.SemaphoreType.DMA((slots,)), pltpu.SemaphoreType.DMA((16,)),
    ]
    vmem = pl.BlockSpec(memory_space=pltpu.VMEM)
    hbm = pl.BlockSpec(memory_space=pl.ANY)
    mixed, gtok, genc, fu, fd, fas, fac, fos, foc, vsum, _, _ = pl.pallas_call(
        functools.partial(layer, dims),
        out_shape=out_shape,
        in_specs=[vmem] * 5 + [hbm] * 3 + [vmem],
        out_specs=[vmem] * (len(out_shape) - 2) + [hbm] * 2,
        scratch_shapes=scratch,
        compiler_params=pltpu.CompilerParams(
            collective_id=0, has_side_effects=True, vmem_limit_bytes=63 * 1024 * 1024
        ),
        cost_estimate=pl.CostEstimate(flops=21_000_000_000, bytes_accessed=30_000_000, transcendentals=8_000_000),
        name="layer",
    )(tokens[0], encoder[0], cot[0], dec_seg, src_seg, attn_w, up_w, down_w, vec)

    return pl.pallas_call(
        functools.partial(closing, (n, q, w, fw, wide)),
        out_shape=(
            jax.ShapeDtypeStruct((1, t, D), bf), jax.ShapeDtypeStruct((1, t, D), f32),
            jax.ShapeDtypeStruct((1, te, D), f32), jax.ShapeDtypeStruct((share, 8 * D), f32),
            jax.ShapeDtypeStruct((share, ff), f32), jax.ShapeDtypeStruct((share, ff), f32),
            jax.ShapeDtypeStruct(vec.shape, f32),
        ),
        in_specs=[hbm] * 10,
        out_specs=[hbm] * 7,
        scratch_shapes=[pltpu.VMEM(a.shape, a.dtype) for a in (mixed, gtok, genc, fu, fd, fas, fac, fos, foc, vsum)] + [
            pltpu.VMEM((share, 8 * D), f32), pltpu.VMEM((share, ff), f32), pltpu.VMEM((share, ff), f32),
            pltpu.VMEM(vec.shape, f32), pltpu.SemaphoreType.DMA((17,)),
        ],
        compiler_params=pltpu.CompilerParams(vmem_limit_bytes=62 * 1024 * 1024),
        name="closing",
    )(mixed, gtok, genc, fu, fd, fas, fac, fos, foc, vsum)


def closing(dims, *refs):
    n, q, w, fw, wide = dims
    given, outs, kept, made, sems = refs[:10], refs[10:17], refs[17:27], refs[27:31], refs[31]
    coming = [pltpu.make_async_copy(given[k], kept[k], sems.at[k]) for k in range(10)]
    straight = [pltpu.make_async_copy(kept[k], outs[k].at[0], sems.at[10 + k]) for k in range(3)]
    going = [pltpu.make_async_copy(made[k], outs[3 + k], sems.at[13 + k]) for k in range(4)]
    for copy in coming:
        copy.start()
    for k in range(3):
        coming[k].wait()
        straight[k].start()
    kept, coming = kept[3:], coming[3:]
    fu, fd, fas, fac, fos, foc, vsum = kept
    o_attn, o_up, o_down, o_vec = made
    coming[0].wait()
    for cc in range(n * q):
        o_up[:, pl.ds(cc * fw, fw)] = fu[cc % n, cc // n].astype(f32)
    going[1].start()
    coming[1].wait()
    for cc in range(n * q):
        o_down[:, pl.ds(cc * fw, fw)] = fd[cc % n, cc // n].astype(f32)
    going[2].start()
    for k in range(2, 7):
        coming[k].wait()
    for block, (ref, k) in enumerate(
        ((fas, 0), (fas, 1), (fas, 2), (fos, None), (fac, 2), (fac, 0), (fac, 1), (foc, None))
    ):
        if k is None:
            got = ref[...]
        else:
            got = jnp.concatenate([ref[cc, :, pl.ds(k * LANES, LANES)][:, :w] for cc in range(n)], axis=-1)
        o_attn[:, pl.ds(block * D, D)] = got.astype(f32)
    going[0].start()

    def heads(k):
        parts = []
        for cc in range(n):
            line, first = 9 + k * wide + cc * LANES // D, cc * LANES % D
            parts.append(vsum[line:line + 1, first:first + LANES][:, :w])
        return jnp.concatenate(parts, axis=-1)

    o_vec[0:6] = vsum[0:6]
    o_vec[6:7] = heads(0)
    o_vec[7:8] = heads(1)
    o_vec[8:9] = vsum[6:7]
    o_vec[9:10] = heads(2)
    o_vec[10:11] = heads(3)
    o_vec[11:13] = vsum[7:9]
    up = 9 + 4 * wide
    o_vec[13:] = vsum[up:up + o_vec.shape[0] - 13]
    going[3].start()
    for copy in straight + going:
        copy.wait()


def solution(mesh):
    return jax.shard_map(
        body, mesh=mesh,
        in_specs=(P("fsdp", "ctx", None), P("fsdp", "ctx", None), P("fsdp", "ctx"), P("fsdp", "ctx"), P("fsdp", None),
                  P("fsdp", None), P("fsdp", None), P(), P("fsdp", "ctx", None)),
        out_specs=(P("fsdp", "ctx", None), P("fsdp", "ctx", None), P("fsdp", "ctx", None), P(("ctx", "fsdp"), None),
                   P(("ctx", "fsdp"), None), P(("ctx", "fsdp"), None), P()),
        check_vma=False,
    )
```

```python
import functools

import jax
import jax.numpy as jnp
from jax import lax
from jax.experimental import pallas as pl
from jax.experimental.pallas import tpu as pltpu
from jax.sharding import PartitionSpec as P

D = 1024
HD = 64
LANES = 128
TILE = 256
EXTRAS = 16
EPS = 1e-05
NEG = -1e30
SCALE = HD ** (-0.5)
bf = jnp.bfloat16
f32 = jnp.float32
ORDER = (0, 1, 2, 3, 5, 6, 7, 4)
OUT_AT = (384, 768)


def dot(a, b):
    return jnp.dot(a, b, preferred_element_type=f32)


def dot_t(a, b):
    return lax.dot_general(a, b, (((1,), (1,)), ((), ())), preferred_element_type=f32)


def t_dot(a, b):
    return lax.dot_general(a, b, (((0,), (0,)), ((), ())), preferred_element_type=f32)


def normed(value):
    centred = value - jnp.mean(value, axis=-1, keepdims=True)
    inv = lax.rsqrt(jnp.mean(centred * centred, axis=-1, keepdims=True) + EPS)
    return centred * inv, inv


def norm_back(value, gain, grad):
    hat, inv = normed(value)
    scaled = grad * gain
    back = inv * (
        scaled
        - jnp.mean(scaled, axis=-1, keepdims=True)
        - hat * jnp.mean(scaled * hat, axis=-1, keepdims=True)
    )
    return back, jnp.sum(grad * hat, axis=0, keepdims=True), jnp.sum(grad, axis=0, keepdims=True)


def gelu_parts(u):
    e = jnp.exp(-0.5 * u * u)
    t = 1.0 / (1.0 + (0.3275911 * 2.0**-0.5) * jnp.abs(u))
    poly = 0.5 * 1.061405429
    for term in (-1.453152027, 1.421413741, -0.284496736, 0.254829592):
        poly = poly * t + 0.5 * term
    tail = poly * t * e
    cdf = jnp.where(u >= 0.0, 1.0 - tail, tail)
    return cdf, cdf + u * (e * 0.3989422804014327)


def subsets(items):
    out = [()]
    for item in items:
        out = out + [s + (item,) for s in out]
    return sorted(out, key=len)


class Net:
    def __init__(self, n, nz, q, send, recv):
        self.n, self.nz = n, nz
        self.c = lax.axis_index("ctx")
        self.z = lax.axis_index("fsdp")
        self.send, self.recv = send, recv
        self.used = self.extras = 0
        self.named = {}
        self.sent = []
        hops = [n >> k for k in range(1, n.bit_length() - 1)]
        self.parity = lax.rem(self.z, q)
        self.delta = {b: b - 2 * b * ((self.c // b) % 2) for b in hops + [1]}
        self.delta["z"] = n * (1 - 2 * self.parity)
        self.plane = Group(self, hops, self.c)
        self.wide = Group(self, ["z"] + hops, self.parity * n + self.c) if q == 2 else self.plane

    def slots(self, count):
        first = self.used
        self.used += count
        return first

    def extra(self):
        self.extras += 1
        return self.send.shape[0] - self.extras

    def slot(self, *key):
        if key not in self.named:
            self.named[key] = self.slots(1)
        return self.named[key]

    def copy(self, src, dst, slot, ctx=None, fsdp=None, out=None):
        return pltpu.make_async_remote_copy(
            src_ref=src,
            dst_ref=dst,
            send_sem=self.send.at[slot if out is None else out],
            recv_sem=self.recv.at[slot],
            device_id=(self.c if ctx is None else ctx, self.z if fsdp is None else fsdp),
            device_id_type=pl.DeviceIdType.MESH,
        )

    def go(self, *args, when=None, **kw):
        made = self.copy(*args, **kw)
        if when is None:
            made.start()
        else:
            pl.when(when)(made.start)
        self.sent.append((made, when))

    def arrived(self, ref, slot):
        self.copy(ref, ref, slot).wait_recv()

    def drain(self):
        for made, when in self.sent:
            if when is None:
                made.wait_send()
            else:
                pl.when(when)(made.wait_send)
        self.sent = []

    def greet(self):
        barrier = pltpu.get_barrier_semaphore()
        for d in range(1, self.n):
            pl.semaphore_signal(
                barrier, inc=1, device_id=(lax.rem(self.c + d, self.n), self.z), device_id_type=pl.DeviceIdType.MESH
            )
        for d in range(1, self.nz):
            pl.semaphore_signal(
                barrier, inc=1, device_id=(self.c, lax.rem(self.z + d, self.nz)), device_id_type=pl.DeviceIdType.MESH
            )
        pl.semaphore_wait(barrier, self.n + self.nz - 2)


class Group:
    def __init__(self, net, hops, own):
        self.net, self.hops, self.own = net, hops, own
        self.blocks = 2 ** (len(hops) + 1)

    def at(self, places):
        index = self.own
        for place in places:
            index = index + self.net.delta[place]
        return index

    def peer(self, hop):
        if hop == "z":
            return {"fsdp": self.net.z + 1 - 2 * self.net.parity}
        return {"ctx": self.net.c + self.net.delta[hop]}

    def chip(self, turn):
        net, count = self.net, len(self.hops)
        index = 0
        for j, hop in enumerate(self.hops):
            far = (turn // (2 ** (count - 1 - j))) % 2
            if hop == "z":
                index = index + net.n * ((net.parity + far) % 2)
            else:
                index = index + hop * (((net.c // hop) + far) % 2)
        return index

    def cuts(self, columns):
        count = max(1, len(self.hops))
        units = columns // LANES
        out, first = [], 0
        for k in range(count):
            size = (units * (k + 1) // count - units * k // count) * LANES
            out.append(pl.ds(first, size))
            first += size
        return out

    def turned(self, k):
        return self.hops[k:] + self.hops[:k]


class Gather:
    def __init__(self, net, group, buf, pool):
        self.net, self.group, self.buf = net, group, buf
        self.parts = group.cuts(buf.shape[2])
        self.out = net.slot(pool, "own")
        self.slot = {}
        for k in range(len(self.parts)):
            for s in subsets(group.turned(k)):
                if s:
                    self.slot[k, s, "hop"] = net.slot(pool, k, s, "hop")
                    self.slot[k, s, "core"] = net.slot(pool, k, s, "core")

    def go(self, ref, slot, hop):
        self.net.copy(ref, ref, slot, out=self.out, **self.group.peer(hop)).start()

    def drain(self):
        ref = self.buf.at[pl.ds(0, self.group.blocks - 1)]
        self.net.copy(ref, ref, self.out, out=self.out).wait_send()

    def ref(self, k, s):
        return self.buf.at[self.group.at(s), :, self.parts[k]]

    def forward(self, k, s, core):
        order = self.group.turned(k)
        later = order[order.index(s[-1]) + 1:] if s else order
        for hop in later:
            self.go(self.ref(k, s), self.slot[k, s + (hop,), "hop"], hop)
        if core:
            self.go(self.ref(k, s), self.slot[k, s, "core"], 1)

    def start(self):
        for k in range(len(self.parts)):
            if self.group.hops:
                self.forward(k, (), False)
        self.go(self.buf.at[self.group.own], self.out, 1)

    def level(self, m):
        for k in range(len(self.parts)):
            for s in subsets(self.group.turned(k)):
                if len(s) == m:
                    self.net.arrived(self.ref(k, s), self.slot[k, s, "hop"])
                    self.forward(k, s, True)

    def levels(self, first=1):
        for m in range(first, len(self.group.hops) + 1):
            self.level(m)

    def done(self):
        self.net.arrived(self.buf.at[self.group.at((1,))], self.out)
        for k in range(len(self.parts)):
            for s in subsets(self.group.turned(k)):
                if s:
                    self.net.arrived(self.ref(k, s + (1,)), self.slot[k, s, "core"])

    def finish(self):
        self.levels()
        self.done()


class Scatter:
    def __init__(self, net, group, part, came, pool):
        self.net, self.group, self.part, self.came = net, group, part, came
        self.parts = group.cuts(part.shape[2])
        self.sets = subsets(group.hops)[::-1]
        self.count = len(self.sets)
        if (pool, "base") not in net.named:
            net.named[pool, "base"] = net.slots(self.count)
        self.base = net.named[pool, "base"]
        self.slot = {}
        for k in range(len(self.parts)):
            for step in range(len(group.hops)):
                for s in subsets(group.turned(k)[step:]):
                    if group.turned(k)[step] in s:
                        self.slot[k, s] = net.slot(pool, k, s)

    def chip(self, k):
        return self.group.chip(self.count - 1 - k)

    def sets_of(self, k):
        hops = self.group.hops
        turn = self.count - 1 - k
        return tuple(hop for j, hop in enumerate(hops) if (turn // (2 ** (len(hops) - 1 - j))) % 2)

    def push(self, k):
        first = self.chip(k)
        mine = lax.rem(self.net.c, 2)
        self.net.copy(
            self.part.at[first + 1 - mine], self.came.at[first + mine], self.base + k, out=self.base, **self.group.peer(1)
        ).start()

    def fold(self):
        part, came, at = self.part, self.came, self.group.at
        for k in range(self.count):
            s = self.sets_of(k)
            self.net.arrived(came.at[at(s + (1,))], self.base + k)
            part[at(s)] = (part[at(s)].astype(f32) + came[at(s + (1,))].astype(f32)).astype(bf)
            for p in range(len(self.parts)):
                self.onward(p, 0, s)

    def onward(self, p, step, s):
        order = self.group.turned(p)
        if step < len(order) and order[step] in s:
            key = tuple(h for h in order if h in s)
            rest = tuple(h for h in s if h != order[step])
            cut = self.parts[p]
            self.net.copy(
                self.part.at[self.group.at(s), :, cut],
                self.came.at[self.group.at(rest), :, cut],
                self.slot[p, key], out=self.base, **self.group.peer(order[step]),
            ).start()

    def reduce(self, result):
        part, came, at = self.part, self.came, self.group.at
        count = len(self.group.hops)
        for step in range(count):
            for p in range(len(self.parts)):
                order = self.group.turned(p)
                cut = self.parts[p]
                for s in subsets(order[step + 1:])[::-1]:
                    far = s + (order[step],)
                    key = tuple(h for h in order if h in far)
                    self.net.arrived(came.at[at(far), :, cut], self.slot[p, key])
                    total = part[at(s), :, cut].astype(f32) + came[at(far), :, cut].astype(f32)
                    if step == count - 1:
                        result(cut, total)
                    else:
                        part[at(s), :, cut] = total.astype(bf)
                        self.onward(p, step + 1, s)
        if not count:
            result(slice(None), part[self.group.own].astype(f32))

    def drain(self):
        ref = self.part.at[pl.ds(0, self.group.blocks - 1)]
        self.net.copy(ref, ref, self.base, out=self.base).wait_send()


def count_slots(n, nz, q):
    hops = n.bit_length() - 2
    total = 13 * (nz - 1) + 6 + 6 * (n - 1) + n.bit_length() + nz.bit_length() - 2
    for h in (hops, hops + 1)[:q]:
        total += 2 * (1 + max(1, h) * 2 * (2**h - 1)) + 2 * (2**h + max(1, h) * (2**h - 1))
    return total


def layer(dims, *refs):
    (n, nz, q, t, te, w, fw, hpd) = dims
    (x_ref, e_ref, g_ref, segd_ref, segs_ref, wsl_ref, up_ref, down_ref, vec_ref,
     mixed_ref, gtok_ref, genc_ref, fu, fd, fas, fac, fos, foc, vt, hold1, hold2,
     n1x, ex, gbuf, nbuf, wbuf, wo, wup, wdown,
     qa1, ka1, v1, vt1, ot1, ob1, lse1, qa2, ka2, v2, vt2, ot2, ob2, lse2,
     x1, x2, pa, ra, pm, rm, dy2f,
     act, du, gu, gd, gas, gac, gos, goc, ru, rd, ras, rac, ros, roc,
     su, sd, vcame, dlt, dqacc, bias_ref, bup_ref,
     send, recv, local) = refs
    length, lenc = n * t, n * te
    rows_wide = q * length
    share = D // (n * nz)
    dz = D // nz
    nq, nk2 = length // TILE, lenc // TILE
    nbt, nbe = TILE // t, TILE // te
    net = Net(n, nz, q, send, recv)
    plane, wide_group = net.plane, net.wide
    c, z, parity = net.c, net.z, net.parity
    lane = lax.broadcasted_iota(jnp.int32, (1, LANES), 1)

    rows1 = pl.ds(0, length)
    dqkv, dq2, dkv2 = act.at[rows1, pl.ds(0, 384)], act.at[rows1, pl.ds(0, LANES)], act.at[pl.ds(0, lenc), pl.ds(LANES, 256)]
    dom = [du.at[:, pl.ds(h * LANES, LANES)] for h in range(hpd)]
    dx = gtok_ref

    def wor_of(j, cc):
        return pm.at[cc, pl.ds(0, w), pl.ds(j * LANES, LANES)]

    wide = -(-n * LANES // D)

    def row(k):
        return vec_ref[k:k + 1, :]

    def into(ref):
        def store(cut, total):
            ref[:, cut] = total
        return store

    zrows = pl.ds(pl.multiple_of(z * dz, dz), dz)

    def feed_cols(zz):
        return pl.ds(pl.multiple_of((lax.rem(zz, q) * n + c) * fw, LANES), fw)

    def local_copy(src, dst, k):
        made = pltpu.make_async_copy(src, dst, local.at[k])
        made.start()
        return made

    if w == LANES:
        own_cols = [
            local_copy(
                wsl_ref.at[:, pl.ds(pl.multiple_of(block * D + c * LANES, LANES), LANES)],
                wbuf.at[zrows, pl.ds(k * LANES, LANES)], k)
            for k, block in enumerate(ORDER)
        ]
    else:
        own_cols = [local_copy(wsl_ref, wbuf.at[zrows, :], 0)]
    own_feed = [
        local_copy(up_ref.at[:, feed_cols(z)], wup.at[zrows, :], 8),
        local_copy(down_ref.at[:, feed_cols(z)], wdown.at[zrows, :], 9),
    ]
    hat, _ = normed(x_ref[...].astype(f32))
    n1x[c, :, pl.ds(0, D)] = (hat * row(0) + row(1)).astype(bf)

    def hot(seg, rows):
        place = lax.broadcasted_iota(jnp.int32, (LANES, rows), 0) % HD
        return jnp.where(place == seg[...], 1.0, 0.0).T.astype(bf)

    n1x[c, :, pl.ds(D, LANES)] = hot(segd_ref, t)
    net.greet()

    groups = ((0, 384), (384, 128), (512, 512))
    wslots = [net.slots(nz - 1) - 1 for _ in groups]
    fslots = [net.slots(nz - 1) - 1 for _ in range(4)]

    ends = jnp.logical_or(z == 0, z == nz - 1)
    inner = jnp.logical_or(z == 1, z == nz - 2)
    far_end = jnp.where(z <= 1, nz - 1, 0)
    near_end = jnp.where(z <= 1, 0, nz - 1)
    relayed = nz >= 4

    def push_z(src_of, dst, slot, relay):
        for d in range(1, nz):
            peer = lax.rem(z + d, nz)
            straight = None
            if relay and d in (1, nz - 1):
                straight = z != (nz - 1 if d == 1 else 0)
            net.go(src_of(peer), dst, slot + d, fsdp=peer, when=straight)

    def relay_z(rows_of, slot):
        rows = rows_of(far_end)
        came = slot + lax.rem(z + nz - far_end, nz)

        @pl.when(inner)
        def _():
            net.arrived(rows, came)

        net.go(rows, rows, slot + jnp.where(z <= 1, 1, nz - 1), out=net.extra(), fsdp=near_end, when=inner)

    def await_z(rows_of, slot, relay):
        for d in range(1, nz):
            source = lax.rem(z + nz - d, nz)
            if not relay:
                net.arrived(rows_of(source), slot + d)
                continue

            @pl.when(jnp.logical_not(jnp.logical_and(inner, source == far_end)))
            def _():
                net.arrived(rows_of(source), slot + d)

    def weight_rows(zz, k):
        first, size = groups[k]
        return wbuf.at[pl.ds(pl.multiple_of(zz * dz, dz), dz), pl.ds(first, size)]

    def push_weights(k):
        push_z(lambda peer: weight_rows(z, k), weight_rows(z, k), wslots[k], relayed and k != 1)

    half = dz // 2

    def feed_rows(k):
        buf = (wup, wdown)[k // 2]
        return lambda zz: buf.at[pl.ds(pl.multiple_of(zz * dz + (k % 2) * half, half), half), :]

    def push_feed(k):
        ref = (up_ref, down_ref)[k // 2]
        push_z(lambda peer: ref.at[pl.ds((k % 2) * half, half), feed_cols(peer)], feed_rows(k)(z), fslots[k], relayed and k < 3)

    gat1 = Gather(net, plane, n1x, "main")
    gat1.start()
    for made in own_cols:
        made.wait()
    push_weights(0)
    ex[c, :, pl.ds(0, D)] = e_ref[...]
    ex[c, :, pl.ds(D, LANES)] = hot(segs_ref, te)
    for k in range(1, len(groups)):
        push_weights(k)
    vt[...] = jnp.zeros_like(vt)
    bias_ref[...] = jnp.zeros_like(bias_ref)
    for k, line in enumerate((6, 7, 9, 10)):
        own = vec_ref[line:line + 1, 0:w]
        for cc in range(1, n):
            own = jnp.where(c == cc, vec_ref[line:line + 1, cc * w:(cc + 1) * w], own)
        bias_ref[k:k + 1, 0:w] = own
    own = vec_ref[13:14, 0:fw]
    for cc in range(1, n * q):
        line, first = 13 + cc * fw // D, cc * fw % D
        own = jnp.where(wide_group.own == cc, vec_ref[line:line + 1, first:first + fw], own)
    bup_ref[0:1, :] = own
    vt[8:9, :] = jnp.sum(g_ref[...].astype(f32), axis=0, keepdims=True)
    if relayed:
        @pl.when(ends)
        def _():
            for came in (ru, rd, rac, roc):
                came[far_end] = jnp.zeros(came.shape[1:], bf)

    gat1.levels()
    gate = Gather(net, plane, ex, "side")
    gate.start()
    gat1.done()
    if relayed:
        relay_z(lambda zz: weight_rows(zz, 0), wslots[0])
    await_z(lambda zz: weight_rows(zz, 0), wslots[0], relayed)

    def tile_of(buf, i, per, columns):
        return buf[pl.ds(i * per, per), :, columns].reshape(TILE, columns.size)

    head_of = lane // HD

    def put_q(qa, q, oh, rows):
        q = (q.astype(bf).astype(f32) * SCALE).astype(bf)
        for h in range(hpd):
            qa[h, rows, :] = jnp.where(head_of == h, q, oh)

    def put_k(ka, k, oh, rows):
        k = k.astype(bf)
        pen = ((oh.astype(f32) - 1.0) * -NEG).astype(bf)
        for h in range(hpd):
            ka[h, rows, :] = jnp.where(head_of == h, k, pen)

    def put_v(v, vt_ref, value, rows, i):
        value = value.astype(bf)
        v[rows, :] = value
        vt_ref[i] = value.astype(f32).T.astype(bf)

    def tile_rows(i):
        return pl.ds(pl.multiple_of(i * TILE, TILE), TILE)

    def qkv_tile(i, _):
        rows = tile_rows(i)
        got = dot(tile_of(n1x, i, nbt, pl.ds(0, D)), wbuf[:, 0:384])
        oh = tile_of(n1x, i, nbt, pl.ds(D, LANES))
        put_q(qa1, got[:, 0:128] + bias_ref[0:1, :], oh, rows)
        put_k(ka1, got[:, 128:256], oh, rows)
        put_v(v1, vt1, got[:, 256:384] + bias_ref[1:2, :], rows, i)
        return _

    lax.fori_loop(0, nq, qkv_tile, 0)

    n1f, n3f = n1x.at[:, :, pl.ds(0, D)], nbuf
    n2f = dy1f = nbuf.at[pl.ds(parity * n, n)] if q == 2 else nbuf
    gf = gbuf if q == 2 else n1f
    n2back = gf.at[pl.ds(0, n)]

    if q == 1:
        away1 = local_copy(n1f, hold1, 10)

    def attend(qa, ka, vt_ref, ot, ob, lse, keys, causal):
        def one(j, _):
            qrows = tile_rows(j)

            def step(i, state, diagonal):
                out = []
                for h in range(hpd):
                    top, total, acc = state[h]
                    s = dot_t(ka[h, tile_rows(i), :], qa[h, qrows, :])
                    if diagonal:
                        kp = lax.broadcasted_iota(jnp.int32, (TILE, TILE), 0)
                        qp = lax.broadcasted_iota(jnp.int32, (TILE, TILE), 1)
                        s = jnp.where(kp <= qp, s, NEG)
                    new = jnp.maximum(top, jnp.max(s, axis=0, keepdims=True))
                    p = jnp.exp(s - new)
                    fix = jnp.exp(top - new)
                    total = total * fix + jnp.sum(p, axis=0, keepdims=True)
                    acc = acc * fix + dot(vt_ref[i, pl.ds(h * HD, HD), :], p.astype(bf))
                    out.append((new, total, acc))
                return tuple(out)

            state = tuple(
                (jnp.full((1, TILE), -3e38, f32), jnp.zeros((1, TILE), f32), jnp.zeros((HD, TILE), f32))
                for _ in range(hpd)
            )
            if causal:
                state = step(j, state, True)
                state = lax.fori_loop(0, j, lambda i, st: step(i, st, False), state)
            else:
                state = lax.fori_loop(0, keys, lambda i, st: step(i, st, False), state)
            for h in range(hpd):
                top, total, acc = state[h]
                ot[j, pl.ds(h * HD, HD), :] = acc * (1.0 / total)
                lse[j, h:h + 1, :] = top + jnp.log(total)
            ob[qrows, :] = ot[j].T.astype(bf)
            return _

        if hpd * HD < LANES:
            ot[...] = jnp.zeros_like(ot)
        lax.fori_loop(0, nq, one, 0)

    await_z(lambda zz: weight_rows(zz, 1), wslots[1], False)
    oslots = [net.slots(n - 1) - 1, net.slots(n - 1) - 1]

    def out_rows(j, cc):
        return wbuf.at[pl.ds(pl.multiple_of(cc * w, w), w), pl.ds(OUT_AT[j], LANES)]

    def push_out(j):
        for d in range(1, n):
            peer = lax.rem(c + d, n)
            net.go(out_rows(j, peer), wor_of(j, c), oslots[j] + d, ctx=peer)
        wor_of(j, c)[...] = wbuf[pl.ds(pl.multiple_of(c * w, w), w), pl.ds(OUT_AT[j], LANES)]

    push_out(0)

    def await_out(j):
        for d in range(1, n):
            net.arrived(wor_of(j, lax.rem(c + n - d, n)), oslots[j] + d)
        if w < LANES:
            wo[j] = jnp.zeros((LANES, D), bf)
        wo[j, pl.ds(0, w), :] = jnp.concatenate(
            [pm[cc, pl.ds(0, w), pl.ds(j * LANES, LANES)][:, :w] for cc in range(n)], axis=-1)

    gate.levels()
    attend(qa1, ka1, vt1, ot1, ob1, lse1, nq, True)

    gate.done()
    await_out(0)

    def partial(scat, rows_of, weight_of, per):
        def one(k, _):
            first = scat.chip(k)
            scat.part[pl.ds(first, 2)] = weight_of(rows_of(first)).astype(bf).reshape(2, per, D)
            scat.push(k)
            return _

        lax.fori_loop(0, scat.count, one, 0)

    def flat(buf, per):
        return lambda first: buf[pl.ds(pl.multiple_of(first * per, 2 * per), 2 * per), :]

    rs1 = Scatter(net, plane, pa.at[pl.ds(0, n)], ra.at[pl.ds(0, n)], "sum")
    partial(rs1, flat(ob1, t), lambda rows: dot(rows, wo[0]), t)

    def kv2_tile(i, _):
        rows = tile_rows(i)
        got = dot(tile_of(ex, i, nbe, pl.ds(0, D)), wbuf[:, 512:768])
        oh = tile_of(ex, i, nbe, pl.ds(D, LANES))
        put_k(ka2, got[:, 0:128], oh, rows)
        put_v(v2, vt2, got[:, 128:256] + bias_ref[3:4, :], rows, i)
        return _

    rs1.fold()
    if relayed:
        relay_z(lambda zz: weight_rows(zz, 2), wslots[2])
    for k in range(4):
        push_feed(k)
    rs1.reduce(into(x1))
    x1[...] = x_ref[...].astype(f32) + (x1[...] + row(8))
    hat, _ = normed(x1[...])
    n2f[c] = (hat * row(2) + row(3)).astype(bf)
    gat1.drain()
    if q == 1:
        away1.wait()
    gat2 = Gather(net, plane, n2f, "main")
    gat2.start()
    rs1.drain()
    gate.drain()
    gat2.levels()
    await_z(lambda zz: weight_rows(zz, 2), wslots[2], relayed)
    push_out(1)
    gat2.done()
    gf[wide_group.own] = g_ref[...]
    gatg = Gather(net, wide_group, gf, "side" if q == 1 else "wideside")
    gatg.start()

    def q2_tile(i, _):
        got = dot(tile_of(n2f, i, nbt, pl.ds(0, D)), wbuf[:, 896:1024])
        put_q(qa2, got + bias_ref[2:3, :], tile_of(n1x, i, nbt, pl.ds(D, LANES)), tile_rows(i))
        return _

    lax.fori_loop(0, nq, q2_tile, 0)
    lax.fori_loop(0, nk2, kv2_tile, 0)
    if relayed:
        relay_z(feed_rows(0), fslots[0])
    away2 = local_copy(n2f, hold2, 11)
    gatg.level(1)
    attend(qa2, ka2, vt2, ot2, ob2, lse2, nk2, False)
    away2.wait()
    gat2.drain()
    await_out(1)
    rs2 = Scatter(net, plane, pa.at[pl.ds(0, n)], ra.at[pl.ds(0, n)], "sum")
    partial(rs2, flat(ob2, t), lambda rows: dot(rows, wo[1]), t)
    gatg.levels(2)
    rs2.fold()
    if relayed:
        relay_z(feed_rows(1), fslots[1])
    rs2.reduce(into(x2))
    x2[...] = x1[...] + (x2[...] + row(11))
    hat, _ = normed(x2[...])
    n3f[wide_group.own] = (hat * row(4) + row(5)).astype(bf)
    gat3 = Gather(net, wide_group, n3f, "main" if q == 1 else "wide")
    gat3.start()
    rs2.drain()
    gatg.done()
    for made in own_feed:
        made.wait()
    gat3.finish()
    for k in range(2):
        await_z(feed_rows(k), fslots[k], relayed)
    if relayed:
        relay_z(feed_rows(2), fslots[2])

    rs3 = Scatter(net, wide_group, pa, ra, "sum" if q == 1 else "widesum")
    rsm = Scatter(net, wide_group, pm, rm, "sum2" if q == 1 else "widesum2")
    fc = min(fw, 512)

    def up_tile(k, _):
        first = rs3.chip(k)
        rows = pl.ds(pl.multiple_of(first * t, 2 * t), 2 * t)
        left = n3f[pl.ds(first, 2)].reshape(2 * t, D)
        for f in range(fw // fc):
            cols = pl.ds(f * fc, fc)
            u = dot(left, wup[:, cols]) + bup_ref[0:1, cols]
            cdf, slope = gelu_parts(u)
            act[rows, cols] = (u * cdf).astype(bf)
            du[rows, cols] = slope.astype(bf)
        return _

    lax.fori_loop(0, rs3.count, up_tile, 0)
    per = TILE // (share * nz)

    def weight_grad(left_of, right, out, columns):
        def one(r, _):
            got = t_dot(left_of(tile_rows(r)), right())
            for k in range(TILE // share):
                out[k % nz, r * per + k // nz, :, columns] = got[k * share:(k + 1) * share].astype(bf)
            return _

        lax.fori_loop(0, D // TILE, one, 0)

    def whole(buf, rows):
        return lambda cols: buf[:, :, cols].reshape(rows, TILE)

    zslots = [net.slots(nz) - 1 for _ in range(6)]
    last = (4, 5)

    def push_grad(mine, came, k):
        if relayed and k not in last:
            step = jnp.where(z == 0, 1, nz - 2)
            net.go(mine.at[far_end], came.at[step], zslots[k] + nz, out=net.extra(), fsdp=step, when=ends)
        for d in range(1, nz):
            peer = lax.rem(z + d, nz)
            when = None
            if relayed and k not in last:
                when = jnp.logical_not(jnp.logical_and(
                    jnp.logical_or(ends, inner), peer == far_end))
            net.go(mine.at[peer], came.at[z], zslots[k] + d, fsdp=peer, when=when)

    def relay_grad(mine, came, k):
        if not relayed:
            return

        @pl.when(inner)
        def _():
            net.arrived(came.at[z], zslots[k] + nz)
            mine[far_end] = (mine[far_end].astype(f32) + came[z].astype(f32)).astype(bf)

        net.go(mine.at[far_end], came.at[z], zslots[k] + lax.rem(far_end - z + nz, nz), out=net.extra(), fsdp=far_end,
               when=inner)

    def grad_arrived(came, k, d):
        peer = lax.rem(z + nz - d, nz)
        if relayed and k not in last and d in (1, nz - 1):
            @pl.when(z != (0 if d == 1 else nz - 1))
            def _():
                net.arrived(came.at[peer], zslots[k] + d)
        else:
            net.arrived(came.at[peer], zslots[k] + d)
        return came[peer].astype(f32)

    def sum_grad(mine, came, k):
        total = mine[z].astype(f32)
        for d in range(1, nz):
            total = total + grad_arrived(came, k, d)
        return total.astype(bf)

    weight_grad(whole(gf, rows_wide), lambda: act[...], gd, pl.ds(0, fw))
    for k in range(2, 4):
        await_z(feed_rows(k), fslots[k], relayed and k < 3)

    push_grad(gd, rd, 1)

    def down_tile(k, sums):
        first = rs3.chip(k)
        rows = pl.ds(pl.multiple_of(first * t, 2 * t), 2 * t)
        grad = gf[pl.ds(first, 2)].reshape(2 * t, D)
        out = []
        for f in range(fw // fc):
            cols = pl.ds(f * fc, fc)
            low = (dot(grad, wdown[:, cols]) * du[rows, cols].astype(f32)).astype(bf)
            du[rows, cols] = low
            out.append(sums[f] + jnp.sum(low.astype(f32), axis=0, keepdims=True))
        pa[pl.ds(first, 2)] = dot_t(du[rows, :], wup[...]).astype(bf).reshape(2, t, D)
        rs3.push(k)
        return tuple(out)

    sums = lax.fori_loop(0, rs3.count, down_tile, tuple(jnp.zeros((1, fc), f32) for _ in range(fw // fc)))
    for f in range(fw // fc):
        for cc in range(n * q):
            place = cc * fw + f * fc
            line = 9 + 4 * wide + place // D
            vt[line:line + 1, pl.ds(place % D, fc)] = jnp.where(wide_group.own == cc, sums[f], 0.0)
    rs3.fold()
    weight_grad(whole(n3f, rows_wide), lambda: du[...], gu, pl.ds(0, fw))
    push_grad(gu, ru, 0)

    gat3.drain()
    gatg.drain()
    rs3.reduce(into(dx))
    back, gain_g, shift_g = norm_back(x2[...], row(4), dx[...])
    vt[4:5, :] = gain_g
    vt[5:6, :] = shift_g
    dx[...] = g_ref[...].astype(f32) + back
    dy = dx[...].astype(bf)
    dy2f[c] = dy
    gat4 = Gather(net, plane, dy2f, "main")
    gat4.start()
    vt[7:8, :] = jnp.sum(dy.astype(f32), axis=0, keepdims=True)
    rs3.drain()
    partial(rsm, flat(act, t), lambda rows: dot_t(rows, wdown[...]), t)
    gat4.levels()
    rsm.fold()
    back2 = local_copy(hold2, n2back, 12)
    gat4.done()

    def attend_back(qa, ka, v, ot, lse, dyf, out_w, keys, causal, dq_ref, dq_cols, dkv_ref, dk_cols, dv_cols):
        def grads(i, _):
            rows = tile_rows(i)
            low = dot_t(tile_of(dyf, i, nbt, pl.ds(0, D)), out_w[...]).astype(bf)
            for h in range(hpd):
                dom[h][rows, :] = jnp.where(head_of == h, low, jnp.zeros_like(low))
            prod = low.astype(f32).T * ot[i]
            for h in range(hpd):
                dlt[i, h:h + 1, :] = jnp.sum(prod[h * HD:(h + 1) * HD], axis=0, keepdims=True)
            dqacc[rows, :] = jnp.zeros((TILE, LANES), f32)
            return _

        lax.fori_loop(0, nq, grads, 0)

        def one(i, _):
            krows = tile_rows(i)

            def step(j, state, diagonal):
                qrows = tile_rows(j)
                dv, dks = state
                new_dks, dqs = [], []
                for h in range(hpd):
                    s = dot_t(ka[h, krows, :], qa[h, qrows, :])
                    p = jnp.exp(s - lse[j, h:h + 1, :])
                    if diagonal:
                        kp = lax.broadcasted_iota(jnp.int32, (TILE, TILE), 0)
                        qp = lax.broadcasted_iota(jnp.int32, (TILE, TILE), 1)
                        p = jnp.where(kp <= qp, p, 0.0)
                    dp = dot_t(v[krows, :], dom[h][qrows, :])
                    ds = (p * (dp - dlt[j, h:h + 1, :])).astype(bf)
                    dv = dv + dot(p.astype(bf), dom[h][qrows, :])
                    new_dks.append(dks[h] + dot(ds, qa[h, qrows, :]))
                    dqs.append(t_dot(ds, ka[h, krows, :]))
                dq = jnp.where(head_of == 0, dqs[0], dqs[-1] if hpd > 1 else 0.0)
                dqacc[qrows, :] = dqacc[qrows, :] + dq
                return dv, tuple(new_dks)

            zero = jnp.zeros((TILE, LANES), f32)
            state = (zero, tuple(zero for _ in range(hpd)))
            if causal:
                state = step(i, state, True)
                state = lax.fori_loop(i + 1, nq, lambda j, st: step(j, st, False), state)
            else:
                state = lax.fori_loop(0, nq, lambda j, st: step(j, st, False), state)
            dv, dks = state
            dk = jnp.where(head_of == 0, dks[0], dks[-1] if hpd > 1 else 0.0)
            dkv_ref[krows, dk_cols] = dk.astype(bf)
            dkv_ref[krows, dv_cols] = dv.astype(bf)
            return _

        lax.fori_loop(0, keys, one, 0)

        def close(i, _):
            rows = tile_rows(i)
            dq_ref[rows, dq_cols] = (dqacc[rows, :] * SCALE).astype(bf)
            return _

        lax.fori_loop(0, nq, close, 0)

    def head_sum(k, ref, cols):
        own = jnp.sum(ref[:, cols].astype(f32), axis=0, keepdims=True)
        for cc in range(n):
            line = 9 + k * wide + cc * LANES // D
            vt[line:line + 1, pl.ds(cc * LANES % D, LANES)] = jnp.where(c == cc, own, 0.0)

    first3 = [pl.ds(k * LANES, LANES) for k in range(3)]
    attend_back(qa2, ka2, v2, ot2, lse2, dy2f, wo.at[1], nk2, False, dq2, first3[0], dkv2, first3[0], first3[1])
    rs4 = Scatter(net, plane, pa.at[pl.ds(0, n)], ra.at[pl.ds(0, n)], "sum")
    partial(rs4, flat(dq2, t), lambda rows: dot_t(rows, wbuf[:, 896:1024]), t)
    def store_mixed(cut, total):
        mixed_ref[:, cut] = (x2[:, cut] + (total + vec_ref[12:13, cut])).astype(bf)

    rsm.reduce(store_mixed)
    rs4.fold()
    relay_grad(gd, rd, 1)

    weight_grad(whole(ex, lenc), lambda: dkv2[...], gac, pl.ds(0, 256))
    back2.wait()
    weight_grad(whole(n2back, length), lambda: dq2[...], gac, pl.ds(256, 128))
    if q == 1:
        back1 = local_copy(hold1, n1f, 13)
    push_grad(gac, rac, 2)

    def out_grad(ob, dyf, out):
        for cut in (0, 1):
            cols = pl.ds(cut * (D // 2), D // 2)
            got = t_dot(ob[...], dyf[:, :, cols].reshape(length, D // 2))
            for k in range(nz):
                out[k, :, cols] = got[k * share:(k + 1) * share].astype(bf)

    rs4.reduce(into(x2))
    back, gain_g, shift_g = norm_back(x1[...], row(2), x2[...])
    vt[2:3, :] = gain_g
    vt[3:4, :] = shift_g
    dx[...] = dx[...] + back
    dy = dx[...].astype(bf)
    dy1f[c] = dy
    gat4.drain()
    gat5 = Gather(net, plane, dy1f, "main")
    gat5.start()
    vt[6:7, :] = jnp.sum(dy.astype(f32), axis=0, keepdims=True)
    head_sum(2, dq2, first3[0])
    head_sum(3, dkv2, first3[1])
    rs4.drain()
    rsm.drain()
    rse = Scatter(net, plane, pm.at[pl.ds(0, n), pl.ds(0, te), :], rm.at[pl.ds(0, n), pl.ds(0, te), :], "sum2")
    partial(rse, flat(dkv2, te), lambda rows: dot_t(rows, wbuf[:, 512:768]), te)
    gat5.levels()
    rse.fold()
    out_grad(ob2, dy2f, goc)
    push_grad(goc, roc, 3)
    gat5.done()
    out_grad(ob1, dy1f, gos)
    push_grad(gos, ros, 5)
    attend_back(qa1, ka1, v1, ot1, lse1, dy1f, wo.at[0], nq, True, dqkv, first3[0], dqkv, first3[1], first3[2])
    relay_grad(gu, ru, 0)
    rs5 = Scatter(net, plane, pa.at[pl.ds(0, n)], ra.at[pl.ds(0, n)], "sum")
    partial(rs5, flat(dqkv, t), lambda rows: dot_t(rows, wbuf[:, 0:384]), t)
    rs5.fold()
    relay_grad(gac, rac, 2)
    rse.reduce(into(genc_ref))
    if q == 1:
        back1.wait()
    weight_grad(whole(n1f, length), lambda: dqkv[...], gas, pl.ds(0, 384))
    push_grad(gas, ras, 4)
    relay_grad(goc, roc, 3)
    rs5.reduce(into(x2))
    back, gain_g, shift_g = norm_back(x_ref[...].astype(f32), row(0), x2[...])
    vt[0:1, :] = gain_g
    vt[1:2, :] = shift_g
    gtok_ref[...] = dx[...] + back
    head_sum(0, dqkv, first3[0])
    head_sum(1, dqkv, first3[2])

    vslots = net.slots(vcame.shape[0])
    pairs = [("ctx", b) for b in plane.hops + [1]] + [("fsdp", 1 << k) for k in range(nz.bit_length() - 1)]

    def swap(k):
        axis, b = pairs[k]
        own = c if axis == "ctx" else z
        peer = own + b - 2 * b * ((own // b) % 2)
        made = net.copy(vt, vcame.at[k], vslots + k, **{axis: peer})
        made.start()
        return made

    def merge(k, made):
        made.wait_send()
        net.arrived(vcame.at[k], vslots + k)
        vt[...] = vt[...] + vcame[k]

    def sum_feed(mine, came, k, total):
        for r in range(q):
            got = 0.0
            for d in range(r, nz, q):
                if d == 0:
                    got = got + mine[z].astype(f32)
                else:
                    got = got + grad_arrived(came, k, d)
            total[:, lax.rem(parity + q - r, q)] = got.astype(bf)

    def sum_heads(mine, came, k):
        mine[z] = sum_grad(mine, came, k)
        return mine.at[z]

    def exchange(total, out):
        slot = net.slots(n - 1) - 1
        out[c] = total[c]
        for d in range(1, n):
            peer = lax.rem(c + d, n)
            net.go(total.at[peer], out.at[c], slot + d, ctx=peer)

        def done():
            for d in range(1, n):
                net.arrived(out.at[lax.rem(c + n - d, n)], slot + d)
        return done

    waits = []
    todo = [
        lambda: (sum_feed(gu, ru, 0, su), waits.append(exchange(su, fu))),
        lambda: (sum_feed(gd, rd, 1, sd), waits.append(exchange(sd, fd))),
        lambda: waits.append(exchange(sum_heads(gac, rac, 2), fac)),
    ]
    for k in range(len(pairs)):
        made = swap(k)
        if todo:
            todo.pop(0)()
        merge(k, made)
    for step in todo:
        step()
    foc[...] = sum_grad(goc, roc, 3)
    waits.append(exchange(sum_heads(gas, ras, 4), fas))
    fos[...] = sum_grad(gos, ros, 5)
    for wait in waits:
        wait()
    rs5.drain()
    rse.drain()
    gat5.drain()
    net.drain()
    assert net.used == count_slots(n, nz, q) and net.extras <= EXTRAS


def body(tokens, encoder, dec_seg, src_seg, attn_w, up_w, down_w, vec, cot):
    n, nz = lax.axis_size("ctx"), lax.axis_size("fsdp")
    c = lax.axis_index("ctx")
    t, te = tokens.shape[1], encoder.shape[1]
    ff = up_w.shape[1]
    q = 1
    w, fw = D // n, ff // (n * q)
    hpd = w // HD
    dz = D // nz
    share = D // (n * nz)
    length, lenc = n * t, n * te

    if w < LANES:
        wsl = lax.dynamic_slice_in_dim(attn_w.reshape(dz, 8, D), c * w, w, axis=2)
        wsl = jnp.stack([wsl[:, k] for k in ORDER], axis=1)
        attn_w = jnp.pad(wsl, ((0, 0), (0, 0), (0, LANES - w))).reshape(dz, 8 * LANES)

    nq, nk2 = length // TILE, lenc // TILE
    slots = count_slots(n, nz, q)
    dims = (n, nz, q, t, te, w, fw, hpd)
    wide = -(-n * LANES // D)
    vrows = -(-(9 + 4 * wide + ff // D) // 8) * 8
    steps = n.bit_length() + nz.bit_length() - 2
    out_shape = (
        jax.ShapeDtypeStruct((t, D), bf),
        jax.ShapeDtypeStruct((t, D), f32),
        jax.ShapeDtypeStruct((te, D), f32),
        jax.ShapeDtypeStruct((n, q, share, fw), bf),
        jax.ShapeDtypeStruct((n, q, share, fw), bf),
        jax.ShapeDtypeStruct((n, share, 384), bf),
        jax.ShapeDtypeStruct((n, share, 384), bf),
        jax.ShapeDtypeStruct((share, D), bf),
        jax.ShapeDtypeStruct((share, D), bf),
        jax.ShapeDtypeStruct((vrows, D), f32),
        jax.ShapeDtypeStruct((n, t, D), bf),
        jax.ShapeDtypeStruct((n, t, D), bf),
    )

    def attn_scratch(keys):
        return [
            pltpu.VMEM((hpd, length, LANES), bf), pltpu.VMEM((hpd, keys, LANES), bf), pltpu.VMEM((keys, LANES), bf),
            pltpu.VMEM((keys // TILE, LANES, TILE), bf), pltpu.VMEM((nq, LANES, TILE), f32),
            pltpu.VMEM((length, LANES), bf), pltpu.VMEM((nq, 8, TILE), f32),
        ]

    scratch = [
        pltpu.VMEM((n, t, D + LANES), bf), pltpu.VMEM((n, te, D + LANES), bf),
        pltpu.VMEM((q * n, t, D) if q == 2 else (1, 16, LANES), bf), pltpu.VMEM((q * n, t, D), bf),
        pltpu.VMEM((D, 8 * LANES), bf), pltpu.VMEM((2, LANES, D), bf),
        pltpu.VMEM((D, fw), bf), pltpu.VMEM((D, fw), bf),
        *attn_scratch(length), *attn_scratch(lenc),
        pltpu.VMEM((t, D), f32), pltpu.VMEM((t, D), f32),
        *[pltpu.VMEM((q * n, t, D), bf) for _ in range(4)], pltpu.VMEM((n, t, D), bf),
        pltpu.VMEM((q * length, fw), bf), pltpu.VMEM((q * length, fw), bf),
    ]
    for _ in range(2):
        scratch += [
            pltpu.VMEM((nz, n, share, fw), bf), pltpu.VMEM((nz, n, share, fw), bf),
            pltpu.VMEM((nz, n, share, 384), bf), pltpu.VMEM((nz, n, share, 384), bf),
            pltpu.VMEM((nz, share, D), bf), pltpu.VMEM((nz, share, D), bf),
        ]
    scratch += [
        pltpu.VMEM((n, q, share, fw), bf), pltpu.VMEM((n, q, share, fw), bf), pltpu.VMEM((steps, vrows, D), f32),
        pltpu.VMEM((nq, 8, TILE), f32), pltpu.VMEM((length, LANES), f32),
        pltpu.VMEM((8, LANES), f32), pltpu.VMEM((8, fw), f32),
        pltpu.SemaphoreType.DMA((slots + EXTRAS,)), pltpu.SemaphoreType.DMA((slots,)), pltpu.SemaphoreType.DMA((16,)),
    ]
    vmem = pl.BlockSpec(memory_space=pltpu.VMEM)
    hbm = pl.BlockSpec(memory_space=pl.ANY)
    mixed, gtok, genc, fu, fd, fas, fac, fos, foc, vsum, _, _ = pl.pallas_call(
        functools.partial(layer, dims),
        out_shape=out_shape,
        in_specs=[vmem] * 5 + [hbm] * 3 + [vmem],
        out_specs=[vmem] * (len(out_shape) - 2) + [hbm] * 2,
        scratch_shapes=scratch,
        compiler_params=pltpu.CompilerParams(
            collective_id=0, has_side_effects=True, vmem_limit_bytes=63 * 1024 * 1024
        ),
        cost_estimate=pl.CostEstimate(flops=21_000_000_000, bytes_accessed=30_000_000, transcendentals=8_000_000),
        name="layer",
    )(tokens[0], encoder[0], cot[0], dec_seg, src_seg, attn_w, up_w, down_w, vec)

    return pl.pallas_call(
        functools.partial(closing, (n, q, w, fw, wide)),
        out_shape=(
            jax.ShapeDtypeStruct((1, t, D), bf), jax.ShapeDtypeStruct((1, t, D), f32),
            jax.ShapeDtypeStruct((1, te, D), f32), jax.ShapeDtypeStruct((share, 8 * D), f32),
            jax.ShapeDtypeStruct((share, ff), f32), jax.ShapeDtypeStruct((share, ff), f32),
            jax.ShapeDtypeStruct(vec.shape, f32),
        ),
        in_specs=[hbm] * 10,
        out_specs=[hbm] * 7,
        scratch_shapes=[pltpu.VMEM(a.shape, a.dtype) for a in (mixed, gtok, genc, fu, fd, fas, fac, fos, foc, vsum)] + [
            pltpu.VMEM((share, 8 * D), f32), pltpu.VMEM((share, ff), f32), pltpu.VMEM((share, ff), f32),
            pltpu.VMEM(vec.shape, f32), pltpu.SemaphoreType.DMA((17,)),
        ],
        compiler_params=pltpu.CompilerParams(vmem_limit_bytes=62 * 1024 * 1024),
        name="closing",
    )(mixed, gtok, genc, fu, fd, fas, fac, fos, foc, vsum)


def closing(dims, *refs):
    n, q, w, fw, wide = dims
    given, outs, kept, made, sems = refs[:10], refs[10:17], refs[17:27], refs[27:31], refs[31]
    coming = [pltpu.make_async_copy(given[k], kept[k], sems.at[k]) for k in range(10)]
    straight = [pltpu.make_async_copy(kept[k], outs[k].at[0], sems.at[10 + k]) for k in range(3)]
    going = [pltpu.make_async_copy(made[k], outs[3 + k], sems.at[13 + k]) for k in range(4)]
    for copy in coming:
        copy.start()
    for k in range(3):
        coming[k].wait()
        straight[k].start()
    kept, coming = kept[3:], coming[3:]
    fu, fd, fas, fac, fos, foc, vsum = kept
    o_attn, o_up, o_down, o_vec = made
    coming[0].wait()
    for cc in range(n * q):
        o_up[:, pl.ds(cc * fw, fw)] = fu[cc % n, cc // n].astype(f32)
    going[1].start()
    coming[1].wait()
    for cc in range(n * q):
        o_down[:, pl.ds(cc * fw, fw)] = fd[cc % n, cc // n].astype(f32)
    going[2].start()
    for k in range(2, 7):
        coming[k].wait()
    for block, (ref, k) in enumerate(
        ((fas, 0), (fas, 1), (fas, 2), (fos, None), (fac, 2), (fac, 0), (fac, 1), (foc, None))
    ):
        if k is None:
            got = ref[...]
        else:
            got = jnp.concatenate([ref[cc, :, pl.ds(k * LANES, LANES)][:, :w] for cc in range(n)], axis=-1)
        o_attn[:, pl.ds(block * D, D)] = got.astype(f32)
    going[0].start()

    def heads(k):
        parts = []
        for cc in range(n):
            line, first = 9 + k * wide + cc * LANES // D, cc * LANES % D
            parts.append(vsum[line:line + 1, first:first + LANES][:, :w])
        return jnp.concatenate(parts, axis=-1)

    o_vec[0:6] = vsum[0:6]
    o_vec[6:7] = heads(0)
    o_vec[7:8] = heads(1)
    o_vec[8:9] = vsum[6:7]
    o_vec[9:10] = heads(2)
    o_vec[10:11] = heads(3)
    o_vec[11:13] = vsum[7:9]
    up = 9 + 4 * wide
    o_vec[13:] = vsum[up:up + o_vec.shape[0] - 13]
    going[3].start()
    for copy in straight + going:
        copy.wait()


def solution(mesh):
    return jax.shard_map(
        body, mesh=mesh,
        in_specs=(P("fsdp", "ctx", None), P("fsdp", "ctx", None), P("fsdp", "ctx"), P("fsdp", "ctx"), P("fsdp", None),
                  P("fsdp", None), P("fsdp", None), P(), P("fsdp", "ctx", None)),
        out_specs=(P("fsdp", "ctx", None), P("fsdp", "ctx", None), P("fsdp", "ctx", None), P(("ctx", "fsdp"), None),
                   P(("ctx", "fsdp"), None), P(("ctx", "fsdp"), None), P()),
        check_vma=False,
    )
```
